128 devices in a mesh: bx: 8 (over y, core), by: 16 (over z, x).
Axes of the slice: x: 4, y: 4, z: 4, core: 2. Of those that a mesh axis runs over, the one named last changes fastest.
Arguments:
- tracers: float32 [22, 2, 2048, 2048], P(None, None, 'bx', 'by'), may hold values from -6 to 6
- mixing: float32 [22, 2], replicated, may hold values from 0.003 to 0.025
- thickness: float32 [22], replicated, may hold values from 0.02 to 0.08
- levels: int32 [2048, 2048], P('bx', 'by'), may hold values from 1 to 22
- land: int32 [2048, 2048], P('bx', 'by'), may hold values 0 or 1
Outputs:
- tracers_new: float32 [22, 2, 2048, 2048], P(None, None, 'bx', 'by')
- surface: float32 [2048, 2048], P('bx', 'by')
- transports: float32 [2, 2048, 2048], P(None, 'bx', 'by')
The draws below stay inside these ranges and needn't reach their ends.
All inputs are finite; a program needn't handle non-finite values. No bound on the sum of `land` on one device may be relied on, other than what follows from the above.
Results may differ from the reference program's by a relative error of at most 0.0003.
Values sent between devices are 32-bit elements; how exact they have to be, the bound alone decides.
No kernel may reach another device: no remote copies, remote signals or barrier semaphores. Data moves between devices by JAX's collectives and lax.ppermute only.
A program may use at most 320 MiB of HBM per device.

```python
import math
import jax
import jax.numpy as jnp
from jax import lax

KL = 22
ITERS = 4
NX = 2048
NY = 2048


def set_ends(drawn, key, low, top_value):
    index_at = [jax.random.randint(jax.random.fold_in(key, axis), (), 0, length) for axis, length in enumerate(drawn.shape)]
    widest = drawn.shape.index(max(drawn.shape))
    beside = index_at[:widest] + [(index_at[widest] + 1) % drawn.shape[widest]] + index_at[widest + 1:]
    return drawn.at[tuple(index_at)].set(low).at[tuple(beside)].set(top_value)


def block_scale(stream_key, shape, split, low, top_value):
    gain, own = 1.0, jax.random.fold_in(stream_key, 6)
    for axis_at, parts in split:
        draws = jnp.exp(jax.random.uniform(jax.random.fold_in(own, axis_at), (parts,), jnp.float32, low / len(split), top_value / len(split)))
        gain = gain * jnp.repeat(draws, shape[axis_at] // parts).reshape([-1 if axis == axis_at else 1 for axis in range(len(shape))])
    return gain


def bell_draw(key, extent, scale, limit, cuts=(), kind=jnp.bfloat16):
    factor_of = block_scale(key, extent, cuts, -0.22, 0.18) if cuts else 1.0
    array = jax.random.normal(key, extent, jnp.float32) * scale * factor_of
    return jnp.minimum(jnp.maximum(array, -limit), limit).astype(kind)


def setup_inputs(seed: int = 0) -> dict:
    key_of = jax.random.split(jax.random.key(seed), 6)
    return {
        "tracers": bell_draw(key_of[0], (KL, 2, NX, NY), 1.0, 6.0, ((2, 8), (3, 16)), jnp.float32),
        "mixing": jnp.clip(jnp.exp(jax.random.uniform(key_of[1], (KL, 2), jnp.float32, math.log(0.003), math.log(0.025))), 0.003, 0.025),
        "thickness": jnp.clip(jnp.exp(jax.random.uniform(key_of[2], (KL,), jnp.float32, math.log(0.02), math.log(0.08))), 0.02, 0.08),
        "levels": set_ends(jax.random.randint(key_of[3], (NX, NY), 1, KL + 1), jax.random.fold_in(key_of[3], 1), 1, KL).astype(jnp.int32),
        "land": set_ends((jax.random.randint(key_of[4], (NX, NY), 0, 4) < 1).astype(jnp.int32), jax.random.fold_in(key_of[4], 1), 0, 1),
    }


GRAVITY = 10.0
OFFSETS = ((-1, 0, 1.0), (1, 0, 1.0), (0, -1, 1.0), (0, 1, 1.0), (-1, -1, 0.25), (1, 1, 0.25), (-1, 1, 0.25), (1, -1, 0.25))


def neighbour(field, di, dj):
    moved = jnp.roll(field, -di, axis=-2) if di != 0 else field
    if dj == 1:
        zeros = jnp.zeros_like(moved[..., :1])
        moved = jnp.concatenate([moved[..., 1:], zeros], axis=-1)
    if dj == -1:
        zeros = jnp.zeros_like(moved[..., :1])
        moved = jnp.concatenate([zeros, moved[..., :-1]], axis=-1)
    return moved


def laplace(field, wet):
    total = neighbour(wet, -1, 0) * (neighbour(field, -1, 0) - field)
    total = total + neighbour(wet, 1, 0) * (neighbour(field, 1, 0) - field)
    total = total + neighbour(wet, 0, -1) * (neighbour(field, 0, -1) - field)
    total = total + neighbour(wet, 0, 1) * (neighbour(field, 0, 1) - field)
    return wet * total


def reference(tracers, mixing, thickness, levels, land):
    ocean = land == 0
    zeros = jnp.zeros(levels.shape, jnp.float32)

    def level(carry, inputs):
        accum, flux_x, flux_y, depth = carry
        field, mix, layer, index = inputs
        wet = jnp.logical_and(ocean, index < levels).astype(jnp.float32)
        first = laplace(field, wet)
        second = laplace(first, wet)
        renewed = field - mix[:, None, None] * second
        density = wet * (0.8 * renewed[1] - 0.2 * renewed[0])
        accum = accum + layer * density
        pressure = GRAVITY * accum
        flux_x = flux_x + layer * wet * neighbour(wet, -1, 0) * (pressure - neighbour(pressure, -1, 0))
        flux_y = flux_y + layer * wet * neighbour(wet, 0, -1) * (pressure - neighbour(pressure, 0, -1))
        depth = depth + layer * wet
        return (accum, flux_x, flux_y, depth), renewed

    inputs = (tracers, mixing, thickness, jnp.arange(tracers.shape[0], dtype=jnp.int32))
    carry, tracers_new = lax.scan(level, (zeros, zeros, zeros, zeros), inputs)
    accum, flux_x, flux_y, depth = carry
    source = flux_x - neighbour(flux_x, 1, 0) + flux_y - neighbour(flux_y, 0, 1)
    weights = [factor * jnp.minimum(depth, neighbour(depth, di, dj)) for di, dj, factor in OFFSETS]
    diagonal = 0.05 + weights[0]
    for extra in weights[1:]:
        diagonal = diagonal + extra

    def operate(field):
        result = diagonal * field
        for weight, (di, dj, factor) in zip(weights, OFFSETS):
            result = result - weight * neighbour(field, di, dj)
        return result

    surface = jnp.zeros_like(source)
    residual, direction = source, source
    norm_now = jnp.sum(residual * residual)
    for step in range(ITERS):
        image = operate(direction)
        alpha = norm_now / jnp.sum(direction * image)
        surface = surface + alpha * direction
        residual = residual - alpha * image
        norm_next = jnp.sum(residual * residual)
        direction = residual + (norm_next / norm_now) * direction
        norm_now = norm_next
    east_flow = weights[0] * (neighbour(surface, -1, 0) - surface)
    north_flow = weights[2] * (neighbour(surface, 0, -1) - surface)
    return tracers_new, surface, jnp.stack([east_flow, north_flow])
```

```python
import functools

import jax
import jax.numpy as jnp
from jax import lax
from jax.experimental import pallas as pl
from jax.experimental.pallas import tpu as pltpu
from jax.sharding import PartitionSpec as P

KL = 22
ROWS = 256
LANES = 128
HALO = 8
EXT = ROWS + 2 * HALO
PAD = 8
BUF = EXT + 2 * PAD
GROUP = 16
TILES = 3
HALF_STEPS = 2
MOMENTS = 8
F32 = jnp.float32
I32 = jnp.int32
VMEM_LIMIT = 48 * 1024 * 1024


def lane_iota(rows):
    return lax.broadcasted_iota(I32, (rows, LANES), 1)


def roll(x, shift):
    return pltpu.roll(x, shift % LANES, 1)


def blocks(start, stop, size):
    out = []
    while start < stop:
        out.append((start, min(size, stop - start)))
        start += size
    return out


CHUNKS = [(0, HALO)] + blocks(HALO, HALO + ROWS, 32) + [(HALO + ROWS, HALO)]


def ext_rows(ref, top_ref, bottom_ref, place, plane, r0, n):
    if r0 < HALO:
        return top_ref[plane]
    if r0 >= HALO + ROWS:
        return bottom_ref[plane]
    return ref[place + (pl.ds(r0 - HALO, n),)]


def wet_levels(levels, land):
    return jnp.where(land == 0, levels, 0)


def pack_kernel(t_ref, top_ref, bottom_ref, levels_ref, land_ref, right_ref, left_ref):
    for r0, n in CHUNKS:
        lane = lane_iota(n)
        group = lane // GROUP
        first = (lane & 8) == 0
        for tile in range(TILES):
            to_right = jnp.zeros((n, LANES), F32)
            to_left = jnp.zeros((n, LANES), F32)
            for g in range(LANES // GROUP):
                k = tile * (LANES // GROUP) + g
                if k < KL:
                    a = ext_rows(t_ref, top_ref, bottom_ref, (k, 0), 2 * k, r0, n)
                    b = ext_rows(t_ref, top_ref, bottom_ref, (k, 1), 2 * k + 1, r0, n)
                elif k == KL:
                    if r0 < HALO:
                        a = top_ref[2 * KL]
                    elif r0 >= HALO + ROWS:
                        a = bottom_ref[2 * KL]
                    else:
                        own = pl.ds(r0 - HALO, n)
                        a = wet_levels(levels_ref[own], land_ref[own]).astype(F32)
                    b = a
                else:
                    continue
                here = group == g
                pair_right = jnp.where(first, roll(a, 8 + GROUP * g), roll(b, GROUP + GROUP * g))
                pair_left = jnp.where(first, roll(a, GROUP * g), roll(b, 8 + GROUP * g))
                to_right = jnp.where(here, pair_right, to_right)
                to_left = jnp.where(here, pair_left, to_left)
            right_ref[tile, pl.ds(r0, n)] = to_right
            left_ref[tile, pl.ds(r0, n)] = to_left


def count_word(effs, word):
    total = None
    for eff in effs:
        bits = jnp.clip(eff - 10 * word, 0, 10) * 3
        mask = (lax.shift_left(jnp.full_like(bits, 1), bits) - 1) & 0o1111111111
        total = mask if total is None else total + mask
    return total


def wet_setup(eff_ref, min_ref, word_ref, top_ref, bottom_ref, levels_ref, land_ref):
    eff_ref[...] = jnp.zeros(eff_ref.shape, I32)
    eff_ref[pl.ds(PAD, HALO)] = top_ref[2 * KL].astype(I32)
    eff_ref[pl.ds(PAD + HALO, ROWS)] = wet_levels(levels_ref[...], land_ref[...])
    eff_ref[pl.ds(PAD + HALO + ROWS, HALO)] = bottom_ref[2 * KL].astype(I32)
    for r0, n in CHUNKS:
        e = eff_ref[pl.ds(PAD + r0, n)]
        up = eff_ref[pl.ds(PAD + r0 - 1, n)]
        down = eff_ref[pl.ds(PAD + r0 + 1, n)]
        west = roll(e, 1)
        east = roll(e, -1)
        if min_ref is not None:
            min_ref[0, pl.ds(r0, n)] = jnp.minimum(e, up)
            min_ref[1, pl.ds(r0, n)] = jnp.minimum(e, west)
        for word in range(3):
            word_ref[word, pl.ds(r0, n)] = count_word((up, down, west, east), word)


def wet_count(word_ref, k, r0, n):
    words = word_ref[k // 10, pl.ds(r0, n)]
    shift = jnp.full((n, LANES), 3 * (k % 10), I32)
    return (lax.shift_right_logical(words, shift) & 7).astype(F32)


def neighbours(ref, r0, n):
    x = ref[pl.ds(PAD + r0, n)]
    around = ref[pl.ds(PAD + r0 - 1, n)] + ref[pl.ds(PAD + r0 + 1, n)]
    return x, around + (roll(x, 1) + roll(x, -1))


def density_kernel(
    mixing_ref,
    thick_ref,
    t_ref,
    top_ref,
    bottom_ref,
    levels_ref,
    land_ref,
    fx_ref,
    fy_ref,
    eff_ref,
    min_ref,
    word_ref,
    u_ref,
    l_ref,
    acc_ref,
):
    part = pl.program_id(0)

    @pl.when(part == 0)
    def _():
        wet_setup(eff_ref, min_ref, word_ref, top_ref, bottom_ref, levels_ref, land_ref)
        u_ref[...] = jnp.zeros(u_ref.shape, F32)
        l_ref[...] = jnp.zeros(l_ref.shape, F32)
        acc_ref[...] = jnp.zeros(acc_ref.shape, F32)
        fx_ref[...] = jnp.zeros(fx_ref.shape, F32)
        fy_ref[...] = jnp.zeros(fy_ref.shape, F32)

    def level(step, carry):
        k = part * (KL // HALF_STEPS) + step
        m0 = 0.2 * mixing_ref[k, 0]
        m1 = 0.8 * mixing_ref[k, 1]
        thick = thick_ref[k]
        for r0, n in CHUNKS:
            a = ext_rows(t_ref, top_ref, bottom_ref, (step, 0), 2 * k, r0, n)
            b = ext_rows(t_ref, top_ref, bottom_ref, (step, 1), 2 * k + 1, r0, n)
            wet = eff_ref[pl.ds(PAD + r0, n)] > k
            u_ref[pl.ds(PAD + r0, n)] = jnp.where(wet, m1 * b - m0 * a, 0.0)
        for r0, n in CHUNKS:
            wet = eff_ref[pl.ds(PAD + r0, n)] > k
            x, around = neighbours(u_ref, r0, n)
            l_ref[pl.ds(PAD + r0, n)] = jnp.where(wet, around, 0.0) - wet_count(word_ref, k, r0, n) * x
        for r0, n in CHUNKS:
            a = ext_rows(t_ref, top_ref, bottom_ref, (step, 0), 2 * k, r0, n)
            b = ext_rows(t_ref, top_ref, bottom_ref, (step, 1), 2 * k + 1, r0, n)
            wet = eff_ref[pl.ds(PAD + r0, n)] > k
            x, around = neighbours(l_ref, r0, n)
            plain = 0.8 * b - 0.2 * a
            density = jnp.where(wet, plain - around, 0.0) + wet_count(word_ref, k, r0, n) * x
            acc_ref[pl.ds(PAD + r0, n)] += thick * density
        for r0, n in CHUNKS:
            here = acc_ref[pl.ds(PAD + r0, n)]
            up = acc_ref[pl.ds(PAD + r0 - 1, n)]
            face_x = min_ref[0, pl.ds(r0, n)] > k
            face_y = min_ref[1, pl.ds(r0, n)] > k
            fx_ref[pl.ds(r0, n)] += thick * jnp.where(face_x, here - up, 0.0)
            fy_ref[pl.ds(r0, n)] += thick * jnp.where(face_y, here - roll(here, 1), 0.0)
        return carry

    lax.fori_loop(0, KL // HALF_STEPS, level, 0)


def two_sum(a, b):
    s = a + b
    v = s - a
    return s, (a - (s - v)) + (b - v)


def quick_sum(a, b):
    s = a + b
    return s, b - (s - a)


def split(a):
    t = a * 4097.0
    high = t - (t - a)
    return high, a - high


def two_prod(a, b, parts_a, parts_b):
    p = a * b
    ah, al = parts_a
    bh, bl = parts_b
    return p, ((ah * bh - p) + ah * bl + al * bh) + al * bl


def pair_add(x, y):
    s, e = two_sum(x[0], y[0])
    return quick_sum(s, e + (x[1] + y[1]))


def pair_mul(x, y):
    p, e = two_prod(x[0], y[0], split(x[0]), split(y[0]))
    return quick_sum(p, e + (x[0] * y[1] + x[1] * y[0]))


def pair_neg(x):
    return -x[0], -x[1]


def pair_div(x, y):
    q = x[0] / y[0]
    rest = pair_add(x, pair_neg(pair_mul(y, (q, jnp.zeros_like(q)))))
    return quick_sum(q, rest[0] / y[0])


def pair_clip(x, top):
    inside = jnp.logical_and(x[0] >= 0.0, x[0] <= top)
    high = jnp.where(inside, x[0], jnp.where(x[0] > top, top, 0.0))
    return high, jnp.where(inside, x[1], 0.0)


def group_totals(x):
    x = x + roll(x, GROUP)
    x = x + roll(x, 2 * GROUP)
    return x + roll(x, 4 * GROUP)


def strip_side(
    side,
    near_ref,
    far_ref,
    keep,
    mixing_ref,
    thick_ref,
    eff_ref,
    min_ref,
    u_ref,
    l_ref,
    acc_ref,
    carry_ref,
    fx_ref,
    fy_ref,
):
    chunks = blocks(0, EXT, 32)

    def field(tile, which, r0, n):
        first = (lane_iota(n) & 8) == 0
        near = near_ref[tile, pl.ds(r0, n)]
        far = far_ref[tile, pl.ds(r0, n)]
        if side == 0:
            low, high = far, near
        else:
            low, high = near, far
        if which == 0:
            return jnp.where(first, low, roll(high, 8))
        return jnp.where(first, roll(low, -8), high)

    for r0, n in chunks:
        lane = lane_iota(n)
        slot = KL - 2 * (LANES // GROUP)
        x = field(2, 0, r0, n)
        outer = (lane & 8) == (0 if side == 0 else 8)
        x = jnp.where(jnp.logical_and(lane // GROUP == slot, jnp.logical_or(jnp.logical_not(outer), keep)), x, 0.0)
        eff_ref[pl.ds(PAD + r0, n)] = group_totals(x).astype(I32)
    for r0, n in chunks:
        e = eff_ref[pl.ds(PAD + r0, n)]
        min_ref[0, pl.ds(r0, n)] = jnp.minimum(e, eff_ref[pl.ds(PAD + r0 - 1, n)])
        min_ref[1, pl.ds(r0, n)] = jnp.minimum(e, roll(e, 1))
    for tile in range(TILES):
        group8 = lane_iota(8) // GROUP
        m0 = jnp.zeros((8, LANES), F32)
        m1 = m0
        thick8 = m0
        for g in range(LANES // GROUP):
            k = tile * (LANES // GROUP) + g
            if k < KL:
                m0 = jnp.where(group8 == g, 0.2 * mixing_ref[k, 0], m0)
                m1 = jnp.where(group8 == g, 0.8 * mixing_ref[k, 1], m1)
                thick8 = jnp.where(group8 == g, thick_ref[k], thick8)
        m0, m1, thick8 = m0[0:1], m1[0:1], thick8[0:1]
        level_of = group8[0:1] + tile * (LANES // GROUP)

        for r0, n in chunks:
            wet = eff_ref[pl.ds(PAD + r0, n)] > level_of
            u_ref[pl.ds(PAD + r0, n)] = jnp.where(
                wet, m1 * field(tile, 1, r0, n) - m0 * field(tile, 0, r0, n), 0.0
            )

        def count(r0, n):
            e = eff_ref[pl.ds(PAD + r0, n)]
            total = jnp.where(eff_ref[pl.ds(PAD + r0 - 1, n)] > level_of, 1.0, 0.0)
            total += jnp.where(eff_ref[pl.ds(PAD + r0 + 1, n)] > level_of, 1.0, 0.0)
            total += jnp.where(roll(e, 1) > level_of, 1.0, 0.0)
            return total + jnp.where(roll(e, -1) > level_of, 1.0, 0.0)

        for r0, n in chunks:
            wet = eff_ref[pl.ds(PAD + r0, n)] > level_of
            x, around = neighbours(u_ref, r0, n)
            l_ref[pl.ds(PAD + r0, n)] = jnp.where(wet, around, 0.0) - count(r0, n) * x
        for r0, n in chunks:
            lane = lane_iota(n)
            wet = eff_ref[pl.ds(PAD + r0, n)] > level_of
            x, around = neighbours(l_ref, r0, n)
            plain = 0.8 * field(tile, 1, r0, n) - 0.2 * field(tile, 0, r0, n)
            density = jnp.where(wet, plain - around, 0.0) + count(r0, n) * x
            layer = thick8 * density
            run = layer
            for step in (1, 2, 4):
                run = run + jnp.where(lane >= step * GROUP, roll(run, step * GROUP), 0.0)
            if tile > 0:
                run = run + carry_ref[pl.ds(r0, n)]
            acc_ref[pl.ds(PAD + r0, n)] = run
            if tile == 0:
                carry_ref[pl.ds(r0, n)] = group_totals(layer)
            elif tile < TILES - 1:
                carry_ref[pl.ds(r0, n)] += group_totals(layer)
        for r0, n in chunks:
            here = acc_ref[pl.ds(PAD + r0, n)]
            up = acc_ref[pl.ds(PAD + r0 - 1, n)]
            face_x = thick8 * jnp.where(min_ref[0, pl.ds(r0, n)] > level_of, here - up, 0.0)
            face_y = thick8 * jnp.where(min_ref[1, pl.ds(r0, n)] > level_of, here - roll(here, 1), 0.0)
            if tile > 0:
                face_x += fx_ref[side, pl.ds(r0, n)]
                face_y += fy_ref[side, pl.ds(r0, n)]
            if tile == TILES - 1:
                face_x = roll(group_totals(face_x), 8)
                face_y = roll(group_totals(face_y), 8)
            fx_ref[side, pl.ds(r0, n)] = face_x
            fy_ref[side, pl.ds(r0, n)] = face_y


def lane_left(main, side):
    lane = lane_iota(main.shape[0])
    a, b = roll(main, 1), roll(side, 1)
    return jnp.where(lane == 0, b, a), jnp.where(lane == 0, a, b)


def lane_right(main, side):
    lane = lane_iota(main.shape[0])
    a, b = roll(main, -1), roll(side, -1)
    return jnp.where(lane == LANES - 1, b, a), jnp.where(lane == LANES - 1, a, b)


def solve_kernel(
    mixing_ref,
    thick_ref,
    fx_ref,
    fy_ref,
    from_left_ref,
    from_right_ref,
    to_right_ref,
    to_left_ref,
    top_ref,
    bottom_ref,
    levels_ref,
    land_ref,
    v_ref,
    d_ref,
    sums_ref,
    eff_ref,
    min_ref,
    u_ref,
    l_ref,
    acc_ref,
    carry_ref,
    sfx_ref,
    sfy_ref,
    full_fx_ref,
    full_fy_ref,
    dl_ref,
    dr_ref,
    w_ref,
    p_ref,
    q_ref,
):
    chunks = blocks(0, EXT, 32)
    by = lax.axis_index("by")
    last = lax.axis_size("by") - 1
    for ref in (eff_ref, u_ref, l_ref, acc_ref, d_ref, v_ref, dl_ref, dr_ref, p_ref, q_ref, full_fx_ref):
        ref[...] = jnp.zeros(ref.shape, ref.dtype)

    common = (mixing_ref, thick_ref)
    rest = (min_ref, u_ref, l_ref, acc_ref, carry_ref, sfx_ref, sfy_ref)
    strip_side(0, to_left_ref, from_left_ref, by != 0, *common, eff_ref.at[0], *rest)
    strip_side(1, to_right_ref, from_right_ref, by != last, *common, eff_ref.at[1], *rest)

    for r0, n in chunks:
        lane = lane_iota(n)
        own = pl.ds(r0, n)
        for full, main, strip in ((full_fx_ref, fx_ref, sfx_ref), (full_fy_ref, fy_ref, sfy_ref)):
            west, east = strip[0, own], strip[1, own]
            full[0, pl.ds(PAD + r0, n)] = jnp.where(
                lane < 4, west, jnp.where(lane >= LANES - 4, east, main[own])
            )
            full[1, pl.ds(PAD + r0, n)] = jnp.where(
                lane < 8, east, jnp.where(lane >= LANES - 8, west, 0.0)
            )
    for r0, n in CHUNKS:
        lane = lane_iota(n)
        if r0 < HALO:
            e_main = top_ref[2 * KL].astype(I32)
        elif r0 >= HALO + ROWS:
            e_main = bottom_ref[2 * KL].astype(I32)
        else:
            own = pl.ds(r0 - HALO, n)
            e_main = wet_levels(levels_ref[own], land_ref[own])
        west = roll(eff_ref[0, pl.ds(PAD + r0, n)], 8)
        east = roll(eff_ref[1, pl.ds(PAD + r0, n)], 8)
        e_side = jnp.where(lane < 8, east, jnp.where(lane >= LANES - 8, west, 0))
        d_main = jnp.zeros((n, LANES), F32)
        d_side = d_main
        for k in range(KL):
            thick = thick_ref[k]
            d_main += jnp.where(e_main > k, thick, 0.0)
            d_side += jnp.where(e_side > k, thick, 0.0)
        here = pl.ds(PAD + r0, n)
        d_ref[0, here], d_ref[1, here] = d_main, d_side
        dl_ref[0, here], dl_ref[1, here] = lane_left(d_main, d_side)
        dr_ref[0, here], dr_ref[1, here] = lane_right(d_main, d_side)

    for r0, n in chunks:
        here = pl.ds(PAD + r0, n)
        above = pl.ds(PAD + r0 - 1, n)
        below = pl.ds(PAD + r0 + 1, n)
        east = lane_right(full_fy_ref[0, here], full_fy_ref[1, here])
        for t in range(2):
            fx = full_fx_ref[t, here] - full_fx_ref[t, below]
            fy = full_fy_ref[t, here] - east[t]
            v_ref[0, t, here] = 10.0 * (fx + fy)
            d = d_ref[t, here]
            left, right = dl_ref[t, here], dr_ref[t, here]
            up, down = d_ref[t, above], d_ref[t, below]
            w_west, w_east = jnp.minimum(d, left), jnp.minimum(d, right)
            w_up, w_down = jnp.minimum(d, up), jnp.minimum(d, down)
            corners = (
                jnp.minimum(d, dl_ref[t, above])
                + jnp.minimum(d, dr_ref[t, below])
                + jnp.minimum(d, dr_ref[t, above])
                + jnp.minimum(d, dl_ref[t, below])
            )
            at = pl.ds(r0, n)
            w_ref[0, t, at] = 0.05 + w_up + w_down + w_west + w_east + 0.25 * corners
            w_ref[1, t, at] = w_west
            w_ref[2, t, at] = w_east
            w_ref[3, t, at] = w_down
            w_ref[4, t, at] = 0.25 * jnp.minimum(down, left)
            w_ref[5, t, at] = 0.25 * jnp.minimum(down, right)
            w_ref[6, t, at] = w_up
            w_ref[7, t, at] = 0.25 * jnp.minimum(up, left)
            w_ref[8, t, at] = 0.25 * jnp.minimum(up, right)

    def power(step, carry):
        for r0, n in chunks:
            here = pl.ds(PAD + r0, n)
            at = pl.ds(r0, n)
            v = (v_ref[step, 0, here], v_ref[step, 1, here])
            left = lane_left(*v)
            right = lane_right(*v)
            for t in range(2):
                w = [w_ref[m, t, at] for m in range(9)]
                p_ref[t, here] = w[3] * v[t] + w[4] * left[t] + w[5] * right[t]
                q_ref[t, here] = w[6] * v[t] + w[7] * left[t] + w[8] * right[t]
                v_ref[step + 1, t, here] = w[0] * v[t] - (w[1] * left[t] + w[2] * right[t])
        for r0, n in chunks:
            here = pl.ds(PAD + r0, n)
            for t in range(2):
                beside = p_ref[t, pl.ds(PAD + r0 - 1, n)] + q_ref[t, pl.ds(PAD + r0 + 1, n)]
                v_ref[step + 1, t, here] -= beside
        return carry

    lax.fori_loop(0, 4, power, 0)

    def dots(step, carry):
        at = pl.ds(pl.multiple_of(PAD + HALO + 8 * step, 8), 8)
        v = [v_ref[i, 0, at] for i in range(5)]
        parts = [split(x) for x in v]
        out = []
        for m in range(MOMENTS):
            i, j = m // 2, (m + 1) // 2
            p, e = two_prod(v[i], v[j], parts[i], parts[j])
            s, f = two_sum(carry[2 * m], p)
            out += [s, carry[2 * m + 1] + (e + f)]
        return tuple(out)

    zero = jnp.zeros((8, LANES), F32)
    sums = lax.fori_loop(0, ROWS // 8, dots, (zero,) * (2 * MOMENTS))
    sub = lax.broadcasted_iota(I32, (8, LANES), 0)
    pairs = [(sums[2 * m], sums[2 * m + 1]) for m in range(MOMENTS)]
    for half in (4, 2, 1):
        merged = []
        for m in range(half):
            a, b = pairs[m], pairs[m + half]
            upper = (sub & half) == 0
            keep = tuple(jnp.where(upper, x, y) for x, y in zip(a, b))
            other = tuple(jnp.where(upper, pltpu.roll(x, 8 - half, 0), pltpu.roll(y, half, 0)) for x, y in zip(a, b))
            merged.append(pair_add(keep, other))
        pairs = merged
    total = pairs[0]
    for shift in (1, 2, 4, 8, 16, 32, 64):
        total = pair_add(total, tuple(roll(x, shift) for x in total))
    lane = lane_iota(8)
    row = jnp.where(lane == sub, total[0], jnp.where(lane == sub + MOMENTS, total[1], 0.0))
    for shift in (4, 2, 1):
        row = row + pltpu.roll(row, shift, 0)
    for at in range(0, sums_ref.shape[0], 8):
        sums_ref[pl.ds(at, 8)] = row


def tracer_kernel(
    mixing_ref,
    t_ref,
    top_ref,
    bottom_ref,
    levels_ref,
    land_ref,
    from_left_ref,
    from_right_ref,
    to_right_ref,
    to_left_ref,
    out_ref,
    eff_ref,
    word_ref,
    u_ref,
    l_ref,
    edge_ref,
    seff_ref,
    su_ref,
    sl_ref,
):
    part = pl.program_id(0)
    by = lax.axis_index("by")
    last = lax.axis_size("by") - 1
    own_chunks = blocks(HALO, HALO + ROWS, 32)

    @pl.when(part == 0)
    def _():
        wet_setup(eff_ref, None, word_ref, top_ref, bottom_ref, levels_ref, land_ref)
        for ref in (u_ref, l_ref, seff_ref, su_ref, sl_ref):
            ref[...] = jnp.zeros(ref.shape, ref.dtype)
        chunks = blocks(0, EXT, 32)
        slot = KL - 2 * (LANES // GROUP)
        for side in range(2):
            near_ref, far_ref = (to_left_ref, from_left_ref) if side == 0 else (to_right_ref, from_right_ref)
            keep = (by != 0) if side == 0 else (by != last)

            def field(tile, which, r0, n):
                first = (lane_iota(n) & 8) == 0
                near = near_ref[tile, pl.ds(r0, n)]
                far = far_ref[tile, pl.ds(r0, n)]
                low, high = (far, near) if side == 0 else (near, far)
                if which == 0:
                    return jnp.where(first, low, roll(high, 8))
                return jnp.where(first, roll(low, -8), high)

            for r0, n in chunks:
                lane = lane_iota(n)
                x = field(2, 0, r0, n)
                inner = (lane & 8) == (8 if side == 0 else 0)
                x = jnp.where(jnp.logical_and(lane // GROUP == slot, jnp.logical_or(inner, keep)), x, 0.0)
                seff_ref[pl.ds(PAD + r0, n)] = group_totals(x).astype(I32)
            for tile in range(TILES):
                group8 = lane_iota(8) // GROUP
                level_of = group8[0:1] + tile * (LANES // GROUP)
                mix = []
                for c in range(2):
                    m = jnp.zeros((8, LANES), F32)
                    for g in range(LANES // GROUP):
                        k = tile * (LANES // GROUP) + g
                        if k < KL:
                            m = jnp.where(group8 == g, mixing_ref[k, c], m)
                    mix.append(m[0:1])

                def count(r0, n):
                    e = seff_ref[pl.ds(PAD + r0, n)]
                    total = jnp.where(seff_ref[pl.ds(PAD + r0 - 1, n)] > level_of, 1.0, 0.0)
                    total += jnp.where(seff_ref[pl.ds(PAD + r0 + 1, n)] > level_of, 1.0, 0.0)
                    total += jnp.where(roll(e, 1) > level_of, 1.0, 0.0)
                    return total + jnp.where(roll(e, -1) > level_of, 1.0, 0.0)

                for c in range(2):
                    for r0, n in chunks:
                        wet = seff_ref[pl.ds(PAD + r0, n)] > level_of
                        su_ref[pl.ds(PAD + r0, n)] = jnp.where(wet, field(tile, c, r0, n), 0.0)
                    for r0, n in chunks:
                        wet = seff_ref[pl.ds(PAD + r0, n)] > level_of
                        x, around = neighbours(su_ref, r0, n)
                        sl_ref[pl.ds(PAD + r0, n)] = jnp.where(wet, around, 0.0) - count(r0, n) * x
                    for r0, n in own_chunks:
                        first = (lane_iota(n) & 8) == 0
                        wet = seff_ref[pl.ds(PAD + r0, n)] > level_of
                        x, around = neighbours(sl_ref, r0, n)
                        second = jnp.where(wet, around, 0.0) - count(r0, n) * x
                        new = field(tile, c, r0, n) - mix[c] * second
                        own = pl.ds(r0 - HALO, n)
                        if side == 0:
                            edge_ref[c, tile, own] = new
                        else:
                            edge_ref[c, tile, own] = jnp.where(first, new, edge_ref[c, tile, own])

    def level(step, carry):
        k = part * (KL // HALF_STEPS) + step
        tile = k // (LANES // GROUP)
        back = (2 * LANES - 8 - GROUP * (k % (LANES // GROUP))) % LANES
        for r0, n in CHUNKS:
            wet = eff_ref[pl.ds(PAD + r0, n)] > k
            for c in range(2):
                a = ext_rows(t_ref, top_ref, bottom_ref, (step, c), 2 * k + c, r0, n)
                u_ref[c, pl.ds(PAD + r0, n)] = jnp.where(wet, a, 0.0)
        for r0, n in CHUNKS:
            wet = eff_ref[pl.ds(PAD + r0, n)] > k
            number = wet_count(word_ref, k, r0, n)
            for c in range(2):
                x, around = neighbours(u_ref.at[c], r0, n)
                l_ref[c, pl.ds(PAD + r0, n)] = jnp.where(wet, around, 0.0) - number * x
        for r0, n in own_chunks:
            lane = lane_iota(n)
            middle = jnp.logical_and(lane >= 4, lane < LANES - 4)
            wet = eff_ref[pl.ds(PAD + r0, n)] > k
            number = wet_count(word_ref, k, r0, n)
            own = pl.ds(r0 - HALO, n)
            for c in range(2):
                x, around = neighbours(l_ref.at[c], r0, n)
                second = jnp.where(wet, around, 0.0) - number * x
                new = t_ref[step, c, own] - mixing_ref[k, c] * second
                edge = pltpu.roll(edge_ref[c, tile, own], back, 1)
                out_ref[step, c, own] = jnp.where(middle, new, edge)
        return carry

    lax.fori_loop(0, KL // HALF_STEPS, level, 0)


def finish_kernel(all_ref, v_ref, d_ref, surface_ref, flow_ref, s_ref):
    zero = jnp.zeros((8, LANES), F32)
    high, low = zero, zero
    for at in range(0, all_ref.shape[0], 8):
        high, e = two_sum(high, all_ref[pl.ds(at, 8)])
        low = low + e
    total = (high, low)
    for shift in (4, 2, 1):
        total = pair_add(total, tuple(pltpu.roll(x, shift, 0) for x in total))
    total = pair_add(total, tuple(roll(x, -MOMENTS) for x in total))
    lane = lane_iota(8)

    def moment(m):
        return tuple(
            jnp.broadcast_to(jnp.sum(jnp.where(lane == m, x, 0.0), axis=1, keepdims=True), (8, LANES))
            for x in total
        )

    rho = [moment(m) for m in range(MOMENTS)]
    pi = list(rho)
    nought = (zero, zero)
    one = (zero + 1.0, zero)
    surface = [nought] * 4
    residual = [one] + [nought] * 3
    direction = list(residual)
    for step in range(4):
        alpha = pair_clip(pair_div(rho[step], pi[step + 1]), 20.0)
        for i in range(step + 1):
            surface[i] = pair_add(surface[i], pair_mul(alpha, direction[i]))
        if step == 3:
            break
        minus = pair_neg(alpha)
        new_rho = list(rho)
        for m in range(step + 1, MOMENTS - 1 - step):
            new_rho[m] = pair_add(rho[m], pair_mul(minus, pi[m + 1]))
        beta = pair_clip(pair_div(pair_mul(minus, new_rho[step + 1]), rho[step]), 400.0)
        for m in range(step + 2, MOMENTS - 1 - step):
            pi[m] = pair_add(new_rho[m], pair_mul(beta, pi[m]))
        rho = new_rho
        for i in range(step + 1, 0, -1):
            residual[i] = pair_add(residual[i], pair_mul(minus, direction[i - 1]))
        for i in range(step + 2):
            direction[i] = pair_add(residual[i], pair_mul(beta, direction[i]))
    weight = [s[0][0:1] for s in surface]

    def combine(side, r0, n):
        at = pl.ds(PAD + r0, n)
        total = weight[0] * v_ref[0, side, at]
        for i in range(1, 4):
            total = total + weight[i] * v_ref[i, side, at]
        return total

    chunks = [(0, HALO)] + blocks(HALO, HALO + ROWS, 32)
    for r0, n in chunks:
        s_ref[pl.ds(r0, n)] = combine(0, r0, n)
    for r0, n in chunks[1:]:
        s = s_ref[pl.ds(r0, n)]
        own = pl.ds(r0 - HALO, n)
        here = pl.ds(PAD + r0, n)
        west, _ = lane_left(s, combine(1, r0, n))
        d_west, _ = lane_left(d_ref[0, here], d_ref[1, here])
        d = d_ref[0, here]
        surface_ref[own] = s
        flow_ref[0, own] = jnp.minimum(d, d_ref[0, pl.ds(PAD + r0 - 1, n)]) * (s_ref[pl.ds(r0 - 1, n)] - s)
        flow_ref[1, own] = jnp.minimum(d, d_west) * (west - s)


VM = pl.BlockSpec(memory_space=pltpu.VMEM)
SM = pl.BlockSpec(memory_space=pltpu.SMEM)


def params(**kwargs):
    return pltpu.CompilerParams(vmem_limit_bytes=VMEM_LIMIT, **kwargs)


def ring(x, axis, step):
    count = lax.axis_size(axis)
    return lax.ppermute(x, axis, [(i, (i + step) % count) for i in range(count)])


def shards(tracers, mixing, thickness, levels, land):
    devices = lax.axis_size("bx") * lax.axis_size("by")
    wet = wet_levels(levels, land).astype(F32)
    flat = tracers.reshape(2 * KL, ROWS, LANES)
    with jax.named_scope("rows"):
        to_up = jnp.concatenate([flat[:, :HALO], wet[None, :HALO]])
        to_down = jnp.concatenate([flat[:, -HALO:], wet[None, -HALO:]])
        top = ring(to_down, "bx", 1)
        bottom = ring(to_up, "bx", -1)
    edge_shape = jax.ShapeDtypeStruct((TILES, EXT, LANES), F32)
    with jax.named_scope("columns"):
        to_right, to_left = pl.pallas_call(
            pack_kernel,
            out_shape=(edge_shape, edge_shape),
            in_specs=[VM] * 5,
            out_specs=(VM, VM),
            compiler_params=params(),
            cost_estimate=pl.CostEstimate(flops=10_000_000, bytes_accessed=7_000_000, transcendentals=0),
        )(tracers, top, bottom, levels, land)
        from_left = ring(to_right, "by", 1)
        from_right = ring(to_left, "by", -1)
    level_block = pl.BlockSpec((KL // HALF_STEPS, 2, ROWS, LANES), lambda i: (i, 0, 0, 0))
    plane = jax.ShapeDtypeStruct((EXT, LANES), F32)
    buf = pltpu.VMEM((BUF, LANES), F32)
    buf2 = pltpu.VMEM((2, BUF, LANES), F32)
    with jax.named_scope("density"):
        fx, fy = pl.pallas_call(
            density_kernel,
            grid=(HALF_STEPS,),
            out_shape=(plane, plane),
            in_specs=[SM, SM, level_block, VM, VM, VM, VM],
            out_specs=(VM, VM),
            scratch_shapes=[
                pltpu.VMEM((BUF, LANES), I32),
                pltpu.VMEM((2, EXT, LANES), I32),
                pltpu.VMEM((3, EXT, LANES), I32),
                buf,
                buf,
                buf,
            ],
            compiler_params=params(),
            cost_estimate=pl.CostEstimate(flops=50_000_000, bytes_accessed=7_000_000, transcendentals=0),
        )(mixing, thickness, tracers, top, bottom, levels, land)
    edges = (from_left, from_right, to_right, to_left)
    with jax.named_scope("powers"):
        powers, depth, sums = pl.pallas_call(
            solve_kernel,
            out_shape=(
                jax.ShapeDtypeStruct((5, 2, BUF, LANES), F32),
                jax.ShapeDtypeStruct((2, BUF, LANES), F32),
                jax.ShapeDtypeStruct((devices, LANES), F32),
            ),
            in_specs=[SM, SM] + [VM] * 10,
            out_specs=(VM, VM, VM),
            scratch_shapes=[
                pltpu.VMEM((2, BUF, LANES), I32),
                pltpu.VMEM((2, EXT, LANES), I32),
                buf,
                buf,
                buf,
                pltpu.VMEM((EXT, LANES), F32),
                pltpu.VMEM((2, EXT, LANES), F32),
                pltpu.VMEM((2, EXT, LANES), F32),
                buf2,
                buf2,
                buf2,
                buf2,
                pltpu.VMEM((9, 2, EXT, LANES), F32),
                buf2,
                buf2,
            ],
            compiler_params=params(),
            cost_estimate=pl.CostEstimate(flops=50_000_000, bytes_accessed=6_000_000, transcendentals=0),
        )(mixing, thickness, fx, fy, *edges, top, bottom, levels, land)
    with jax.named_scope("sums"):
        everyone = lax.all_to_all(sums, ("bx", "by"), 0, 0, tiled=True)
    with jax.named_scope("tracers"):
        tracers_new = pl.pallas_call(
            tracer_kernel,
            grid=(HALF_STEPS,),
            out_shape=jax.ShapeDtypeStruct(tracers.shape, F32),
            in_specs=[SM, level_block] + [VM] * 8,
            out_specs=level_block,
            scratch_shapes=[
                pltpu.VMEM((BUF, LANES), I32),
                pltpu.VMEM((3, EXT, LANES), I32),
                buf2,
                buf2,
                pltpu.VMEM((2, TILES, ROWS, LANES), F32),
                pltpu.VMEM((BUF, LANES), I32),
                buf,
                buf,
            ],
            compiler_params=params(),
            cost_estimate=pl.CostEstimate(flops=80_000_000, bytes_accessed=13_000_000, transcendentals=0),
        )(mixing, tracers, top, bottom, levels, land, *edges)
    with jax.named_scope("surface"):
        surface, transports = pl.pallas_call(
            finish_kernel,
            out_shape=(
                jax.ShapeDtypeStruct((ROWS, LANES), F32),
                jax.ShapeDtypeStruct((2, ROWS, LANES), F32),
            ),
            in_specs=[VM] * 3,
            out_specs=(VM, VM),
            scratch_shapes=[pltpu.VMEM((HALO + ROWS, LANES), F32)],
            compiler_params=params(),
            cost_estimate=pl.CostEstimate(flops=1_000_000, bytes_accessed=3_000_000, transcendentals=0),
        )(everyone, powers, depth)
    return tracers_new, surface, transports


def solution(mesh):
    in_specs = (P(None, None, "bx", "by"), P(), P(), P("bx", "by"), P("bx", "by"))
    out_specs = (P(None, None, "bx", "by"), P("bx", "by"), P(None, "bx", "by"))
    return jax.shard_map(shards, mesh=mesh, in_specs=in_specs, out_specs=out_specs, check_vma=False)
```

```python
import jax
import jax.numpy as jnp
from jax import lax
from jax.experimental import pallas as pl
from jax.experimental.pallas import tpu as pltpu
from jax.sharding import PartitionSpec as P

KL = 22
ROWS = 256
LANES = 128
HALO = 8
EXT = ROWS + 2 * HALO
PAD = 8
BUF = EXT + 2 * PAD
GROUP = 16
GROUPS = LANES // GROUP
TILES = 3
LOADS = 4
MOMENTS = 8
F32 = jnp.float32
I32 = jnp.int32
VMEM_LIMIT = 20 * 1024 * 1024


def lane_iota(rows):
    return lax.broadcasted_iota(I32, (rows, LANES), 1)


def first_half(rows):
    return (lane_iota(rows) & 8) == 0


def roll(x, shift):
    return pltpu.roll(x, shift % LANES, 1)


def blocks(start, stop, size):
    out = []
    while start < stop:
        out.append((start, min(size, stop - start)))
        start += size
    return out


CHUNKS = blocks(0, EXT, 32)
OWN_CHUNKS = blocks(HALO, HALO + ROWS, 32)


def wet_levels(levels, land):
    return jnp.where(land == 0, levels, 0)


def edge_slot(k):
    return k % TILES, k // TILES


def place(x, k, old):
    _, g = edge_slot(k)
    return jnp.where(lane_iota(x.shape[0]) // GROUP == g, roll(x, 8 + GROUP * g), old)


def to_neighbours(a, b):
    first = first_half(a.shape[0])
    return jnp.where(first, a, roll(b, 8)), jnp.where(first, roll(b, -8), a)


def own_edges_kernel(t_ref, levels_ref, land_ref, ext_ref, eff_ref, edge_ref, right_ref, left_ref, sems):
    parts = blocks(0, KL, -(-KL // LOADS))

    def copy(i):
        start, count = parts[i]
        return pltpu.make_async_copy(
            t_ref.at[pl.ds(2 * start, 2 * count)],
            ext_ref.at[pl.ds(2 * start, 2 * count), pl.ds(HALO, ROWS)],
            sems.at[i],
        )

    for i in range(len(parts)):
        copy(i).start()
    eff_ref[pl.ds(HALO, ROWS)] = wet_levels(levels_ref[...], land_ref[...])
    size = 64
    tile_eff, _ = edge_slot(KL)

    def clear(step, carry):
        at = pl.ds(pl.multiple_of(HALO + size * step, 8), size)
        zero = jnp.zeros((size, LANES), F32)
        for c in range(2):
            for tile in range(TILES):
                edge_ref[c, tile, at] = zero
            edge_ref[c, tile_eff, at] = place(eff_ref[at].astype(F32), KL, zero)
        return carry

    lax.fori_loop(0, ROWS // size, clear, 0)
    for i, (start, count) in enumerate(parts):
        copy(i).wait()

        def rows(step, carry):
            at = pl.ds(pl.multiple_of(HALO + size * step, 8), size)
            for k in range(start, start + count):
                tile, _ = edge_slot(k)
                for c in range(2):
                    edge_ref[c, tile, at] = place(ext_ref[2 * k + c, at], k, edge_ref[c, tile, at])
            return carry

        lax.fori_loop(0, ROWS // size, rows, 0)

    def send(step, carry):
        at = pl.ds(pl.multiple_of(HALO + size * step, 8), size)
        for tile in range(TILES):
            right_ref[tile, at], left_ref[tile, at] = to_neighbours(edge_ref[0, tile, at], edge_ref[1, tile, at])
        return carry

    lax.fori_loop(0, ROWS // size, send, 0)


def halo_edges_kernel(
    top_ref, bottom_ref, ext_in, eff_in, edge_in, right_in, left_in, ext_ref, eff_ref, edge_ref, right_ref, left_ref
):
    for r0, ref in ((0, top_ref), (HALO + ROWS, bottom_ref)):
        at = pl.ds(r0, HALO)
        eff = ref[2 * KL]
        eff_ref[at] = eff.astype(I32)
        held = [[jnp.zeros((HALO, LANES), F32) for _ in range(TILES)] for _ in range(2)]
        for k in range(KL + 1):
            tile, _ = edge_slot(k)
            for c in range(2):
                if k < KL:
                    x = ref[2 * k + c]
                    ext_ref[2 * k + c, at] = x
                else:
                    x = eff
                held[c][tile] = place(x, k, held[c][tile])
        for tile in range(TILES):
            for c in range(2):
                edge_ref[c, tile, at] = held[c][tile]
            right_ref[tile, at], left_ref[tile, at] = to_neighbours(held[0][tile], held[1][tile])


def count_word(effs, word):
    total = None
    for eff in effs:
        bits = jnp.clip(eff - 10 * word, 0, 10) * 3
        mask = (lax.shift_left(jnp.full_like(bits, 1), bits) - 1) & 0o1111111111
        total = mask if total is None else total + mask
    return total


def neighbours(ref, r0, n):
    x = ref[pl.ds(PAD + r0, n)]
    around = ref[pl.ds(PAD + r0 - 1, n)] + ref[pl.ds(PAD + r0 + 1, n)]
    return x, around + (roll(x, 1) + roll(x, -1))


def block_kernel(
    mixing_ref,
    thick_ref,
    ext_ref,
    eff_in,
    new_ref,
    fx_ref,
    fy_ref,
    eff_ref,
    min_ref,
    word_ref,
    u_ref,
    l_ref,
    acc_ref,
):
    eff_ref[...] = jnp.zeros(eff_ref.shape, I32)
    eff_ref[pl.ds(PAD, EXT)] = eff_in[...]
    for ref in (u_ref, l_ref, acc_ref, fx_ref, fy_ref):
        ref[...] = jnp.zeros(ref.shape, F32)
    for r0, n in CHUNKS:
        e = eff_ref[pl.ds(PAD + r0, n)]
        min_ref[0, pl.ds(r0, n)] = jnp.minimum(e, eff_ref[pl.ds(PAD + r0 - 1, n)])
        min_ref[1, pl.ds(r0, n)] = jnp.minimum(e, roll(e, 1))
        effs = (eff_ref[pl.ds(PAD + r0 - 1, n)], eff_ref[pl.ds(PAD + r0 + 1, n)], roll(e, 1), roll(e, -1))
        for word in range(3):
            word_ref[word, pl.ds(r0, n)] = count_word(effs, word)

    def count(k, r0, n):
        words = word_ref[k // 10, pl.ds(r0, n)]
        shift = jnp.full((n, LANES), 3 * (k % 10), I32)
        return (lax.shift_right_logical(words, shift) & 7).astype(F32)

    def stage(step, late):
        k = jnp.clip(step - late, 0, KL - 1)
        valid = jnp.logical_and(step >= late, step < KL + late)
        return k, jnp.where(valid, thick_ref[k], 0.0)

    def body(step, carry):
        ku, _ = stage(step, 0)
        kl, _ = stage(step, 1)
        kd, thick_d = stage(step, 2)
        kf, thick_f = stage(step, 3)

        def flux(r0, n):
            here = acc_ref[pl.ds(PAD + r0, n)]
            up = acc_ref[pl.ds(PAD + r0 - 1, n)]
            face_x = min_ref[0, pl.ds(r0, n)] > kf
            face_y = min_ref[1, pl.ds(r0, n)] > kf
            fx_ref[pl.ds(r0, n)] += thick_f * jnp.where(face_x, here - up, 0.0)
            fy_ref[pl.ds(r0, n)] += thick_f * jnp.where(face_y, here - roll(here, 1), 0.0)

        def density(r0, n):
            wet = eff_ref[pl.ds(PAD + r0, n)] > kd
            number = count(kd, r0, n)
            new = []
            for c in range(2):
                x, around = neighbours(l_ref.at[c], r0, n)
                second = jnp.where(wet, around, 0.0) - number * x
                value = ext_ref[2 * kd + c, pl.ds(r0, n)] - mixing_ref[kd, c] * second
                low, high = max(r0, HALO), min(r0 + n, HALO + ROWS)
                new_ref[2 * kd + c, pl.ds(low - HALO, high - low)] = value[low - r0 : high - r0]
                new.append(value)
            plain = 0.8 * new[1] - 0.2 * new[0]
            acc_ref[pl.ds(PAD + r0, n)] += thick_d * jnp.where(wet, plain, 0.0)

        def first(r0, n):
            wet = eff_ref[pl.ds(PAD + r0, n)] > kl
            number = count(kl, r0, n)
            for c in range(2):
                x, around = neighbours(u_ref.at[c], r0, n)
                l_ref[c, pl.ds(PAD + r0, n)] = jnp.where(wet, around, 0.0) - number * x

        def masked(r0, n):
            wet = eff_ref[pl.ds(PAD + r0, n)] > ku
            for c in range(2):
                u_ref[c, pl.ds(PAD + r0, n)] = jnp.where(wet, ext_ref[2 * ku + c, pl.ds(r0, n)], 0.0)

        work = (flux, density, first, masked)
        for turn in range(len(CHUNKS) + len(work) - 1):
            for late, part in enumerate(work):
                if 0 <= turn - late < len(CHUNKS):
                    part(*CHUNKS[turn - late])
        return carry

    lax.fori_loop(0, KL + 3, body, 0)


def patch_kernel(new_in, edge_ref, new_ref):
    size = 32

    def level(k, carry):
        tile = k % TILES
        back = (2 * LANES - 8 - GROUP * (k // TILES)) % LANES
        for r0, n in blocks(0, ROWS, size):
            lane = lane_iota(n)
            middle = jnp.logical_and(lane >= 4, lane < LANES - 4)
            own = pl.ds(r0, n)
            for c in range(2):
                edge = pltpu.roll(edge_ref[c, tile, own], back, 1)
                new_ref[2 * k + c, own] = jnp.where(middle, new_in[2 * k + c, own], edge)
        return carry

    lax.fori_loop(0, KL, level, 0)


def two_sum(a, b):
    s = a + b
    v = s - a
    return s, (a - (s - v)) + (b - v)


def quick_sum(a, b):
    s = a + b
    return s, b - (s - a)


def split(a):
    t = a * 4097.0
    high = t - (t - a)
    return high, a - high


def two_prod(a, b, parts_a, parts_b):
    p = a * b
    ah, al = parts_a
    bh, bl = parts_b
    return p, ((ah * bh - p) + ah * bl + al * bh) + al * bl


def pair_add(x, y):
    s, e = two_sum(x[0], y[0])
    return quick_sum(s, e + (x[1] + y[1]))


def pair_mul(x, y):
    p, e = two_prod(x[0], y[0], split(x[0]), split(y[0]))
    return quick_sum(p, e + (x[0] * y[1] + x[1] * y[0]))


def pair_neg(x):
    return -x[0], -x[1]


def pair_div(x, y):
    q = x[0] / y[0]
    rest = pair_add(x, pair_neg(pair_mul(y, (q, jnp.zeros_like(q)))))
    return quick_sum(q, rest[0] / y[0])


def pair_clip(x, top):
    inside = jnp.logical_and(x[0] >= 0.0, x[0] <= top)
    high = jnp.where(inside, x[0], jnp.where(x[0] > top, top, 0.0))
    return high, jnp.where(inside, x[1], 0.0)


def group_totals(x):
    x = x + roll(x, GROUP)
    x = x + roll(x, 2 * GROUP)
    return x + roll(x, 4 * GROUP)


def lane_left(main, side):
    lane = lane_iota(main.shape[0])
    a, b = roll(main, 1), roll(side, 1)
    return jnp.where(lane == 0, b, a), jnp.where(lane == 0, a, b)


def lane_right(main, side):
    lane = lane_iota(main.shape[0])
    a, b = roll(main, -1), roll(side, -1)
    return jnp.where(lane == LANES - 1, b, a), jnp.where(lane == LANES - 1, a, b)


SIDES = (0, 1)


def solve_kernel(
    mixing_ref,
    thick_ref,
    fx_ref,
    fy_ref,
    from_left_ref,
    from_right_ref,
    edge_ref,
    eff_in,
    v_ref,
    d_ref,
    sums_ref,
    new_ref,
    e_ref,
    west_ref,
    east_ref,
    f_ref,
    u_ref,
    l_ref,
    n_ref,
    acc_ref,
    eff_ref,
    full_fx_ref,
    full_fy_ref,
    dl_ref,
    dr_ref,
    w_ref,
    p_ref,
    q_ref,
):
    by = lax.axis_index("by")
    open_side = (by != 0, by != lax.axis_size("by") - 1)

    def clear(ref):
        ref[...] = jnp.zeros(ref.shape, ref.dtype)

    for ref in (e_ref, west_ref, east_ref):
        clear(ref)
    for ref in (u_ref, l_ref, acc_ref, d_ref, v_ref, dl_ref, dr_ref, p_ref, q_ref, full_fx_ref, full_fy_ref):
        rank = len(ref.shape) - 2
        lead = [()]
        for size in ref.shape[:rank]:
            lead = [i + (j,) for i in lead for j in range(size)]
        for i in lead:
            for r0 in (0, BUF - PAD):
                ref[i + (pl.ds(r0, PAD),)] = jnp.zeros((PAD, LANES), F32)

    def field(side, c, tile, r0, n):
        own = edge_ref[c, tile, pl.ds(r0, n)]
        first = first_half(n)
        if side == 0:
            far = from_left_ref[tile, pl.ds(r0, n)]
            return jnp.where(first, roll(far, -8) if c else far, own)
        far = from_right_ref[tile, pl.ds(r0, n)]
        return jnp.where(first, own, roll(far, 8) if c else far)

    tile_eff, slot = edge_slot(KL)
    for side in SIDES:
        for r0, n in CHUNKS:
            lane = lane_iota(n)
            x = field(side, 0, tile_eff, r0, n)
            inner = (lane & 8) == (8 if side == 0 else 0)
            keep = jnp.logical_and(lane // GROUP == slot, jnp.logical_or(inner, open_side[side]))
            e = group_totals(jnp.where(keep, x, 0.0)).astype(I32)
            at = pl.ds(PAD + r0, n)
            e_ref[side, at] = e
            west_ref[side, at] = roll(e, 1)
            east_ref[side, at] = roll(e, -1)

    group8 = lane_iota(8) // GROUP

    def by_group(tile, values):
        out = jnp.zeros((8, LANES), F32)
        for g in range(GROUPS):
            k = TILES * g + tile
            value = values(jnp.minimum(k, KL - 1))
            out = jnp.where(group8 == g, jnp.where(k < KL, value, 0.0), out)
        return out[0:1]

    def level_lanes(tile):
        return (group8 * TILES + tile)[0:1]

    def tile_step(tile, carry):
        level_of = level_lanes(tile)
        mix = [by_group(tile, lambda k, c=c: mixing_ref[k, c]) for c in range(2)]
        thick = by_group(tile, lambda k: thick_ref[k])

        def masked(side, r0, n):
            at = pl.ds(PAD + r0, n)
            wet = e_ref[side, at] > level_of
            for c in range(2):
                x = field(side, c, tile, r0, n)
                f_ref[side, c, pl.ds(r0, n)] = x
                u_ref[side, c, at] = jnp.where(wet, x, 0.0)

        def first(side, r0, n):
            at = pl.ds(PAD + r0, n)
            wet = e_ref[side, at] > level_of
            number = jnp.where(e_ref[side, pl.ds(PAD + r0 - 1, n)] > level_of, 1.0, 0.0)
            number += jnp.where(e_ref[side, pl.ds(PAD + r0 + 1, n)] > level_of, 1.0, 0.0)
            number += jnp.where(west_ref[side, at] > level_of, 1.0, 0.0)
            number += jnp.where(east_ref[side, at] > level_of, 1.0, 0.0)
            n_ref[side, pl.ds(r0, n)] = number
            for c in range(2):
                x, around = neighbours(u_ref.at[side, c], r0, n)
                l_ref[side, c, at] = jnp.where(wet, around, 0.0) - number * x

        def density(side, r0, n):
            at = pl.ds(PAD + r0, n)
            wet = e_ref[side, at] > level_of
            number = n_ref[side, pl.ds(r0, n)]
            new = []
            for c in range(2):
                x, around = neighbours(l_ref.at[side, c], r0, n)
                second = jnp.where(wet, around, 0.0) - number * x
                new.append(f_ref[side, c, pl.ds(r0, n)] - mix[c] * second)
            acc_ref[side, tile, at] = thick * jnp.where(wet, 0.8 * new[1] - 0.2 * new[0], 0.0)
            low, high = max(r0, HALO), min(r0 + n, HALO + ROWS)
            own = pl.ds(low - HALO, high - low)
            for c in range(2):
                value = new[c][low - r0 : high - r0]
                if side == 1:
                    value = jnp.where(first_half(high - low), value, new_ref[c, tile, own])
                new_ref[c, tile, own] = value

        for part in (masked, first, density):
            for side in SIDES:
                for r0, n in CHUNKS:
                    part(side, r0, n)
        return carry

    lax.fori_loop(0, TILES, tile_step, 0)

    for side in SIDES:
        for r0, n in CHUNKS:
            lane = lane_iota(n)
            at = pl.ds(PAD + r0, n)
            layers = [acc_ref[side, tile, at] for tile in range(TILES)]
            run = (layers[0] + layers[1]) + layers[2]
            run = jnp.where(lane >= GROUP, roll(run, GROUP), 0.0)
            for step in (1, 2, 4):
                run = run + jnp.where(lane >= step * GROUP, roll(run, step * GROUP), 0.0)
            for tile in range(TILES):
                run = run + layers[tile]
                acc_ref[side, tile, at] = run
    thick = [by_group(tile, lambda k: thick_ref[k]) for tile in range(TILES)]
    for r0, n in CHUNKS:
        lane = lane_iota(n)
        own = pl.ds(r0, n)
        at = pl.ds(PAD + r0, n)
        totals = []
        for side in SIDES:
            e = e_ref[side, at]
            min_x = jnp.minimum(e, e_ref[side, pl.ds(PAD + r0 - 1, n)])
            min_y = jnp.minimum(e, west_ref[side, at])
            face_x = jnp.zeros((n, LANES), F32)
            face_y = face_x
            for tile in range(TILES):
                here = acc_ref[side, tile, at]
                up = acc_ref[side, tile, pl.ds(PAD + r0 - 1, n)]
                level_of = level_lanes(tile)
                face_x += thick[tile] * jnp.where(min_x > level_of, here - up, 0.0)
                face_y += thick[tile] * jnp.where(min_y > level_of, here - roll(here, 1), 0.0)
            totals.append([roll(group_totals(x), 8) for x in (face_x, face_y)])
        for full, main, west, east in (
            (full_fx_ref, fx_ref, totals[0][0], totals[1][0]),
            (full_fy_ref, fy_ref, totals[0][1], totals[1][1]),
        ):
            full[0, at] = jnp.where(lane < 4, west, jnp.where(lane >= LANES - 4, east, main[own]))
            full[1, at] = jnp.where(lane < 8, east, jnp.where(lane >= LANES - 8, west, 0.0))
        west = roll(e_ref[0, at], 8)
        east = roll(e_ref[1, at], 8)
        eff_ref[0, own] = eff_in[own]
        eff_ref[1, own] = jnp.where(lane < 8, east, jnp.where(lane >= LANES - 8, west, 0))

    def depths(step, carry):
        n = 16
        r0 = pl.multiple_of(step * n, 8)
        for t in range(2):
            e = eff_ref[t, pl.ds(r0, n)]
            d = jnp.zeros((n, LANES), F32)
            for k in range(KL):
                d += jnp.where(e > k, thick_ref[k], 0.0)
            d_ref[t, pl.ds(pl.multiple_of(PAD + r0, 8), n)] = d
        return carry

    lax.fori_loop(0, EXT // 16, depths, 0)
    for r0, n in CHUNKS:
        here = pl.ds(PAD + r0, n)
        d_main, d_side = d_ref[0, here], d_ref[1, here]
        dl_ref[0, here], dl_ref[1, here] = lane_left(d_main, d_side)
        dr_ref[0, here], dr_ref[1, here] = lane_right(d_main, d_side)

    for r0, n in CHUNKS:
        here = pl.ds(PAD + r0, n)
        east = lane_right(full_fy_ref[0, here], full_fy_ref[1, here])
        for t in range(2):
            fx = full_fx_ref[t, here] - full_fx_ref[t, pl.ds(PAD + r0 + 1, n)]
            fy = full_fy_ref[t, here] - east[t]
            v_ref[0, t, here] = 10.0 * (fx + fy)

    def weights(t, carry):
        for r0, n in CHUNKS:
            here = pl.ds(PAD + r0, n)
            above = pl.ds(PAD + r0 - 1, n)
            below = pl.ds(PAD + r0 + 1, n)
            d = d_ref[t, here]
            left, right = dl_ref[t, here], dr_ref[t, here]
            up, down = d_ref[t, above], d_ref[t, below]
            w_west, w_east = jnp.minimum(d, left), jnp.minimum(d, right)
            w_up, w_down = jnp.minimum(d, up), jnp.minimum(d, down)
            corners = (
                jnp.minimum(d, dl_ref[t, above])
                + jnp.minimum(d, dr_ref[t, below])
                + jnp.minimum(d, dr_ref[t, above])
                + jnp.minimum(d, dl_ref[t, below])
            )
            at = pl.ds(r0, n)
            w_ref[0, t, at] = 0.05 + w_up + w_down + w_west + w_east + 0.25 * corners
            w_ref[1, t, at] = w_west
            w_ref[2, t, at] = w_east
            w_ref[3, t, at] = w_down
            w_ref[4, t, at] = 0.25 * jnp.minimum(down, left)
            w_ref[5, t, at] = 0.25 * jnp.minimum(down, right)
            w_ref[6, t, at] = w_up
            w_ref[7, t, at] = 0.25 * jnp.minimum(up, left)
            w_ref[8, t, at] = 0.25 * jnp.minimum(up, right)
        return carry

    lax.fori_loop(0, 2, weights, 0)

    def power(step, carry):
        for r0, n in CHUNKS:
            here = pl.ds(PAD + r0, n)
            at = pl.ds(r0, n)
            v = (v_ref[step, 0, here], v_ref[step, 1, here])
            left = lane_left(*v)
            right = lane_right(*v)
            for t in range(2):
                w = [w_ref[m, t, at] for m in range(9)]
                p_ref[t, here] = w[3] * v[t] + w[4] * left[t] + w[5] * right[t]
                q_ref[t, here] = w[6] * v[t] + w[7] * left[t] + w[8] * right[t]
                v_ref[step + 1, t, here] = w[0] * v[t] - (w[1] * left[t] + w[2] * right[t])
        for r0, n in CHUNKS:
            here = pl.ds(PAD + r0, n)
            for t in range(2):
                beside = p_ref[t, pl.ds(PAD + r0 - 1, n)] + q_ref[t, pl.ds(PAD + r0 + 1, n)]
                v_ref[step + 1, t, here] -= beside
        return carry

    lax.fori_loop(0, 4, power, 0)

    def dots(step, carry):
        at = pl.ds(pl.multiple_of(PAD + HALO + 8 * step, 8), 8)
        v = [v_ref[i, 0, at] for i in range(5)]
        parts = [split(x) for x in v]
        out = []
        for m in range(MOMENTS):
            i, j = m // 2, (m + 1) // 2
            p, e = two_prod(v[i], v[j], parts[i], parts[j])
            s, f = two_sum(carry[2 * m], p)
            out += [s, carry[2 * m + 1] + (e + f)]
        return tuple(out)

    zero = jnp.zeros((8, LANES), F32)
    sums = lax.fori_loop(0, ROWS // 8, dots, (zero,) * (2 * MOMENTS), unroll=4)
    sub = lax.broadcasted_iota(I32, (8, LANES), 0)
    pairs = [(sums[2 * m], sums[2 * m + 1]) for m in range(MOMENTS)]
    for half in (4, 2, 1):
        merged = []
        for m in range(half):
            a, b = pairs[m], pairs[m + half]
            upper = (sub & half) == 0
            keep = tuple(jnp.where(upper, x, y) for x, y in zip(a, b))
            other = tuple(jnp.where(upper, pltpu.roll(x, 8 - half, 0), pltpu.roll(y, half, 0)) for x, y in zip(a, b))
            merged.append(pair_add(keep, other))
        pairs = merged
    total = pairs[0]
    for shift in (1, 2, 4, 8, 16, 32, 64):
        total = pair_add(total, tuple(roll(x, shift) for x in total))
    lane = lane_iota(8)
    row = jnp.where(lane == sub, total[0], jnp.where(lane == sub + MOMENTS, total[1], 0.0))
    for shift in (4, 2, 1):
        row = row + pltpu.roll(row, shift, 0)
    for at in range(0, sums_ref.shape[0], 8):
        sums_ref[pl.ds(at, 8)] = row


def finish_kernel(all_ref, v_ref, d_ref, surface_ref, flow_ref, s_ref):
    zero = jnp.zeros((8, LANES), F32)
    high, low = zero, zero
    for at in range(0, all_ref.shape[0], 8):
        high, e = two_sum(high, all_ref[pl.ds(at, 8)])
        low = low + e
    total = (high, low)
    for shift in (4, 2, 1):
        total = pair_add(total, tuple(pltpu.roll(x, shift, 0) for x in total))
    total = pair_add(total, tuple(roll(x, -MOMENTS) for x in total))
    lane = lane_iota(8)

    def moment(m):
        return tuple(
            jnp.broadcast_to(jnp.sum(jnp.where(lane == m, x, 0.0), axis=1, keepdims=True), (8, LANES))
            for x in total
        )

    rho = [moment(m) for m in range(MOMENTS)]
    pi = list(rho)
    nought = (zero, zero)
    one = (zero + 1.0, zero)
    surface = [nought] * 4
    residual = [one] + [nought] * 3
    direction = list(residual)
    for step in range(4):
        alpha = pair_clip(pair_div(rho[step], pi[step + 1]), 20.0)
        for i in range(step + 1):
            surface[i] = pair_add(surface[i], pair_mul(alpha, direction[i]))
        if step == 3:
            break
        minus = pair_neg(alpha)
        new_rho = list(rho)
        for m in range(step + 1, MOMENTS - 1 - step):
            new_rho[m] = pair_add(rho[m], pair_mul(minus, pi[m + 1]))
        beta = pair_clip(pair_div(pair_mul(minus, new_rho[step + 1]), rho[step]), 400.0)
        for m in range(step + 2, MOMENTS - 1 - step):
            pi[m] = pair_add(new_rho[m], pair_mul(beta, pi[m]))
        rho = new_rho
        for i in range(step + 1, 0, -1):
            residual[i] = pair_add(residual[i], pair_mul(minus, direction[i - 1]))
        for i in range(step + 2):
            direction[i] = pair_add(residual[i], pair_mul(beta, direction[i]))
    weight = [s[0][0:1] for s in surface]

    def combine(side, r0, n):
        at = pl.ds(PAD + r0, n)
        total = weight[0] * v_ref[0, side, at]
        for i in range(1, 4):
            total = total + weight[i] * v_ref[i, side, at]
        return total

    chunks = [(0, HALO)] + blocks(HALO, HALO + ROWS, 32)
    for r0, n in chunks:
        s_ref[pl.ds(r0, n)] = combine(0, r0, n)
    for r0, n in chunks[1:]:
        s = s_ref[pl.ds(r0, n)]
        own = pl.ds(r0 - HALO, n)
        here = pl.ds(PAD + r0, n)
        west, _ = lane_left(s, combine(1, r0, n))
        d_west, _ = lane_left(d_ref[0, here], d_ref[1, here])
        d = d_ref[0, here]
        surface_ref[own] = s
        flow_ref[0, own] = jnp.minimum(d, d_ref[0, pl.ds(PAD + r0 - 1, n)]) * (s_ref[pl.ds(r0 - 1, n)] - s)
        flow_ref[1, own] = jnp.minimum(d, d_west) * (west - s)


VM = pl.BlockSpec(memory_space=pltpu.VMEM)
SM = pl.BlockSpec(memory_space=pltpu.SMEM)
ANY = pl.BlockSpec(memory_space=pl.ANY)


def params(**kwargs):
    return pltpu.CompilerParams(vmem_limit_bytes=VMEM_LIMIT, **kwargs)


def cost(flops, moved):
    return pl.CostEstimate(flops=flops, bytes_accessed=moved, transcendentals=0)


def ring(x, axis, step):
    count = lax.axis_size(axis)
    return lax.ppermute(x, axis, [(i, (i + step) % count) for i in range(count)])


def shape(*sizes, dtype=F32):
    return jax.ShapeDtypeStruct(sizes, dtype)


def scratch(*lead, rows=BUF, dtype=F32):
    return pltpu.VMEM(lead + (rows, LANES), dtype)


def shards(tracers, mixing, thickness, levels, land):
    devices = lax.axis_size("bx") * lax.axis_size("by")
    planes = 2 * KL
    wet = wet_levels(levels, land).astype(F32)
    flat = tracers.reshape(planes, ROWS, LANES)
    with jax.named_scope("rows"):
        to_up = jnp.concatenate([flat[:, :HALO], wet[None, :HALO]])
        to_down = jnp.concatenate([flat[:, -HALO:], wet[None, -HALO:]])
        top = ring(to_down, "bx", 1)
        bottom = ring(to_up, "bx", -1)
    with jax.named_scope("columns"):
        edges = (
            shape(planes, EXT, LANES),
            shape(EXT, LANES, dtype=I32),
            shape(2, TILES, EXT, LANES),
            shape(TILES, EXT, LANES),
            shape(TILES, EXT, LANES),
        )
        own = pl.pallas_call(
            own_edges_kernel,
            out_shape=edges,
            in_specs=[ANY, VM, VM],
            out_specs=(VM,) * 5,
            scratch_shapes=[pltpu.SemaphoreType.DMA((LOADS,))],
            compiler_params=params(),
            cost_estimate=cost(10_000_000, 7_000_000),
        )(flat, levels, land)
        ext, eff, edge, to_right, to_left = pl.pallas_call(
            halo_edges_kernel,
            out_shape=edges,
            in_specs=[VM] * 7,
            out_specs=(VM,) * 5,
            input_output_aliases={i + 2: i for i in range(5)},
            compiler_params=params(),
            cost_estimate=cost(1_000_000, 700_000),
        )(top, bottom, *own)
        from_left = ring(to_right, "by", 1)
        from_right = ring(to_left, "by", -1)
    with jax.named_scope("block"):
        new, fx, fy = pl.pallas_call(
            block_kernel,
            out_shape=(shape(planes, ROWS, LANES), shape(EXT, LANES), shape(EXT, LANES)),
            in_specs=[SM, SM, VM, VM],
            out_specs=(VM,) * 3,
            scratch_shapes=[
                scratch(dtype=I32),
                scratch(2, rows=EXT, dtype=I32),
                scratch(3, rows=EXT, dtype=I32),
                scratch(2),
                scratch(2),
                scratch(),
            ],
            compiler_params=params(),
            cost_estimate=cost(50_000_000, 12_000_000),
        )(mixing, thickness, ext, eff)
    with jax.named_scope("powers"):
        powers, depth, sums, new_edge = pl.pallas_call(
            solve_kernel,
            out_shape=(
                shape(5, 2, BUF, LANES),
                shape(2, BUF, LANES),
                shape(devices, LANES),
                shape(2, TILES, ROWS, LANES),
            ),
            in_specs=[SM, SM] + [VM] * 6,
            out_specs=(VM,) * 4,
            scratch_shapes=[
                scratch(2, dtype=I32),
                scratch(2, dtype=I32),
                scratch(2, dtype=I32),
                scratch(2, 2, rows=EXT),
                scratch(2, 2),
                scratch(2, 2),
                scratch(2, rows=EXT),
                scratch(2, TILES),
                scratch(2, rows=EXT, dtype=I32),
                scratch(2),
                scratch(2),
                scratch(2),
                scratch(2),
                scratch(9, 2, rows=EXT),
                scratch(2),
                scratch(2),
            ],
            compiler_params=params(),
            cost_estimate=cost(50_000_000, 6_000_000),
        )(mixing, thickness, fx, fy, from_left, from_right, edge, eff)
    with jax.named_scope("sums"):
        everyone = lax.all_to_all(sums, ("bx", "by"), 0, 0, tiled=True)
    with jax.named_scope("patch"):
        tracers_new = pl.pallas_call(
            patch_kernel,
            out_shape=shape(planes, ROWS, LANES),
            in_specs=[VM, VM],
            out_specs=VM,
            input_output_aliases={0: 0},
            compiler_params=params(),
            cost_estimate=cost(10_000_000, 12_000_000),
        )(new, new_edge)
    with jax.named_scope("surface"):
        surface, transports = pl.pallas_call(
            finish_kernel,
            out_shape=(shape(ROWS, LANES), shape(2, ROWS, LANES)),
            in_specs=[VM] * 3,
            out_specs=(VM, VM),
            scratch_shapes=[scratch(rows=HALO + ROWS)],
            compiler_params=params(),
            cost_estimate=cost(1_000_000, 3_000_000),
        )(everyone, powers, depth)
    return tracers_new.reshape(tracers.shape), surface, transports


def solution(mesh):
    in_specs = (P(None, None, "bx", "by"), P(), P(), P("bx", "by"), P("bx", "by"))
    out_specs = (P(None, None, "bx", "by"), P("bx", "by"), P(None, "bx", "by"))
    return jax.shard_map(shards, mesh=mesh, in_specs=in_specs, out_specs=out_specs, check_vma=False)
```

```python
import jax
import jax.numpy as jnp
from jax import lax
from jax.experimental import pallas as pl
from jax.experimental.pallas import tpu as pltpu
from jax.sharding import PartitionSpec as P

KL = 22
ROWS = 256
LANES = 128
HALO = 8
EXT = ROWS + 2 * HALO
PAD = 8
BUF = EXT + 2 * PAD
GROUP = 16
GROUPS = LANES // GROUP
TILES = 3
LOADS = 4
MOMENTS = 8
PATCH_LEVELS = 2
F32 = jnp.float32
I32 = jnp.int32
VMEM_LIMIT = 48 * 1024 * 1024


def lane_iota(rows):
    return lax.broadcasted_iota(I32, (rows, LANES), 1)


def first_half(rows):
    return (lane_iota(rows) & 8) == 0


def roll(x, shift):
    return pltpu.roll(x, shift % LANES, 1)


def blocks(start, stop, size):
    out = []
    while start < stop:
        out.append((start, min(size, stop - start)))
        start += size
    return out


CHUNKS = blocks(0, EXT, 32)
OWN_CHUNKS = blocks(HALO, HALO + ROWS, 32)


def wet_levels(levels, land):
    return jnp.where(land == 0, levels, 0)


def extend_eff(ref, base, top_ref, bottom_ref, wet_ref):
    ref[pl.ds(base, HALO)] = top_ref[2 * KL].astype(I32)
    ref[pl.ds(base + HALO, ROWS)] = wet_ref[...].astype(I32)
    ref[pl.ds(base + HALO + ROWS, HALO)] = bottom_ref[2 * KL].astype(I32)


def edge_slot(k):
    return k % TILES, k // TILES


def place(x, k, old):
    _, g = edge_slot(k)
    return jnp.where(lane_iota(x.shape[0]) // GROUP == g, roll(x, 8 + GROUP * g), old)


def to_neighbours(a, b):
    first = first_half(a.shape[0])
    return jnp.where(first, a, roll(b, 8)), jnp.where(first, roll(b, -8), a)


def own_edges_kernel(t_ref, wet_ref, edge_ref, right_ref, left_ref, own_ref, sems):
    parts = blocks(0, KL, -(-KL // LOADS))

    def copy(i):
        start, count = parts[i]
        planes = pl.ds(2 * start, 2 * count)
        return pltpu.make_async_copy(t_ref.at[planes], own_ref.at[planes], sems.at[i])

    for i in range(len(parts)):
        copy(i).start()
    size = 64
    tile_eff, _ = edge_slot(KL)

    def rows_of(step):
        own = pl.ds(pl.multiple_of(size * step, 8), size)
        return own, pl.ds(pl.multiple_of(HALO + size * step, 8), size)

    def clear(step, carry):
        own, at = rows_of(step)
        zero = jnp.zeros((size, LANES), F32)
        for c in range(2):
            for tile in range(TILES):
                edge_ref[c, tile, at] = zero
            edge_ref[c, tile_eff, at] = place(wet_ref[own], KL, zero)
        return carry

    lax.fori_loop(0, ROWS // size, clear, 0)
    for i, (start, count) in enumerate(parts):
        copy(i).wait()

        def rows(step, carry):
            own, at = rows_of(step)
            for k in range(start, start + count):
                tile, _ = edge_slot(k)
                for c in range(2):
                    edge_ref[c, tile, at] = place(own_ref[2 * k + c, own], k, edge_ref[c, tile, at])
            return carry

        lax.fori_loop(0, ROWS // size, rows, 0)

    def send(step, carry):
        _, at = rows_of(step)
        for tile in range(TILES):
            right_ref[tile, at], left_ref[tile, at] = to_neighbours(edge_ref[0, tile, at], edge_ref[1, tile, at])
        return carry

    lax.fori_loop(0, ROWS // size, send, 0)


def halo_edges_kernel(top_ref, bottom_ref, edge_in, right_in, left_in, edge_ref, right_ref, left_ref):
    for r0, ref in ((0, top_ref), (HALO + ROWS, bottom_ref)):
        at = pl.ds(r0, HALO)
        held = [[jnp.zeros((HALO, LANES), F32) for _ in range(TILES)] for _ in range(2)]
        for k in range(KL + 1):
            tile, _ = edge_slot(k)
            for c in range(2):
                x = ref[2 * k + c] if k < KL else ref[2 * KL]
                held[c][tile] = place(x, k, held[c][tile])
        for tile in range(TILES):
            for c in range(2):
                edge_ref[c, tile, at] = held[c][tile]
            right_ref[tile, at], left_ref[tile, at] = to_neighbours(held[0][tile], held[1][tile])


def count_word(effs, word):
    total = None
    for eff in effs:
        bits = jnp.clip(eff - 10 * word, 0, 10) * 3
        mask = (lax.shift_left(jnp.full_like(bits, 1), bits) - 1) & 0o1111111111
        total = mask if total is None else total + mask
    return total


def neighbours(ref, r0, n):
    x = ref[pl.ds(PAD + r0, n)]
    around = ref[pl.ds(PAD + r0 - 1, n)] + ref[pl.ds(PAD + r0 + 1, n)]
    return x, around + (roll(x, 1) + roll(x, -1))


def block_kernel(
    mixing_ref,
    thick_ref,
    t_ref,
    top_ref,
    bottom_ref,
    wet_ref,
    new_ref,
    fx_ref,
    fy_ref,
    ext_ref,
    eff_ref,
    min_ref,
    word_ref,
    u_ref,
    l_ref,
    acc_ref,
    in_sems,
    out_sems,
):
    def held(k):
        return ext_ref.at[pl.ds(2 * k, 2), pl.ds(HALO, ROWS)]

    def load(k):
        return pltpu.make_async_copy(t_ref.at[pl.ds(2 * k, 2)], held(k), in_sems.at[k])

    def store(k):
        return pltpu.make_async_copy(held(k), new_ref.at[pl.ds(2 * k, 2)], out_sems.at[k])

    def each(body):
        def step(k, carry):
            body(k)
            return carry

        lax.fori_loop(0, KL, step, 0)

    each(lambda k: load(k).start())
    eff_ref[...] = jnp.zeros(eff_ref.shape, I32)
    extend_eff(eff_ref, PAD, top_ref, bottom_ref, wet_ref)
    ext_ref[:, pl.ds(0, HALO)] = top_ref[pl.ds(0, 2 * KL)]
    ext_ref[:, pl.ds(HALO + ROWS, HALO)] = bottom_ref[pl.ds(0, 2 * KL)]
    for ref in (u_ref, l_ref, acc_ref, fx_ref, fy_ref):
        ref[...] = jnp.zeros(ref.shape, F32)
    for r0, n in CHUNKS:
        e = eff_ref[pl.ds(PAD + r0, n)]
        min_ref[0, pl.ds(r0, n)] = jnp.minimum(e, eff_ref[pl.ds(PAD + r0 - 1, n)])
        min_ref[1, pl.ds(r0, n)] = jnp.minimum(e, roll(e, 1))
        effs = (eff_ref[pl.ds(PAD + r0 - 1, n)], eff_ref[pl.ds(PAD + r0 + 1, n)], roll(e, 1), roll(e, -1))
        for word in range(3):
            word_ref[word, pl.ds(r0, n)] = count_word(effs, word)

    def count(k, r0, n):
        words = word_ref[k // 10, pl.ds(r0, n)]
        shift = jnp.full((n, LANES), 3 * (k % 10), I32)
        return (lax.shift_right_logical(words, shift) & 7).astype(F32)

    def stage(step, late):
        k = jnp.clip(step - late, 0, KL - 1)
        valid = jnp.logical_and(step >= late, step < KL + late)
        return k, jnp.where(valid, thick_ref[k], 0.0)

    def body(step, carry):
        @pl.when(step < KL)
        def _():
            load(step).wait()

        @pl.when(step >= 4)
        def _():
            store(step - 4).start()

        ku, _ = stage(step, 0)
        kl, _ = stage(step, 1)
        kd, thick_d = stage(step, 2)
        kf, thick_f = stage(step, 3)
        mix = [jnp.where(step < KL + 2, mixing_ref[kd, c], 0.0) for c in range(2)]

        def flux(r0, n):
            here = acc_ref[pl.ds(PAD + r0, n)]
            up = acc_ref[pl.ds(PAD + r0 - 1, n)]
            face_x = min_ref[0, pl.ds(r0, n)] > kf
            face_y = min_ref[1, pl.ds(r0, n)] > kf
            fx_ref[pl.ds(r0, n)] += thick_f * jnp.where(face_x, here - up, 0.0)
            fy_ref[pl.ds(r0, n)] += thick_f * jnp.where(face_y, here - roll(here, 1), 0.0)

        def density(r0, n):
            wet = eff_ref[pl.ds(PAD + r0, n)] > kd
            number = count(kd, r0, n)
            new = []
            for c in range(2):
                x, around = neighbours(l_ref.at[c], r0, n)
                second = jnp.where(wet, around, 0.0) - number * x
                value = ext_ref[2 * kd + c, pl.ds(r0, n)] - mix[c] * second
                low, high = max(r0, HALO), min(r0 + n, HALO + ROWS)
                ext_ref[2 * kd + c, pl.ds(low, high - low)] = value[low - r0 : high - r0]
                new.append(value)
            plain = 0.8 * new[1] - 0.2 * new[0]
            acc_ref[pl.ds(PAD + r0, n)] += thick_d * jnp.where(wet, plain, 0.0)

        def first(r0, n):
            wet = eff_ref[pl.ds(PAD + r0, n)] > kl
            number = count(kl, r0, n)
            for c in range(2):
                x, around = neighbours(u_ref.at[c], r0, n)
                l_ref[c, pl.ds(PAD + r0, n)] = jnp.where(wet, around, 0.0) - number * x

        def masked(r0, n):
            wet = eff_ref[pl.ds(PAD + r0, n)] > ku
            for c in range(2):
                u_ref[c, pl.ds(PAD + r0, n)] = jnp.where(wet, ext_ref[2 * ku + c, pl.ds(r0, n)], 0.0)

        work = (flux, density, first, masked)
        for turn in range(len(CHUNKS) + len(work) - 1):
            for late, part in enumerate(work):
                if 0 <= turn - late < len(CHUNKS):
                    part(*CHUNKS[turn - late])
        return carry

    lax.fori_loop(0, KL + 3, body, 0)
    store(KL - 1).start()
    each(lambda k: store(k).wait())


def patch_kernel(new_in, edge_ref, new_ref):
    for part in range(PATCH_LEVELS):
        k = pl.program_id(0) * PATCH_LEVELS + part
        tile = k % TILES
        back = (2 * LANES - 8 - GROUP * (k // TILES)) % LANES
        for r0, n in blocks(0, ROWS, 64):
            lane = lane_iota(n)
            middle = jnp.logical_and(lane >= 4, lane < LANES - 4)
            own = pl.ds(r0, n)
            for c in range(2):
                edge = pltpu.roll(edge_ref[c, tile, own], back, 1)
                new_ref[2 * part + c, own] = jnp.where(middle, new_in[2 * part + c, own], edge)


def two_sum(a, b):
    s = a + b
    v = s - a
    return s, (a - (s - v)) + (b - v)


def quick_sum(a, b):
    s = a + b
    return s, b - (s - a)


def split(a):
    t = a * 4097.0
    high = t - (t - a)
    return high, a - high


def two_prod(a, b, parts_a, parts_b):
    p = a * b
    ah, al = parts_a
    bh, bl = parts_b
    return p, ((ah * bh - p) + ah * bl + al * bh) + al * bl


def pair_add(x, y):
    s, e = two_sum(x[0], y[0])
    return quick_sum(s, e + (x[1] + y[1]))


def pair_mul(x, y):
    p, e = two_prod(x[0], y[0], split(x[0]), split(y[0]))
    return quick_sum(p, e + (x[0] * y[1] + x[1] * y[0]))


def pair_neg(x):
    return -x[0], -x[1]


def pair_div(x, y):
    q = x[0] / y[0]
    rest = pair_add(x, pair_neg(pair_mul(y, (q, jnp.zeros_like(q)))))
    return quick_sum(q, rest[0] / y[0])


def pair_clip(x, top):
    inside = jnp.logical_and(x[0] >= 0.0, x[0] <= top)
    high = jnp.where(inside, x[0], jnp.where(x[0] > top, top, 0.0))
    return high, jnp.where(inside, x[1], 0.0)


def group_totals(x):
    x = x + roll(x, GROUP)
    x = x + roll(x, 2 * GROUP)
    return x + roll(x, 4 * GROUP)


def lane_left(main, side):
    lane = lane_iota(main.shape[0])
    a, b = roll(main, 1), roll(side, 1)
    return jnp.where(lane == 0, b, a), jnp.where(lane == 0, a, b)


def lane_right(main, side):
    lane = lane_iota(main.shape[0])
    a, b = roll(main, -1), roll(side, -1)
    return jnp.where(lane == LANES - 1, b, a), jnp.where(lane == LANES - 1, a, b)


SIDES = (0, 1)


def solve_kernel(
    mixing_ref,
    thick_ref,
    fx_ref,
    fy_ref,
    from_left_ref,
    from_right_ref,
    edge_ref,
    top_ref,
    bottom_ref,
    wet_ref,
    v_ref,
    d_ref,
    sums_ref,
    new_ref,
    e_ref,
    west_ref,
    east_ref,
    f_ref,
    u_ref,
    l_ref,
    n_ref,
    acc_ref,
    eff_ref,
    full_fx_ref,
    full_fy_ref,
    dl_ref,
    dr_ref,
    w_ref,
    p_ref,
    q_ref,
):
    by = lax.axis_index("by")
    open_side = (by != 0, by != lax.axis_size("by") - 1)

    def clear(ref):
        ref[...] = jnp.zeros(ref.shape, ref.dtype)

    for ref in (e_ref, west_ref, east_ref):
        clear(ref)
    for ref in (u_ref, l_ref, acc_ref, d_ref, v_ref, dl_ref, dr_ref, p_ref, q_ref, full_fx_ref, full_fy_ref):
        rank = len(ref.shape) - 2
        lead = [()]
        for size in ref.shape[:rank]:
            lead = [i + (j,) for i in lead for j in range(size)]
        for i in lead:
            for r0 in (0, BUF - PAD):
                ref[i + (pl.ds(r0, PAD),)] = jnp.zeros((PAD, LANES), F32)

    def field(side, c, tile, r0, n):
        own = edge_ref[c, tile, pl.ds(r0, n)]
        first = first_half(n)
        if side == 0:
            far = from_left_ref[tile, pl.ds(r0, n)]
            return jnp.where(first, roll(far, -8) if c else far, own)
        far = from_right_ref[tile, pl.ds(r0, n)]
        return jnp.where(first, own, roll(far, 8) if c else far)

    tile_eff, slot = edge_slot(KL)
    for side in SIDES:
        for r0, n in CHUNKS:
            lane = lane_iota(n)
            x = field(side, 0, tile_eff, r0, n)
            inner = (lane & 8) == (8 if side == 0 else 0)
            keep = jnp.logical_and(lane // GROUP == slot, jnp.logical_or(inner, open_side[side]))
            e = group_totals(jnp.where(keep, x, 0.0)).astype(I32)
            at = pl.ds(PAD + r0, n)
            e_ref[side, at] = e
            west_ref[side, at] = roll(e, 1)
            east_ref[side, at] = roll(e, -1)

    group8 = lane_iota(8) // GROUP

    def by_group(tile, values):
        out = jnp.zeros((8, LANES), F32)
        for g in range(GROUPS):
            k = TILES * g + tile
            value = values(jnp.minimum(k, KL - 1))
            out = jnp.where(group8 == g, jnp.where(k < KL, value, 0.0), out)
        return out[0:1]

    def level_lanes(tile):
        return (group8 * TILES + tile)[0:1]

    def tile_step(tile, carry):
        level_of = level_lanes(tile)
        mix = [by_group(tile, lambda k, c=c: mixing_ref[k, c]) for c in range(2)]
        thick = by_group(tile, lambda k: thick_ref[k])

        def masked(side, r0, n):
            at = pl.ds(PAD + r0, n)
            wet = e_ref[side, at] > level_of
            for c in range(2):
                x = field(side, c, tile, r0, n)
                f_ref[side, c, pl.ds(r0, n)] = x
                u_ref[side, c, at] = jnp.where(wet, x, 0.0)

        def first(side, r0, n):
            at = pl.ds(PAD + r0, n)
            wet = e_ref[side, at] > level_of
            number = jnp.where(e_ref[side, pl.ds(PAD + r0 - 1, n)] > level_of, 1.0, 0.0)
            number += jnp.where(e_ref[side, pl.ds(PAD + r0 + 1, n)] > level_of, 1.0, 0.0)
            number += jnp.where(west_ref[side, at] > level_of, 1.0, 0.0)
            number += jnp.where(east_ref[side, at] > level_of, 1.0, 0.0)
            n_ref[side, pl.ds(r0, n)] = number
            for c in range(2):
                x, around = neighbours(u_ref.at[side, c], r0, n)
                l_ref[side, c, at] = jnp.where(wet, around, 0.0) - number * x

        def density(side, r0, n):
            at = pl.ds(PAD + r0, n)
            wet = e_ref[side, at] > level_of
            number = n_ref[side, pl.ds(r0, n)]
            new = []
            for c in range(2):
                x, around = neighbours(l_ref.at[side, c], r0, n)
                second = jnp.where(wet, around, 0.0) - number * x
                new.append(f_ref[side, c, pl.ds(r0, n)] - mix[c] * second)
            acc_ref[side, tile, at] = thick * jnp.where(wet, 0.8 * new[1] - 0.2 * new[0], 0.0)
            low, high = max(r0, HALO), min(r0 + n, HALO + ROWS)
            own = pl.ds(low - HALO, high - low)
            for c in range(2):
                value = new[c][low - r0 : high - r0]
                if side == 1:
                    value = jnp.where(first_half(high - low), value, new_ref[c, tile, own])
                new_ref[c, tile, own] = value

        for part in (masked, first, density):
            for side in SIDES:
                for r0, n in CHUNKS:
                    part(side, r0, n)
        return carry

    lax.fori_loop(0, TILES, tile_step, 0)

    for side in SIDES:
        for r0, n in CHUNKS:
            lane = lane_iota(n)
            at = pl.ds(PAD + r0, n)
            layers = [acc_ref[side, tile, at] for tile in range(TILES)]
            run = (layers[0] + layers[1]) + layers[2]
            run = jnp.where(lane >= GROUP, roll(run, GROUP), 0.0)
            for step in (1, 2, 4):
                run = run + jnp.where(lane >= step * GROUP, roll(run, step * GROUP), 0.0)
            for tile in range(TILES):
                run = run + layers[tile]
                acc_ref[side, tile, at] = run
    thick = [by_group(tile, lambda k: thick_ref[k]) for tile in range(TILES)]
    extend_eff(eff_ref.at[0], 0, top_ref, bottom_ref, wet_ref)
    table = jnp.zeros((8, LANES), F32)
    for k in range(KL):
        table += jnp.where(lane_iota(8) > k, thick_ref[k], 0.0)
    for r0, n in blocks(0, EXT, EXT // 2):
        lane = lane_iota(n)
        own = pl.ds(r0, n)
        at = pl.ds(PAD + r0, n)
        faces = []
        for side in SIDES:
            e = e_ref[side, at]
            min_x = jnp.minimum(e, e_ref[side, pl.ds(PAD + r0 - 1, n)])
            min_y = jnp.minimum(e, west_ref[side, at])
            face_x = jnp.zeros((n, LANES), F32)
            face_y = face_x
            for tile in range(TILES):
                here = acc_ref[side, tile, at]
                up = acc_ref[side, tile, pl.ds(PAD + r0 - 1, n)]
                level_of = level_lanes(tile)
                face_x += thick[tile] * jnp.where(min_x > level_of, here - up, 0.0)
                face_y += thick[tile] * jnp.where(min_y > level_of, here - roll(here, 1), 0.0)
            faces += [face_x, face_y]
        for shift in (GROUP, 2 * GROUP, 4 * GROUP):
            faces = [x + roll(x, shift) for x in faces]
        faces = [roll(x, 8) for x in faces]
        for full, main, west, east in (
            (full_fx_ref, fx_ref, faces[0], faces[2]),
            (full_fy_ref, fy_ref, faces[1], faces[3]),
        ):
            full[0, at] = jnp.where(lane < 4, west, jnp.where(lane >= LANES - 4, east, main[own]))
            full[1, at] = jnp.where(lane < 8, east, jnp.where(lane >= LANES - 8, west, 0.0))
        west = roll(e_ref[0, at], 8)
        east = roll(e_ref[1, at], 8)
        eff_ref[1, own] = jnp.where(lane < 8, east, jnp.where(lane >= LANES - 8, west, 0))
    for t in range(2):
        for r0, n in blocks(0, EXT, 8):
            d_ref[t, pl.ds(PAD + r0, n)] = jnp.take_along_axis(table, eff_ref[t, pl.ds(r0, n)], axis=1)
    for r0, n in CHUNKS:
        here = pl.ds(PAD + r0, n)
        d_main, d_side = d_ref[0, here], d_ref[1, here]
        dl_ref[0, here], dl_ref[1, here] = lane_left(d_main, d_side)
        dr_ref[0, here], dr_ref[1, here] = lane_right(d_main, d_side)

    for r0, n in CHUNKS:
        here = pl.ds(PAD + r0, n)
        east = lane_right(full_fy_ref[0, here], full_fy_ref[1, here])
        for t in range(2):
            fx = full_fx_ref[t, here] - full_fx_ref[t, pl.ds(PAD + r0 + 1, n)]
            fy = full_fy_ref[t, here] - east[t]
            v_ref[0, t, here] = 10.0 * (fx + fy)

    def weights(t, carry):
        for r0, n in CHUNKS:
            here = pl.ds(PAD + r0, n)
            above = pl.ds(PAD + r0 - 1, n)
            below = pl.ds(PAD + r0 + 1, n)
            d = d_ref[t, here]
            left, right = dl_ref[t, here], dr_ref[t, here]
            up, down = d_ref[t, above], d_ref[t, below]
            w_west, w_east = jnp.minimum(d, left), jnp.minimum(d, right)
            w_up, w_down = jnp.minimum(d, up), jnp.minimum(d, down)
            corners = (
                jnp.minimum(d, dl_ref[t, above])
                + jnp.minimum(d, dr_ref[t, below])
                + jnp.minimum(d, dr_ref[t, above])
                + jnp.minimum(d, dl_ref[t, below])
            )
            at = pl.ds(r0, n)
            w_ref[0, t, at] = 0.05 + w_up + w_down + w_west + w_east + 0.25 * corners
            w_ref[1, t, at] = w_west
            w_ref[2, t, at] = w_east
            w_ref[3, t, at] = w_down
            w_ref[4, t, at] = 0.25 * jnp.minimum(down, left)
            w_ref[5, t, at] = 0.25 * jnp.minimum(down, right)
            w_ref[6, t, at] = w_up
            w_ref[7, t, at] = 0.25 * jnp.minimum(up, left)
            w_ref[8, t, at] = 0.25 * jnp.minimum(up, right)
        return carry

    lax.fori_loop(0, 2, weights, 0)

    def power(step, carry):
        for r0, n in CHUNKS:
            here = pl.ds(PAD + r0, n)
            at = pl.ds(r0, n)
            v = (v_ref[step, 0, here], v_ref[step, 1, here])
            left = lane_left(*v)
            right = lane_right(*v)
            for t in range(2):
                w = [w_ref[m, t, at] for m in range(9)]
                p_ref[t, here] = w[3] * v[t] + w[4] * left[t] + w[5] * right[t]
                q_ref[t, here] = w[6] * v[t] + w[7] * left[t] + w[8] * right[t]
                v_ref[step + 1, t, here] = w[0] * v[t] - (w[1] * left[t] + w[2] * right[t])
        for r0, n in CHUNKS:
            here = pl.ds(PAD + r0, n)
            for t in range(2):
                beside = p_ref[t, pl.ds(PAD + r0 - 1, n)] + q_ref[t, pl.ds(PAD + r0 + 1, n)]
                v_ref[step + 1, t, here] -= beside
        return carry

    lax.fori_loop(0, 4, power, 0)

    def dots(step, carry):
        at = pl.ds(pl.multiple_of(PAD + HALO + 8 * step, 8), 8)
        v = [v_ref[i, 0, at] for i in range(5)]
        parts = [split(x) for x in v]
        out = []
        for m in range(MOMENTS):
            i, j = m // 2, (m + 1) // 2
            p, e = two_prod(v[i], v[j], parts[i], parts[j])
            s, f = two_sum(carry[2 * m], p)
            out += [s, carry[2 * m + 1] + (e + f)]
        return tuple(out)

    zero = jnp.zeros((8, LANES), F32)
    sums = lax.fori_loop(0, ROWS // 8, dots, (zero,) * (2 * MOMENTS), unroll=4)
    sub = lax.broadcasted_iota(I32, (8, LANES), 0)
    pairs = [(sums[2 * m], sums[2 * m + 1]) for m in range(MOMENTS)]
    for half in (4, 2, 1):
        merged = []
        for m in range(half):
            a, b = pairs[m], pairs[m + half]
            upper = (sub & half) == 0
            keep = tuple(jnp.where(upper, x, y) for x, y in zip(a, b))
            other = tuple(jnp.where(upper, pltpu.roll(x, 8 - half, 0), pltpu.roll(y, half, 0)) for x, y in zip(a, b))
            merged.append(pair_add(keep, other))
        pairs = merged
    wide = [jnp.concatenate([x, jnp.zeros((LANES - 8, LANES), F32)]).T for x in pairs[0]]
    rows = [tuple(x[at : at + 8] for x in wide) for at in range(0, LANES, 8)]
    while len(rows) > 1:
        rows = [pair_add(rows[i], rows[i + 1]) for i in range(0, len(rows), 2)]
    total = rows[0]
    for shift in (4, 2, 1):
        total = pair_add(total, tuple(pltpu.roll(x, shift, 0) for x in total))
    row = total[0] + roll(total[1], MOMENTS)
    for at in range(0, sums_ref.shape[0], 8):
        sums_ref[pl.ds(at, 8)] = row


def finish_kernel(all_ref, v_ref, d_ref, surface_ref, flow_ref, s_ref):
    zero = jnp.zeros((8, LANES), F32)
    high, low = zero, zero
    for at in range(0, all_ref.shape[0], 8):
        high, e = two_sum(high, all_ref[pl.ds(at, 8)])
        low = low + e
    total = (high, low)
    for shift in (4, 2, 1):
        total = pair_add(total, tuple(pltpu.roll(x, shift, 0) for x in total))
    total = pair_add(total, tuple(roll(x, -MOMENTS) for x in total))
    lane = lane_iota(8)

    def moment(m):
        return tuple(
            jnp.broadcast_to(jnp.sum(jnp.where(lane == m, x, 0.0), axis=1, keepdims=True), (8, LANES))
            for x in total
        )

    rho = [moment(m) for m in range(MOMENTS)]
    pi = list(rho)
    nought = (zero, zero)
    one = (zero + 1.0, zero)
    surface = [nought] * 4
    residual = [one] + [nought] * 3
    direction = list(residual)
    for step in range(4):
        alpha = pair_clip(pair_div(rho[step], pi[step + 1]), 20.0)
        for i in range(step + 1):
            surface[i] = pair_add(surface[i], pair_mul(alpha, direction[i]))
        if step == 3:
            break
        minus = pair_neg(alpha)
        new_rho = list(rho)
        for m in range(step + 1, MOMENTS - 1 - step):
            new_rho[m] = pair_add(rho[m], pair_mul(minus, pi[m + 1]))
        beta = pair_clip(pair_div(pair_mul(minus, new_rho[step + 1]), rho[step]), 400.0)
        for m in range(step + 2, MOMENTS - 1 - step):
            pi[m] = pair_add(new_rho[m], pair_mul(beta, pi[m]))
        rho = new_rho
        for i in range(step + 1, 0, -1):
            residual[i] = pair_add(residual[i], pair_mul(minus, direction[i - 1]))
        for i in range(step + 2):
            direction[i] = pair_add(residual[i], pair_mul(beta, direction[i]))
    weight = [s[0][0:1] for s in surface]

    def combine(side, r0, n):
        at = pl.ds(PAD + r0, n)
        total = weight[0] * v_ref[0, side, at]
        for i in range(1, 4):
            total = total + weight[i] * v_ref[i, side, at]
        return total

    chunks = [(0, HALO)] + blocks(HALO, HALO + ROWS, 32)
    for r0, n in chunks:
        s_ref[pl.ds(r0, n)] = combine(0, r0, n)
    for r0, n in chunks[1:]:
        s = s_ref[pl.ds(r0, n)]
        own = pl.ds(r0 - HALO, n)
        here = pl.ds(PAD + r0, n)
        west, _ = lane_left(s, combine(1, r0, n))
        d_west, _ = lane_left(d_ref[0, here], d_ref[1, here])
        d = d_ref[0, here]
        surface_ref[own] = s
        flow_ref[0, own] = jnp.minimum(d, d_ref[0, pl.ds(PAD + r0 - 1, n)]) * (s_ref[pl.ds(r0 - 1, n)] - s)
        flow_ref[1, own] = jnp.minimum(d, d_west) * (west - s)


VM = pl.BlockSpec(memory_space=pltpu.VMEM)
SM = pl.BlockSpec(memory_space=pltpu.SMEM)
HBM = pl.BlockSpec(memory_space=pltpu.HBM)


def params(**kwargs):
    return pltpu.CompilerParams(vmem_limit_bytes=VMEM_LIMIT, **kwargs)


def cost(flops, moved):
    return pl.CostEstimate(flops=flops, bytes_accessed=moved, transcendentals=0)


def ring(x, axis, step):
    count = lax.axis_size(axis)
    return lax.ppermute(x, axis, [(i, (i + step) % count) for i in range(count)])


def shape(*sizes, dtype=F32):
    return jax.ShapeDtypeStruct(sizes, dtype)


def scratch(*lead, rows=BUF, dtype=F32):
    return pltpu.VMEM(lead + (rows, LANES), dtype)


def shards(tracers, mixing, thickness, levels, land):
    devices = lax.axis_size("bx") * lax.axis_size("by")
    planes = 2 * KL
    wet = wet_levels(levels, land).astype(F32)
    flat = tracers.reshape(planes, ROWS, LANES)
    with jax.named_scope("rows"):
        to_up = jnp.concatenate([flat[:, :HALO], wet[None, :HALO]])
        to_down = jnp.concatenate([flat[:, -HALO:], wet[None, -HALO:]])
        top = ring(to_down, "bx", 1)
        bottom = ring(to_up, "bx", -1)
    with jax.named_scope("columns"):
        edges = (shape(2, TILES, EXT, LANES), shape(TILES, EXT, LANES), shape(TILES, EXT, LANES))
        own = pl.pallas_call(
            own_edges_kernel,
            out_shape=edges,
            in_specs=[HBM, VM],
            out_specs=(VM,) * 3,
            scratch_shapes=[scratch(planes, rows=ROWS), pltpu.SemaphoreType.DMA((LOADS,))],
            compiler_params=params(),
            cost_estimate=cost(10_000_000, 7_000_000),
        )(flat, wet)
        edge, to_right, to_left = pl.pallas_call(
            halo_edges_kernel,
            out_shape=edges,
            in_specs=[VM] * 5,
            out_specs=(VM,) * 3,
            input_output_aliases={i + 2: i for i in range(3)},
            compiler_params=params(),
            cost_estimate=cost(1_000_000, 700_000),
        )(top, bottom, *own)
        from_left = ring(to_right, "by", 1)
        from_right = ring(to_left, "by", -1)
    with jax.named_scope("block"):
        new, fx, fy = pl.pallas_call(
            block_kernel,
            out_shape=(shape(planes, ROWS, LANES), shape(EXT, LANES), shape(EXT, LANES)),
            in_specs=[SM, SM, HBM, VM, VM, VM],
            out_specs=(HBM, VM, VM),
            scratch_shapes=[
                scratch(planes, rows=EXT),
                scratch(dtype=I32),
                scratch(2, rows=EXT, dtype=I32),
                scratch(3, rows=EXT, dtype=I32),
                scratch(2),
                scratch(2),
                scratch(),
                pltpu.SemaphoreType.DMA((KL,)),
                pltpu.SemaphoreType.DMA((KL,)),
            ],
            compiler_params=params(),
            cost_estimate=cost(50_000_000, 12_000_000),
        )(mixing, thickness, flat, top, bottom, wet)
    with jax.named_scope("powers"):
        powers, depth, sums, new_edge = pl.pallas_call(
            solve_kernel,
            out_shape=(
                shape(5, 2, BUF, LANES),
                shape(2, BUF, LANES),
                shape(devices, LANES),
                shape(2, TILES, ROWS, LANES),
            ),
            in_specs=[SM, SM] + [VM] * 8,
            out_specs=(VM,) * 4,
            scratch_shapes=[
                scratch(2, dtype=I32),
                scratch(2, dtype=I32),
                scratch(2, dtype=I32),
                scratch(2, 2, rows=EXT),
                scratch(2, 2),
                scratch(2, 2),
                scratch(2, rows=EXT),
                scratch(2, TILES),
                scratch(2, rows=EXT, dtype=I32),
                scratch(2),
                scratch(2),
                scratch(2),
                scratch(2),
                scratch(9, 2, rows=EXT),
                scratch(2),
                scratch(2),
            ],
            compiler_params=params(),
            cost_estimate=cost(50_000_000, 6_000_000),
        )(mixing, thickness, fx, fy, from_left, from_right, edge, top, bottom, wet)
    with jax.named_scope("sums"):
        everyone = lax.all_to_all(sums, ("bx", "by"), 0, 0, tiled=True)
    with jax.named_scope("patch"):
        level_block = pl.BlockSpec((2 * PATCH_LEVELS, ROWS, LANES), lambda i: (i, 0, 0))
        tracers_new = pl.pallas_call(
            patch_kernel,
            grid=(KL // PATCH_LEVELS,),
            out_shape=shape(planes, ROWS, LANES),
            in_specs=[level_block, VM],
            out_specs=level_block,
            input_output_aliases={0: 0},
            compiler_params=params(),
            cost_estimate=cost(10_000_000, 12_000_000),
        )(new, new_edge)
    with jax.named_scope("surface"):
        surface, transports = pl.pallas_call(
            finish_kernel,
            out_shape=(shape(ROWS, LANES), shape(2, ROWS, LANES)),
            in_specs=[VM] * 3,
            out_specs=(VM, VM),
            scratch_shapes=[scratch(rows=HALO + ROWS)],
            compiler_params=params(),
            cost_estimate=cost(1_000_000, 3_000_000),
        )(everyone, powers, depth)
    return tracers_new.reshape(tracers.shape), surface, transports


def solution(mesh):
    in_specs = (P(None, None, "bx", "by"), P(), P(), P("bx", "by"), P("bx", "by"))
    out_specs = (P(None, None, "bx", "by"), P("bx", "by"), P(None, "bx", "by"))
    return jax.shard_map(shards, mesh=mesh, in_specs=in_specs, out_specs=out_specs, check_vma=False)
```

```python
import jax
import jax.numpy as jnp
from jax import lax
from jax.experimental import pallas as pl
from jax.experimental.pallas import tpu as pltpu
from jax.sharding import PartitionSpec as P

KL = 22
ROWS = 256
LANES = 128
HALO = 8
EXT = ROWS + 2 * HALO
PAD = 8
BUF = EXT + 2 * PAD
GROUP = 16
GROUPS = LANES // GROUP
TILES = 3
LOADS = 4
MOMENTS = 8
PATCH = 2
GRAVITY = 10.0
SEEN = HALO + ROWS
F32 = jnp.float32
I32 = jnp.int32
MIB = 1024 * 1024


def lane_iota(rows):
    return lax.broadcasted_iota(I32, (rows, LANES), 1)


def first_half(rows):
    return (lane_iota(rows) & 8) == 0


def roll(x, shift):
    return pltpu.roll(x, shift % LANES, 1)


def blocks(start, stop, size):
    out = []
    while start < stop:
        out.append((start, min(size, stop - start)))
        start += size
    return out


CHUNKS = blocks(0, EXT, 32)
OWN_CHUNKS = blocks(HALO, HALO + ROWS, 32)


def wet_levels(levels, land):
    return jnp.where(land == 0, levels, 0)


def extend_eff(ref, base, top_ref, bottom_ref, wet_ref):
    ref[pl.ds(base, HALO)] = top_ref[2 * KL].astype(I32)
    ref[pl.ds(base + HALO, ROWS)] = wet_ref[...].astype(I32)
    ref[pl.ds(base + HALO + ROWS, HALO)] = bottom_ref[2 * KL].astype(I32)


def edge_slot(k):
    return k % TILES, k // TILES


def place(x, k, old):
    _, g = edge_slot(k)
    return jnp.where(lane_iota(x.shape[0]) // GROUP == g, roll(x, 8 + GROUP * g), old)


def to_neighbours(a, b):
    first = first_half(a.shape[0])
    return jnp.where(first, a, roll(b, 8)), jnp.where(first, roll(b, -8), a)


def own_edges_kernel(t_ref, wet_ref, edge_ref, right_ref, left_ref, own_ref, sems):
    parts = blocks(0, KL, -(-KL // LOADS))

    def copy(i):
        start, count = parts[i]
        planes = pl.ds(2 * start, 2 * count)
        return pltpu.make_async_copy(t_ref.at[planes], own_ref.at[planes], sems.at[i])

    for i in range(len(parts)):
        copy(i).start()
    size = 128
    tile_eff, _ = edge_slot(KL)

    def rows_of(step):
        own = pl.ds(pl.multiple_of(size * step, 8), size)
        return own, pl.ds(pl.multiple_of(HALO + size * step, 8), size)

    def clear(step, carry):
        own, at = rows_of(step)
        zero = jnp.zeros((size, LANES), F32)
        for c in range(2):
            for tile in range(TILES):
                edge_ref[c, tile, at] = zero
            edge_ref[c, tile_eff, at] = place(wet_ref[own], KL, zero)
        return carry

    lax.fori_loop(0, ROWS // size, clear, 0)
    for i, (start, count) in enumerate(parts):
        copy(i).wait()

        def rows(step, carry):
            own, at = rows_of(step)
            for k in range(start, start + count):
                tile, _ = edge_slot(k)
                for c in range(2):
                    edge_ref[c, tile, at] = place(own_ref[2 * k + c, own], k, edge_ref[c, tile, at])
            return carry

        lax.fori_loop(0, ROWS // size, rows, 0)

    def send(step, carry):
        _, at = rows_of(step)
        for tile in range(TILES):
            right_ref[tile, at], left_ref[tile, at] = to_neighbours(edge_ref[0, tile, at], edge_ref[1, tile, at])
        return carry

    lax.fori_loop(0, ROWS // size, send, 0)


def halo_edges_kernel(top_ref, bottom_ref, edge_in, right_in, left_in, edge_ref, right_ref, left_ref):
    for r0, ref in ((0, top_ref), (HALO + ROWS, bottom_ref)):
        at = pl.ds(r0, HALO)
        held = [[jnp.zeros((HALO, LANES), F32) for _ in range(TILES)] for _ in range(2)]
        for k in range(KL + 1):
            tile, _ = edge_slot(k)
            for c in range(2):
                x = ref[2 * k + c] if k < KL else ref[2 * KL]
                held[c][tile] = place(x, k, held[c][tile])
        for tile in range(TILES):
            for c in range(2):
                edge_ref[c, tile, at] = held[c][tile]
            right_ref[tile, at], left_ref[tile, at] = to_neighbours(held[0][tile], held[1][tile])


def count_word(effs, word):
    total = None
    for eff in effs:
        bits = jnp.clip(eff - 10 * word, 0, 10) * 3
        mask = (lax.shift_left(jnp.full_like(bits, 1), bits) - 1) & 0o1111111111
        total = mask if total is None else total + mask
    return total


def neighbours(ref, r0, n):
    x = ref[pl.ds(PAD + r0, n)]
    around = ref[pl.ds(PAD + r0 - 1, n)] + ref[pl.ds(PAD + r0 + 1, n)]
    return x, around + (roll(x, 1) + roll(x, -1))


def block_kernel(
    mixing_ref,
    thick_ref,
    t_ref,
    top_ref,
    bottom_ref,
    wet_ref,
    new_ref,
    source_ref,
    wet_ext_ref,
    ext_ref,
    eff_ref,
    min_ref,
    word_ref,
    u_ref,
    l_ref,
    acc_ref,
    fx_ref,
    fy_ref,
    in_sems,
    out_sems,
):
    def held(k):
        return ext_ref.at[pl.ds(2 * k, 2), pl.ds(HALO, ROWS)]

    def load(k):
        return pltpu.make_async_copy(t_ref.at[pl.ds(2 * k, 2)], held(k), in_sems.at[k])

    def store(k):
        return pltpu.make_async_copy(held(k), new_ref.at[pl.ds(2 * k, 2)], out_sems.at[k])

    def each(body):
        def step(k, carry):
            body(k)
            return carry

        lax.fori_loop(0, KL, step, 0)

    each(lambda k: load(k).start())
    eff_ref[...] = jnp.zeros(eff_ref.shape, I32)
    extend_eff(eff_ref, PAD, top_ref, bottom_ref, wet_ref)
    ext_ref[:, pl.ds(0, HALO)] = top_ref[pl.ds(0, 2 * KL)]
    ext_ref[:, pl.ds(HALO + ROWS, HALO)] = bottom_ref[pl.ds(0, 2 * KL)]
    for ref in (u_ref, l_ref, acc_ref, fx_ref, fy_ref):
        ref[...] = jnp.zeros(ref.shape, F32)
    for r0, n in CHUNKS:
        e = eff_ref[pl.ds(PAD + r0, n)]
        min_ref[0, pl.ds(r0, n)] = jnp.minimum(e, eff_ref[pl.ds(PAD + r0 - 1, n)])
        min_ref[1, pl.ds(r0, n)] = jnp.minimum(e, roll(e, 1))
        effs = (eff_ref[pl.ds(PAD + r0 - 1, n)], eff_ref[pl.ds(PAD + r0 + 1, n)], roll(e, 1), roll(e, -1))
        for word in range(3):
            word_ref[word, pl.ds(r0, n)] = count_word(effs, word)

    def count(k, r0, n):
        words = word_ref[k // 10, pl.ds(r0, n)]
        shift = jnp.full((n, LANES), 3 * (k % 10), I32)
        return (lax.shift_right_logical(words, shift) & 7).astype(F32)

    def body(step, stages):
        if 0 in stages:
            load(step).wait()
        if 3 in stages:
            store(step - 3).start()
        ku, kl, kd, kf = (step - late for late in range(4))

        def flux(r0, n):
            here = acc_ref[pl.ds(PAD + r0, n)]
            up = acc_ref[pl.ds(PAD + r0 - 1, n)]
            face_x = min_ref[0, pl.ds(r0, n)] > kf
            face_y = min_ref[1, pl.ds(r0, n)] > kf
            fx_ref[pl.ds(PAD + r0, n)] += thick_ref[kf] * jnp.where(face_x, here - up, 0.0)
            fy_ref[pl.ds(PAD + r0, n)] += thick_ref[kf] * jnp.where(face_y, here - roll(here, 1), 0.0)

        def density(r0, n):
            wet = eff_ref[pl.ds(PAD + r0, n)] > kd
            number = count(kd, r0, n)
            new = []
            for c in range(2):
                x, around = neighbours(l_ref.at[c], r0, n)
                second = jnp.where(wet, around, 0.0) - number * x
                value = ext_ref[2 * kd + c, pl.ds(r0, n)] - mixing_ref[kd, c] * second
                low, high = max(r0, HALO), min(r0 + n, HALO + ROWS)
                ext_ref[2 * kd + c, pl.ds(low, high - low)] = value[low - r0 : high - r0]
                new.append(value)
            plain = 0.8 * new[1] - 0.2 * new[0]
            acc_ref[pl.ds(PAD + r0, n)] += thick_ref[kd] * jnp.where(wet, plain, 0.0)

        def first(r0, n):
            wet = eff_ref[pl.ds(PAD + r0, n)] > kl
            number = count(kl, r0, n)
            for c in range(2):
                x, around = neighbours(u_ref.at[c], r0, n)
                l_ref[c, pl.ds(PAD + r0, n)] = jnp.where(wet, around, 0.0) - number * x

        def masked(r0, n):
            wet = eff_ref[pl.ds(PAD + r0, n)] > ku
            for c in range(2):
                u_ref[c, pl.ds(PAD + r0, n)] = jnp.where(wet, ext_ref[2 * ku + c, pl.ds(r0, n)], 0.0)

        work = ((3, flux), (2, density), (1, first), (0, masked))
        work = [part for late, part in work if late in stages]
        for turn in range(len(CHUNKS) + len(work) - 1):
            for late, part in enumerate(work):
                if 0 <= turn - late < len(CHUNKS):
                    part(*CHUNKS[turn - late])

    def all_stages(step, carry):
        body(step, range(4))
        return carry

    for step in range(3):
        body(step, range(step + 1))
    lax.fori_loop(3, KL, all_stages, 0)
    for step in range(KL, KL + 3):
        body(step, range(step - KL + 1, 4))
    for r0, n in CHUNKS:
        fx = fx_ref[pl.ds(PAD + r0, n)] - fx_ref[pl.ds(PAD + r0 + 1, n)]
        fy = fy_ref[pl.ds(PAD + r0, n)]
        source_ref[pl.ds(r0, n)] = GRAVITY * (fx + (fy - roll(fy, -1)))
        wet_ext_ref[pl.ds(r0, n)] = eff_ref[pl.ds(PAD + r0, n)]
    each(lambda k: store(k).wait())


def patch_kernel(new_ref, edge_ref, out_ref, held_ref, in_sems, out_sems):
    def planes(k):
        return pl.ds(2 * PATCH * k, 2 * PATCH)

    def load(k):
        return pltpu.make_async_copy(new_ref.at[planes(k)], held_ref.at[planes(k)], in_sems.at[k])

    def store(k):
        return pltpu.make_async_copy(held_ref.at[planes(k)], out_ref.at[planes(k)], out_sems.at[k])

    def each(body):
        def step(k, carry):
            body(k)
            return carry

        lax.fori_loop(0, KL // PATCH, step, 0)

    def levels(part):
        load(part).wait()
        for i in range(PATCH):
            k = part * PATCH + i
            tile = k % TILES
            back = (2 * LANES - 8 - GROUP * (k // TILES)) % LANES
            for c in range(2):
                for r0, n in blocks(0, ROWS, 64):
                    lane = lane_iota(n)
                    middle = jnp.logical_and(lane >= 4, lane < LANES - 4)
                    own = pl.ds(r0, n)
                    edge = pltpu.roll(edge_ref[c, tile, own], back, 1)
                    held_ref[2 * k + c, own] = jnp.where(middle, held_ref[2 * k + c, own], edge)
        store(part).start()

    each(lambda k: load(k).start())
    each(levels)
    each(lambda k: store(k).wait())


def two_sum(a, b):
    s = a + b
    v = s - a
    return s, (a - (s - v)) + (b - v)


def quick_sum(a, b):
    s = a + b
    return s, b - (s - a)


def split(a):
    t = a * 4097.0
    high = t - (t - a)
    return high, a - high


def two_prod(a, b, parts_a, parts_b):
    p = a * b
    ah, al = parts_a
    bh, bl = parts_b
    return p, ((ah * bh - p) + ah * bl + al * bh) + al * bl


def pair_add(x, y):
    s, e = two_sum(x[0], y[0])
    return quick_sum(s, e + (x[1] + y[1]))


def pair_mul(x, y):
    p, e = two_prod(x[0], y[0], split(x[0]), split(y[0]))
    return quick_sum(p, e + (x[0] * y[1] + x[1] * y[0]))


def pair_neg(x):
    return -x[0], -x[1]


def pair_div(x, y):
    q = x[0] / y[0]
    rest = pair_add(x, pair_neg(pair_mul(y, (q, jnp.zeros_like(q)))))
    return quick_sum(q, rest[0] / y[0])


def pair_clip(x, top):
    inside = jnp.logical_and(x[0] >= 0.0, x[0] <= top)
    high = jnp.where(inside, x[0], jnp.where(x[0] > top, top, 0.0))
    return high, jnp.where(inside, x[1], 0.0)


def group_totals(x):
    x = x + roll(x, GROUP)
    x = x + roll(x, 2 * GROUP)
    return x + roll(x, 4 * GROUP)


def lane_left(main, side):
    lane = lane_iota(main.shape[0])
    a, b = roll(main, 1), roll(side, 1)
    return jnp.where(lane == 0, b, a), jnp.where(lane == 0, a, b)


def lane_right(main, side):
    lane = lane_iota(main.shape[0])
    a, b = roll(main, -1), roll(side, -1)
    return jnp.where(lane == LANES - 1, b, a), jnp.where(lane == LANES - 1, a, b)


SIDES = (0, 1)


def solve_kernel(
    mixing_ref,
    thick_ref,
    source_ref,
    wet_ext_ref,
    from_left_ref,
    from_right_ref,
    edge_ref,
    seen_ref,
    beside_ref,
    depth_ref,
    sums_ref,
    new_ref,
    v_ref,
    d_ref,
    e_ref,
    west_ref,
    east_ref,
    f_ref,
    u_ref,
    l_ref,
    n_ref,
    acc_ref,
    fx_ref,
    fy_ref,
    dl_ref,
    dr_ref,
    w_ref,
    p_ref,
    q_ref,
):
    by = lax.axis_index("by")
    open_side = (by != 0, by != lax.axis_size("by") - 1)

    def clear(ref):
        ref[...] = jnp.zeros(ref.shape, ref.dtype)

    for ref in (e_ref, west_ref, east_ref):
        clear(ref)
    for ref in (u_ref, l_ref, acc_ref, d_ref, v_ref, dl_ref, dr_ref, p_ref, q_ref, fx_ref):
        rank = len(ref.shape) - 2
        lead = [()]
        for size in ref.shape[:rank]:
            lead = [i + (j,) for i in lead for j in range(size)]
        for i in lead:
            for r0 in (0, BUF - PAD):
                ref[i + (pl.ds(r0, PAD),)] = jnp.zeros((PAD, LANES), F32)

    def field(side, c, tile, r0, n):
        own = edge_ref[c, tile, pl.ds(r0, n)]
        first = first_half(n)
        if side == 0:
            far = from_left_ref[tile, pl.ds(r0, n)]
            return jnp.where(first, roll(far, -8) if c else far, own)
        far = from_right_ref[tile, pl.ds(r0, n)]
        return jnp.where(first, own, roll(far, 8) if c else far)

    tile_eff, slot = edge_slot(KL)
    for side in SIDES:
        for r0, n in CHUNKS:
            lane = lane_iota(n)
            x = field(side, 0, tile_eff, r0, n)
            inner = (lane & 8) == (8 if side == 0 else 0)
            keep = jnp.logical_and(lane // GROUP == slot, jnp.logical_or(inner, open_side[side]))
            e = group_totals(jnp.where(keep, x, 0.0)).astype(I32)
            at = pl.ds(PAD + r0, n)
            e_ref[side, at] = e
            west_ref[side, at] = roll(e, 1)
            east_ref[side, at] = roll(e, -1)

    group8 = lane_iota(8) // GROUP

    def by_group(tile, values):
        out = jnp.zeros((8, LANES), F32)
        for g in range(GROUPS):
            k = TILES * g + tile
            value = values(jnp.minimum(k, KL - 1))
            out = jnp.where(group8 == g, jnp.where(k < KL, value, 0.0), out)
        return out[0:1]

    def level_lanes(tile):
        return (group8 * TILES + tile)[0:1]

    def tile_step(tile, carry):
        level_of = level_lanes(tile)
        mix = [by_group(tile, lambda k, c=c: mixing_ref[k, c]) for c in range(2)]
        thick = by_group(tile, lambda k: thick_ref[k])

        def masked(side, r0, n):
            at = pl.ds(PAD + r0, n)
            wet = e_ref[side, at] > level_of
            for c in range(2):
                x = field(side, c, tile, r0, n)
                f_ref[side, c, pl.ds(r0, n)] = x
                u_ref[side, c, at] = jnp.where(wet, x, 0.0)

        def first(side, r0, n):
            at = pl.ds(PAD + r0, n)
            wet = e_ref[side, at] > level_of
            number = jnp.where(e_ref[side, pl.ds(PAD + r0 - 1, n)] > level_of, 1.0, 0.0)
            number += jnp.where(e_ref[side, pl.ds(PAD + r0 + 1, n)] > level_of, 1.0, 0.0)
            number += jnp.where(west_ref[side, at] > level_of, 1.0, 0.0)
            number += jnp.where(east_ref[side, at] > level_of, 1.0, 0.0)
            n_ref[side, pl.ds(r0, n)] = number
            for c in range(2):
                x, around = neighbours(u_ref.at[side, c], r0, n)
                l_ref[side, c, at] = jnp.where(wet, around, 0.0) - number * x

        def density(side, r0, n):
            at = pl.ds(PAD + r0, n)
            wet = e_ref[side, at] > level_of
            number = n_ref[side, pl.ds(r0, n)]
            new = []
            for c in range(2):
                x, around = neighbours(l_ref.at[side, c], r0, n)
                second = jnp.where(wet, around, 0.0) - number * x
                new.append(f_ref[side, c, pl.ds(r0, n)] - mix[c] * second)
            acc_ref[side, tile, at] = thick * jnp.where(wet, 0.8 * new[1] - 0.2 * new[0], 0.0)
            low, high = max(r0, HALO), min(r0 + n, HALO + ROWS)
            own = pl.ds(low - HALO, high - low)
            for c in range(2):
                value = new[c][low - r0 : high - r0]
                if side == 1:
                    value = jnp.where(first_half(high - low), value, new_ref[c, tile, own])
                new_ref[c, tile, own] = value

        for part in (masked, first, density):
            for side in SIDES:
                for r0, n in CHUNKS:
                    part(side, r0, n)
        return carry

    lax.fori_loop(0, TILES, tile_step, 0)

    for side in SIDES:
        for r0, n in CHUNKS:
            lane = lane_iota(n)
            at = pl.ds(PAD + r0, n)
            layers = [acc_ref[side, tile, at] for tile in range(TILES)]
            run = (layers[0] + layers[1]) + layers[2]
            run = jnp.where(lane >= GROUP, roll(run, GROUP), 0.0)
            for step in (1, 2, 4):
                run = run + jnp.where(lane >= step * GROUP, roll(run, step * GROUP), 0.0)
            for tile in range(TILES):
                run = run + layers[tile]
                acc_ref[side, tile, at] = run
    thick = [by_group(tile, lambda k: thick_ref[k]) for tile in range(TILES)]
    table = jnp.zeros((8, LANES), F32)
    for k in range(KL):
        table += jnp.where(lane_iota(8) > k, thick_ref[k], 0.0)
    halves = blocks(0, EXT, EXT // 2)
    for r0, n in halves:
        at = pl.ds(PAD + r0, n)
        for side in SIDES:
            e = e_ref[side, at]
            min_x = jnp.minimum(e, e_ref[side, pl.ds(PAD + r0 - 1, n)])
            min_y = jnp.minimum(e, west_ref[side, at])
            face_x = jnp.zeros((n, LANES), F32)
            face_y = face_x
            for tile in range(TILES):
                here = acc_ref[side, tile, at]
                up = acc_ref[side, tile, pl.ds(PAD + r0 - 1, n)]
                level_of = level_lanes(tile)
                face_x += thick[tile] * jnp.where(min_x > level_of, here - up, 0.0)
                face_y += thick[tile] * jnp.where(min_y > level_of, here - roll(here, 1), 0.0)
            fx_ref[side, at] = face_x
            fy_ref[side, pl.ds(r0, n)] = face_y
    for r0, n in halves:
        lane = lane_iota(n)
        at = pl.ds(PAD + r0, n)
        own = pl.ds(r0, n)
        sources = []
        for side in SIDES:
            fy = fy_ref[side, own]
            sources.append(fx_ref[side, at] - fx_ref[side, pl.ds(PAD + r0 + 1, n)] + (fy - roll(fy, -1)))
        for shift in (GROUP, 2 * GROUP, 4 * GROUP):
            sources = [x + roll(x, shift) for x in sources]
        west, east = (GRAVITY * roll(x, 8) for x in sources)
        v_ref[0, 0, at] = jnp.where(lane < 3, west, jnp.where(lane >= LANES - 3, east, source_ref[own]))
        v_ref[0, 1, at] = jnp.where(lane < 8, east, jnp.where(lane >= LANES - 8, west, 0.0))
    for r0, n in halves:
        lane = lane_iota(n)
        at = pl.ds(PAD + r0, n)
        west = roll(e_ref[0, at], 8)
        east = roll(e_ref[1, at], 8)
        beside = jnp.where(lane < 8, east, jnp.where(lane >= LANES - 8, west, 0))
        main = wet_ext_ref[pl.ds(r0, n)]
        for t, wet in enumerate((main, beside)):
            for i in range(0, n, 8):
                d_ref[t, pl.ds(PAD + r0 + i, 8)] = jnp.take_along_axis(table, wet[i : i + 8], axis=1)
    for r0, n in CHUNKS:
        here = pl.ds(PAD + r0, n)
        d_main, d_side = d_ref[0, here], d_ref[1, here]
        dl_ref[0, here], dl_ref[1, here] = lane_left(d_main, d_side)
        dr_ref[0, here], dr_ref[1, here] = lane_right(d_main, d_side)

    def weights(t, carry):
        for r0, n in CHUNKS:
            here = pl.ds(PAD + r0, n)
            above = pl.ds(PAD + r0 - 1, n)
            below = pl.ds(PAD + r0 + 1, n)
            d = d_ref[t, here]
            left, right = dl_ref[t, here], dr_ref[t, here]
            up, down = d_ref[t, above], d_ref[t, below]
            w_west, w_east = jnp.minimum(d, left), jnp.minimum(d, right)
            w_up, w_down = jnp.minimum(d, up), jnp.minimum(d, down)
            corners = (
                jnp.minimum(d, dl_ref[t, above])
                + jnp.minimum(d, dr_ref[t, below])
                + jnp.minimum(d, dr_ref[t, above])
                + jnp.minimum(d, dl_ref[t, below])
            )
            at = pl.ds(r0, n)
            w_ref[0, t, at] = 0.05 + w_up + w_down + w_west + w_east + 0.25 * corners
            w_ref[1, t, at] = w_west
            w_ref[2, t, at] = w_east
            w_ref[3, t, at] = w_down
            w_ref[4, t, at] = 0.25 * jnp.minimum(down, left)
            w_ref[5, t, at] = 0.25 * jnp.minimum(down, right)
            w_ref[6, t, at] = w_up
            w_ref[7, t, at] = 0.25 * jnp.minimum(up, left)
            w_ref[8, t, at] = 0.25 * jnp.minimum(up, right)
        return carry

    lax.fori_loop(0, 2, weights, 0)

    def power(step, carry):
        for r0, n in CHUNKS:
            here = pl.ds(PAD + r0, n)
            at = pl.ds(r0, n)
            v = (v_ref[step, 0, here], v_ref[step, 1, here])
            left = lane_left(*v)
            right = lane_right(*v)
            for t in range(2):
                w = [w_ref[m, t, at] for m in range(9)]
                p_ref[t, here] = w[3] * v[t] + w[4] * left[t] + w[5] * right[t]
                q_ref[t, here] = w[6] * v[t] + w[7] * left[t] + w[8] * right[t]
                v_ref[step + 1, t, here] = w[0] * v[t] - (w[1] * left[t] + w[2] * right[t])
        for r0, n in CHUNKS:
            here = pl.ds(PAD + r0, n)
            for t in range(2):
                beside = p_ref[t, pl.ds(PAD + r0 - 1, n)] + q_ref[t, pl.ds(PAD + r0 + 1, n)]
                v_ref[step + 1, t, here] -= beside
        return carry

    lax.fori_loop(0, 4, power, 0)

    for i in range(4):
        seen_ref[i] = v_ref[i, 0, pl.ds(PAD, SEEN)]
    depth_ref[...] = d_ref[0, pl.ds(PAD, SEEN)]
    for r0, n in OWN_CHUNKS:
        lane = lane_iota(n)
        at = pl.ds(PAD + r0, n)
        beside = roll(d_ref[1, at], 5)
        for i in range(4):
            beside = jnp.where(lane == i, roll(v_ref[i, 1, at], i + 1), beside)
        beside_ref[pl.ds(r0 - HALO, n)] = beside

    def dots(step, carry):
        at = pl.ds(pl.multiple_of(PAD + HALO + 8 * step, 8), 8)
        v = [v_ref[i, 0, at] for i in range(5)]
        parts = [split(x) for x in v]
        out = []
        for m in range(MOMENTS):
            i, j = m // 2, (m + 1) // 2
            p, e = two_prod(v[i], v[j], parts[i], parts[j])
            s, f = two_sum(carry[2 * m], p)
            out += [s, carry[2 * m + 1] + (e + f)]
        return tuple(out)

    zero = jnp.zeros((8, LANES), F32)
    sums = lax.fori_loop(0, ROWS // 8, dots, (zero,) * (2 * MOMENTS), unroll=4)
    sub = lax.broadcasted_iota(I32, (8, LANES), 0)
    pairs = [(sums[2 * m], sums[2 * m + 1]) for m in range(MOMENTS)]
    for half in (4, 2, 1):
        merged = []
        for m in range(half):
            a, b = pairs[m], pairs[m + half]
            upper = (sub & half) == 0
            keep = tuple(jnp.where(upper, x, y) for x, y in zip(a, b))
            other = tuple(jnp.where(upper, pltpu.roll(x, 8 - half, 0), pltpu.roll(y, half, 0)) for x, y in zip(a, b))
            merged.append(pair_add(keep, other))
        pairs = merged
    wide = [jnp.concatenate([x, jnp.zeros((LANES - 8, LANES), F32)]).T for x in pairs[0]]
    rows = [tuple(x[at : at + 8] for x in wide) for at in range(0, LANES, 8)]
    while len(rows) > 1:
        rows = [pair_add(rows[i], rows[i + 1]) for i in range(0, len(rows), 2)]
    total = rows[0]
    for shift in (4, 2, 1):
        total = pair_add(total, tuple(pltpu.roll(x, shift, 0) for x in total))
    row = total[0] + roll(total[1], MOMENTS)
    for at in range(0, sums_ref.shape[0], 8):
        sums_ref[pl.ds(at, 8)] = row


def finish_kernel(all_ref, seen_ref, beside_ref, depth_ref, surface_ref, flow_ref, s_ref):
    zero = jnp.zeros((8, LANES), F32)
    high, low = zero, zero
    for at in range(0, all_ref.shape[0], 8):
        high, e = two_sum(high, all_ref[pl.ds(at, 8)])
        low = low + e
    total = (high, low)
    for shift in (4, 2, 1):
        total = pair_add(total, tuple(pltpu.roll(x, shift, 0) for x in total))
    total = pair_add(total, tuple(roll(x, -MOMENTS) for x in total))
    lane = lane_iota(8)

    def moment(m):
        return tuple(
            jnp.broadcast_to(jnp.sum(jnp.where(lane == m, x, 0.0), axis=1, keepdims=True), (8, LANES))
            for x in total
        )

    rho = [moment(m) for m in range(MOMENTS)]
    pi = list(rho)
    nought = (zero, zero)
    one = (zero + 1.0, zero)
    surface = [nought] * 4
    residual = [one] + [nought] * 3
    direction = list(residual)
    for step in range(4):
        alpha = pair_clip(pair_div(rho[step], pi[step + 1]), 20.0)
        for i in range(step + 1):
            surface[i] = pair_add(surface[i], pair_mul(alpha, direction[i]))
        if step == 3:
            break
        minus = pair_neg(alpha)
        new_rho = list(rho)
        for m in range(step + 1, MOMENTS - 1 - step):
            new_rho[m] = pair_add(rho[m], pair_mul(minus, pi[m + 1]))
        beta = pair_clip(pair_div(pair_mul(minus, new_rho[step + 1]), rho[step]), 400.0)
        for m in range(step + 2, MOMENTS - 1 - step):
            pi[m] = pair_add(new_rho[m], pair_mul(beta, pi[m]))
        rho = new_rho
        for i in range(step + 1, 0, -1):
            residual[i] = pair_add(residual[i], pair_mul(minus, direction[i - 1]))
        for i in range(step + 2):
            direction[i] = pair_add(residual[i], pair_mul(beta, direction[i]))
    weight = [s[0][0:1] for s in surface]
    lane = lane_iota(1)
    by_lane = jnp.zeros((1, LANES), F32)
    for i in range(4):
        by_lane = jnp.where(lane == i, weight[i], by_lane)
    for r0, n in blocks(0, SEEN, 88):
        at = pl.ds(r0, n)
        total = weight[0] * seen_ref[0, at]
        for i in range(1, 4):
            total = total + weight[i] * seen_ref[i, at]
        s_ref[at] = total
    for r0, n in blocks(HALO, SEEN, 128):
        at = pl.ds(r0, n)
        above = pl.ds(r0 - 1, n)
        own = pl.ds(r0 - HALO, n)
        lane = lane_iota(n)
        s, d = s_ref[at], depth_ref[at]
        beside = beside_ref[own]
        d_west = jnp.where(lane == 0, roll(beside, -4), roll(d, 1))
        beside = by_lane * beside
        beside = beside + roll(beside, -1)
        west = jnp.where(lane == 0, beside + roll(beside, -2), roll(s, 1))
        surface_ref[own] = s
        flow_ref[0, own] = jnp.minimum(d, depth_ref[above]) * (s_ref[above] - s)
        flow_ref[1, own] = jnp.minimum(d, d_west) * (west - s)


VM = pl.BlockSpec(memory_space=pltpu.VMEM)
SM = pl.BlockSpec(memory_space=pltpu.SMEM)
HBM = pl.BlockSpec(memory_space=pltpu.HBM)


def params(limit):
    return pltpu.CompilerParams(vmem_limit_bytes=limit * MIB)


def cost(flops, moved):
    return pl.CostEstimate(flops=flops, bytes_accessed=moved, transcendentals=0)


def ring(x, axis, step):
    count = lax.axis_size(axis)
    return lax.ppermute(x, axis, [(i, (i + step) % count) for i in range(count)])


def shape(*sizes, dtype=F32):
    return jax.ShapeDtypeStruct(sizes, dtype)


def scratch(*lead, rows=BUF, dtype=F32):
    return pltpu.VMEM(lead + (rows, LANES), dtype)


def shards(tracers, mixing, thickness, levels, land):
    devices = lax.axis_size("bx") * lax.axis_size("by")
    planes = 2 * KL
    wet = wet_levels(levels, land).astype(F32)
    flat = tracers.reshape(planes, ROWS, LANES)
    with jax.named_scope("rows"):
        to_up = jnp.concatenate([flat[:, :HALO], wet[None, :HALO]])
        to_down = jnp.concatenate([flat[:, -HALO:], wet[None, -HALO:]])
        top = ring(to_down, "bx", 1)
        bottom = ring(to_up, "bx", -1)
    with jax.named_scope("columns"):
        edges = (shape(2, TILES, EXT, LANES), shape(TILES, EXT, LANES), shape(TILES, EXT, LANES))
        own = pl.pallas_call(
            own_edges_kernel,
            out_shape=edges,
            in_specs=[HBM, VM],
            out_specs=(VM,) * 3,
            scratch_shapes=[scratch(planes, rows=ROWS), pltpu.SemaphoreType.DMA((LOADS,))],
            compiler_params=params(48),
            cost_estimate=cost(10_000_000, 7_000_000),
        )(flat, wet)
        edge, to_right, to_left = pl.pallas_call(
            halo_edges_kernel,
            out_shape=edges,
            in_specs=[VM] * 5,
            out_specs=(VM,) * 3,
            input_output_aliases={i + 2: i for i in range(3)},
            compiler_params=params(16),
            cost_estimate=cost(1_000_000, 700_000),
        )(top, bottom, *own)
        from_left = ring(to_right, "by", 1)
        from_right = ring(to_left, "by", -1)
    with jax.named_scope("block"):
        new, source, wet_ext = pl.pallas_call(
            block_kernel,
            out_shape=(shape(planes, ROWS, LANES), shape(EXT, LANES), shape(EXT, LANES, dtype=I32)),
            in_specs=[SM, SM, HBM, VM, VM, VM],
            out_specs=(HBM, VM, VM),
            scratch_shapes=[
                scratch(planes, rows=EXT),
                scratch(dtype=I32),
                scratch(2, rows=EXT, dtype=I32),
                scratch(3, rows=EXT, dtype=I32),
                scratch(2),
                scratch(2),
                scratch(),
                scratch(),
                scratch(),
                pltpu.SemaphoreType.DMA((KL,)),
                pltpu.SemaphoreType.DMA((KL,)),
            ],
            compiler_params=params(48),
            cost_estimate=cost(50_000_000, 12_000_000),
        )(mixing, thickness, flat, top, bottom, wet)
    with jax.named_scope("powers"):
        seen, beside, depth, sums, new_edge = pl.pallas_call(
            solve_kernel,
            out_shape=(
                shape(4, SEEN, LANES),
                shape(ROWS, LANES),
                shape(SEEN, LANES),
                shape(devices, LANES),
                shape(2, TILES, ROWS, LANES),
            ),
            in_specs=[SM, SM] + [VM] * 5,
            out_specs=(VM,) * 5,
            scratch_shapes=[
                scratch(5, 2),
                scratch(2),
                scratch(2, dtype=I32),
                scratch(2, dtype=I32),
                scratch(2, dtype=I32),
                scratch(2, 2, rows=EXT),
                scratch(2, 2),
                scratch(2, 2),
                scratch(2, rows=EXT),
                scratch(2, TILES),
                scratch(2),
                scratch(2, rows=EXT),
                scratch(2),
                scratch(2),
                scratch(9, 2, rows=EXT),
                scratch(2),
                scratch(2),
            ],
            compiler_params=params(20),
            cost_estimate=cost(50_000_000, 6_000_000),
        )(mixing, thickness, source, wet_ext, from_left, from_right, edge)
    with jax.named_scope("sums"):
        everyone = lax.all_to_all(sums, ("bx", "by"), 0, 0, tiled=True)
    with jax.named_scope("patch"):
        tracers_new = pl.pallas_call(
            patch_kernel,
            out_shape=shape(planes, ROWS, LANES),
            in_specs=[HBM, VM],
            out_specs=HBM,
            scratch_shapes=[
                scratch(planes, rows=ROWS),
                pltpu.SemaphoreType.DMA((KL // PATCH,)),
                pltpu.SemaphoreType.DMA((KL // PATCH,)),
            ],
            compiler_params=params(48),
            cost_estimate=cost(10_000_000, 12_000_000),
        )(new, new_edge)
    with jax.named_scope("surface"):
        surface, transports = pl.pallas_call(
            finish_kernel,
            out_shape=(shape(ROWS, LANES), shape(2, ROWS, LANES)),
            in_specs=[VM] * 4,
            out_specs=(VM, VM),
            scratch_shapes=[scratch(rows=SEEN)],
            compiler_params=params(8),
            cost_estimate=cost(1_000_000, 3_000_000),
        )(everyone, seen, beside, depth)
    return tracers_new.reshape(tracers.shape), surface, transports


def solution(mesh):
    in_specs = (P(None, None, "bx", "by"), P(), P(), P("bx", "by"), P("bx", "by"))
    out_specs = (P(None, None, "bx", "by"), P("bx", "by"), P(None, "bx", "by"))
    return jax.shard_map(shards, mesh=mesh, in_specs=in_specs, out_specs=out_specs, check_vma=False)
```

```python
import jax
import jax.numpy as jnp
from jax import lax
from jax.experimental import pallas as pl
from jax.experimental.pallas import tpu as pltpu
from jax.sharding import PartitionSpec as P

KL = 22
ROWS = 256
LANES = 128
HALO = 8
EXT = ROWS + 2 * HALO
PAD = 8
BUF = EXT + 2 * PAD
GROUP = 16
GROUPS = LANES // GROUP
TILES = 3
LOADS = 4
MOMENTS = 8
PATCH = 2
GRAVITY = 10.0
SEEN = HALO + ROWS
F32 = jnp.float32
I32 = jnp.int32
MIB = 1024 * 1024


def lane_iota(rows):
    return lax.broadcasted_iota(I32, (rows, LANES), 1)


def first_half(rows):
    return (lane_iota(rows) & 8) == 0


def tall(x, n):
    return jnp.concatenate([x] * (n // 8)) if n > 8 else x


def roll(x, shift):
    return pltpu.roll(x, shift % LANES, 1)


def blocks(start, stop, size):
    out = []
    while start < stop:
        out.append((start, min(size, stop - start)))
        start += size
    return out


CHUNKS = blocks(0, EXT, 32)
OWN_CHUNKS = blocks(HALO, HALO + ROWS, 32)


def interleave(parts):
    for turn in range(len(CHUNKS) + len(parts) - 1):
        for late, part in enumerate(parts):
            if 0 <= turn - late < len(CHUNKS):
                part(*CHUNKS[turn - late])


def wet_levels(levels, land):
    return jnp.where(land == 0, levels, 0)


def tops(thick_ref):
    out = [jnp.float32(0.0)]
    for k in range(KL):
        out.append(out[-1] + thick_ref[k])
    return out


def depth_table(levels):
    table = jnp.zeros((8, LANES), F32)
    for k, top in enumerate(levels):
        table = jnp.where(lane_iota(8) == k, top, table)
    return table


def look_up(table, index):
    rows = [jnp.take_along_axis(table, index[i : i + 8], axis=1) for i in range(0, index.shape[0], 8)]
    return jnp.concatenate(rows) if len(rows) > 1 else rows[0]


def edge_slot(k):
    return k % TILES, k // TILES


def place(x, k, old):
    _, g = edge_slot(k)
    return jnp.where(lane_iota(x.shape[0]) // GROUP == g, roll(x, 8 + GROUP * g), old)


def to_neighbours(a, b):
    first = first_half(a.shape[0])
    return jnp.where(first, a, roll(b, 8)), jnp.where(first, roll(b, -8), a)


def own_edges_kernel(t_ref, wet_ref, edge_ref, right_ref, left_ref, own_ref, sems):
    parts = blocks(0, KL, -(-KL // LOADS))

    def copy(i):
        start, count = parts[i]
        planes = pl.ds(2 * start, 2 * count)
        return pltpu.make_async_copy(t_ref.at[planes], own_ref.at[planes], sems.at[i])

    for i in range(len(parts)):
        copy(i).start()
    size = 128
    tile_eff, _ = edge_slot(KL)

    def rows_of(step):
        own = pl.ds(pl.multiple_of(size * step, 8), size)
        return own, pl.ds(pl.multiple_of(HALO + size * step, 8), size)

    def clear(step, carry):
        own, at = rows_of(step)
        zero = jnp.zeros((size, LANES), F32)
        for c in range(2):
            for tile in range(TILES):
                edge_ref[c, tile, at] = zero
            edge_ref[c, tile_eff, at] = place(wet_ref[own], KL, zero)
        return carry

    lax.fori_loop(0, ROWS // size, clear, 0)
    for i, (start, count) in enumerate(parts):
        copy(i).wait()

        def rows(step, carry):
            own, at = rows_of(step)
            for k in range(start, start + count):
                tile, _ = edge_slot(k)
                for c in range(2):
                    edge_ref[c, tile, at] = place(own_ref[2 * k + c, own], k, edge_ref[c, tile, at])
            return carry

        lax.fori_loop(0, ROWS // size, rows, 0)

    def send(step, carry):
        _, at = rows_of(step)
        for tile in range(TILES):
            right_ref[tile, at], left_ref[tile, at] = to_neighbours(edge_ref[0, tile, at], edge_ref[1, tile, at])
        return carry

    lax.fori_loop(0, ROWS // size, send, 0)


def halo_edges_kernel(top_ref, bottom_ref, edge_in, right_in, left_in, edge_ref, right_ref, left_ref):
    for r0, ref in ((0, top_ref), (HALO + ROWS, bottom_ref)):
        at = pl.ds(r0, HALO)
        held = [[jnp.zeros((HALO, LANES), F32) for _ in range(TILES)] for _ in range(2)]
        for k in range(KL + 1):
            tile, _ = edge_slot(k)
            for c in range(2):
                x = ref[2 * k + c] if k < KL else ref[2 * KL]
                held[c][tile] = place(x, k, held[c][tile])
        for tile in range(TILES):
            for c in range(2):
                edge_ref[c, tile, at] = held[c][tile]
            right_ref[tile, at], left_ref[tile, at] = to_neighbours(held[0][tile], held[1][tile])


def count_word(effs, word):
    total = None
    for eff in effs:
        bits = jnp.clip(eff - 10 * word, 0, 10) * 3
        mask = (lax.shift_left(jnp.full_like(bits, 1), bits) - 1) & 0o1111111111
        total = mask if total is None else total + mask
    return total


def neighbours(ref, r0, n):
    x = ref[pl.ds(PAD + r0, n)]
    around = ref[pl.ds(PAD + r0 - 1, n)] + ref[pl.ds(PAD + r0 + 1, n)]
    return x, around + (roll(x, 1) + roll(x, -1))


def block_kernel(
    mixing_ref,
    thick_ref,
    t_ref,
    top_ref,
    bottom_ref,
    wet_ref,
    new_ref,
    source_ref,
    depth_ref,
    ext_ref,
    eff_ref,
    face_ref,
    word_ref,
    u_ref,
    l_ref,
    n_ref,
    rho_ref,
    fx_ref,
    fy_ref,
    begin_ref,
    in_sems,
    out_sems,
):
    def held(k):
        return ext_ref.at[pl.ds(2 * k, 2), pl.ds(HALO, ROWS)]

    def load(k):
        return pltpu.make_async_copy(t_ref.at[pl.ds(2 * k, 2)], held(k), in_sems.at[k])

    def store(k):
        return pltpu.make_async_copy(held(k), new_ref.at[pl.ds(2 * k, 2)], out_sems.at[k])

    def each(body):
        def step(k, carry):
            body(k)
            return carry

        lax.fori_loop(0, KL, step, 0)

    each(lambda k: load(k).start())
    eff_ref[...] = jnp.zeros(eff_ref.shape, I32)
    eff_ref[pl.ds(PAD, HALO)] = top_ref[2 * KL].astype(I32)
    eff_ref[pl.ds(PAD + HALO, ROWS)] = wet_ref[...].astype(I32)
    eff_ref[pl.ds(PAD + HALO + ROWS, HALO)] = bottom_ref[2 * KL].astype(I32)
    ext_ref[:, pl.ds(0, HALO)] = top_ref[pl.ds(0, 2 * KL)]
    ext_ref[:, pl.ds(HALO + ROWS, HALO)] = bottom_ref[pl.ds(0, 2 * KL)]
    for ref in (u_ref, l_ref, rho_ref, fx_ref, fy_ref):
        ref[...] = jnp.zeros(ref.shape, F32)
    levels = tops(thick_ref)
    table = depth_table(levels)
    for k in range(KL):
        begin_ref[k] = levels[k]
    for r0, n in CHUNKS:
        e = eff_ref[pl.ds(PAD + r0, n)]
        up = eff_ref[pl.ds(PAD + r0 - 1, n)]
        west = roll(e, 1)
        depth_ref[pl.ds(r0, n)] = look_up(table, e)
        face_ref[0, pl.ds(r0, n)] = look_up(table, jnp.minimum(e, up))
        face_ref[1, pl.ds(r0, n)] = look_up(table, jnp.minimum(e, west))
        effs = (up, eff_ref[pl.ds(PAD + r0 + 1, n)], west, roll(e, -1))
        for word in range(3):
            word_ref[word, pl.ds(r0, n)] = count_word(effs, word)

    def count(k, r0, n):
        words = word_ref[k // 10, pl.ds(r0, n)]
        shift = jnp.full((n, LANES), 3 * (k % 10), I32)
        return (lax.shift_right_logical(words, shift) & 7).astype(F32)

    def body(step, stages):
        if 0 in stages:
            load(step).wait()
        if 3 in stages:
            store(step - 3).start()
        ku, kl, kd, kf = (step - late for late in range(4))

        def flux(r0, n):
            here = rho_ref[pl.ds(PAD + r0, n)]
            up = rho_ref[pl.ds(PAD + r0 - 1, n)]
            below_x = jnp.maximum(face_ref[0, pl.ds(r0, n)] - begin_ref[kf], 0.0)
            below_y = jnp.maximum(face_ref[1, pl.ds(r0, n)] - begin_ref[kf], 0.0)
            fx_ref[pl.ds(PAD + r0, n)] += below_x * (here - up)
            fy_ref[pl.ds(PAD + r0, n)] += below_y * (here - roll(here, 1))

        def density(r0, n):
            wet = eff_ref[pl.ds(PAD + r0, n)] > kd
            number = n_ref[pl.ds(r0, n)]
            new = []
            for c in range(2):
                x, around = neighbours(l_ref.at[c], r0, n)
                second = jnp.where(wet, around, 0.0) - number * x
                value = ext_ref[2 * kd + c, pl.ds(r0, n)] - mixing_ref[kd, c] * second
                low, high = max(r0, HALO), min(r0 + n, HALO + ROWS)
                ext_ref[2 * kd + c, pl.ds(low, high - low)] = value[low - r0 : high - r0]
                new.append(value)
            rho_ref[pl.ds(PAD + r0, n)] = (0.8 * thick_ref[kd]) * new[1] - (0.2 * thick_ref[kd]) * new[0]

        def first(r0, n):
            wet = eff_ref[pl.ds(PAD + r0, n)] > kl
            number = count(kl, r0, n)
            n_ref[pl.ds(r0, n)] = number
            for c in range(2):
                x, around = neighbours(u_ref.at[c], r0, n)
                l_ref[c, pl.ds(PAD + r0, n)] = jnp.where(wet, around, 0.0) - number * x

        def masked(r0, n):
            wet = eff_ref[pl.ds(PAD + r0, n)] > ku
            for c in range(2):
                u_ref[c, pl.ds(PAD + r0, n)] = jnp.where(wet, ext_ref[2 * ku + c, pl.ds(r0, n)], 0.0)

        work = ((3, flux), (2, density), (1, first), (0, masked))
        interleave([part for late, part in work if late in stages])

    def all_stages(step, carry):
        body(step, range(4))
        return carry

    for step in range(3):
        body(step, range(step + 1))
    lax.fori_loop(3, KL, all_stages, 0)
    for step in range(KL, KL + 3):
        body(step, range(step - KL + 1, 4))
    for r0, n in CHUNKS:
        fx = fx_ref[pl.ds(PAD + r0, n)] - fx_ref[pl.ds(PAD + r0 + 1, n)]
        fy = fy_ref[pl.ds(PAD + r0, n)]
        source_ref[pl.ds(r0, n)] = GRAVITY * (fx + (fy - roll(fy, -1)))
    each(lambda k: store(k).wait())


def patch_kernel(new_ref, edge_ref, out_ref, held_ref, in_sems, out_sems):
    def planes(k):
        return pl.ds(2 * PATCH * k, 2 * PATCH)

    def load(k):
        return pltpu.make_async_copy(new_ref.at[planes(k)], held_ref.at[planes(k)], in_sems.at[k])

    def store(k):
        return pltpu.make_async_copy(held_ref.at[planes(k)], out_ref.at[planes(k)], out_sems.at[k])

    def each(body):
        def step(k, carry):
            body(k)
            return carry

        lax.fori_loop(0, KL // PATCH, step, 0)

    def levels(part):
        load(part).wait()
        for i in range(PATCH):
            k = part * PATCH + i
            tile = k % TILES
            back = (2 * LANES - 8 - GROUP * (k // TILES)) % LANES
            for c in range(2):
                for r0, n in blocks(0, ROWS, 64):
                    lane = lane_iota(n)
                    middle = jnp.logical_and(lane >= 4, lane < LANES - 4)
                    own = pl.ds(r0, n)
                    edge = pltpu.roll(edge_ref[c, tile, own], back, 1)
                    held_ref[2 * k + c, own] = jnp.where(middle, held_ref[2 * k + c, own], edge)
        store(part).start()

    each(lambda k: load(k).start())
    each(levels)
    each(lambda k: store(k).wait())


def two_sum(a, b):
    s = a + b
    v = s - a
    return s, (a - (s - v)) + (b - v)


def quick_sum(a, b):
    s = a + b
    return s, b - (s - a)


def split(a):
    t = a * 4097.0
    high = t - (t - a)
    return high, a - high


def two_prod(a, b, parts_a, parts_b):
    p = a * b
    ah, al = parts_a
    bh, bl = parts_b
    return p, ((ah * bh - p) + ah * bl + al * bh) + al * bl


def pair_add(x, y):
    s, e = two_sum(x[0], y[0])
    return quick_sum(s, e + (x[1] + y[1]))


def loose_add(x, y):
    s, e = two_sum(x[0], y[0])
    return s, e + (x[1] + y[1])


def pair_mul(x, y):
    p, e = two_prod(x[0], y[0], split(x[0]), split(y[0]))
    return quick_sum(p, e + (x[0] * y[1] + x[1] * y[0]))


def pair_neg(x):
    return -x[0], -x[1]


def pair_div(x, y):
    q = x[0] / y[0]
    rest = pair_add(x, pair_neg(pair_mul(y, (q, jnp.zeros_like(q)))))
    return quick_sum(q, rest[0] / y[0])


def pair_clip(x, top):
    inside = jnp.logical_and(x[0] >= 0.0, x[0] <= top)
    high = jnp.where(inside, x[0], jnp.where(x[0] > top, top, 0.0))
    return high, jnp.where(inside, x[1], 0.0)


def group_totals(x):
    x = x + roll(x, GROUP)
    x = x + roll(x, 2 * GROUP)
    return x + roll(x, 4 * GROUP)


def lane_left(main, side):
    lane = lane_iota(main.shape[0])
    a, b = roll(main, 1), roll(side, 1)
    return jnp.where(lane == 0, b, a), jnp.where(lane == 0, a, b)


def lane_right(main, side):
    lane = lane_iota(main.shape[0])
    a, b = roll(main, -1), roll(side, -1)
    return jnp.where(lane == LANES - 1, b, a), jnp.where(lane == LANES - 1, a, b)


SIDES = (0, 1)


def solve_kernel(
    mixing_ref,
    thick_ref,
    source_ref,
    depth_in,
    from_left_ref,
    from_right_ref,
    edge_ref,
    seen_ref,
    beside_ref,
    depth_ref,
    sums_ref,
    new_ref,
    v_ref,
    d_ref,
    e_ref,
    west_ref,
    east_ref,
    f_ref,
    u_ref,
    l_ref,
    n_ref,
    rho_ref,
    fx_ref,
    fy_ref,
    face_ref,
    lanes_ref,
    dl_ref,
    dr_ref,
    w_ref,
    p_ref,
    q_ref,
):
    by = lax.axis_index("by")
    open_side = (by != 0, by != lax.axis_size("by") - 1)

    def clear(ref):
        ref[...] = jnp.zeros(ref.shape, ref.dtype)

    for ref in (e_ref, west_ref, east_ref):
        clear(ref)
    for ref in (u_ref, l_ref, rho_ref, d_ref, v_ref, dl_ref, dr_ref, p_ref, q_ref, fx_ref):
        rank = len(ref.shape) - 2
        lead = [()]
        for size in ref.shape[:rank]:
            lead = [i + (j,) for i in lead for j in range(size)]
        for i in lead:
            for r0 in (0, BUF - PAD):
                ref[i + (pl.ds(r0, PAD),)] = jnp.zeros((PAD, LANES), F32)

    def field(side, c, tile, r0, n):
        own = edge_ref[c, tile, pl.ds(r0, n)]
        first = first_half(n)
        if side == 0:
            far = from_left_ref[tile, pl.ds(r0, n)]
            return jnp.where(first, roll(far, -8) if c else far, own)
        far = from_right_ref[tile, pl.ds(r0, n)]
        return jnp.where(first, own, roll(far, 8) if c else far)

    tile_eff, slot = edge_slot(KL)
    for side in SIDES:
        for r0, n in CHUNKS:
            lane = lane_iota(n)
            x = field(side, 0, tile_eff, r0, n)
            inner = (lane & 8) == (8 if side == 0 else 0)
            keep = jnp.logical_and(lane // GROUP == slot, jnp.logical_or(inner, open_side[side]))
            e = group_totals(jnp.where(keep, x, 0.0)).astype(I32)
            at = pl.ds(PAD + r0, n)
            e_ref[side, at] = e
            west_ref[side, at] = roll(e, 1)
            east_ref[side, at] = roll(e, -1)

    levels = tops(thick_ref)
    table = depth_table(levels)
    group8 = lane_iota(8) // GROUP
    for tile in range(TILES):
        held = [jnp.zeros((8, LANES), F32) for _ in range(4)]
        for g in range(GROUPS):
            k = TILES * g + tile
            if k < KL:
                values = (mixing_ref[k, 0], mixing_ref[k, 1], thick_ref[k], levels[k])
            else:
                values = (0.0, 0.0, 0.0, levels[KL])
            held = [jnp.where(group8 == g, x, old) for x, old in zip(values, held)]
        for i in range(4):
            lanes_ref[tile, i] = held[i]
    for side in SIDES:
        for r0, n in CHUNKS:
            e = e_ref[side, pl.ds(PAD + r0, n)]
            face_ref[side, 0, pl.ds(r0, n)] = look_up(table, jnp.minimum(e, e_ref[side, pl.ds(PAD + r0 - 1, n)]))
            face_ref[side, 1, pl.ds(r0, n)] = look_up(table, jnp.minimum(e, west_ref[side, pl.ds(PAD + r0, n)]))
    pieces = [(tile, side) for tile in range(TILES) for side in SIDES]

    def stages(piece):
        tile, side = pieces[piece]
        slot = piece % 3
        level_of = group8 * TILES + tile
        mix = [lanes_ref[tile, c] for c in range(2)]
        thick = lanes_ref[tile, 2]
        begin = lanes_ref[tile, 3]

        def masked(r0, n):
            at = pl.ds(PAD + r0, n)
            wet = e_ref[side, at] > tall(level_of, n)
            for c in range(2):
                x = field(side, c, tile, r0, n)
                f_ref[slot, c, pl.ds(r0, n)] = x
                u_ref[c, at] = jnp.where(wet, x, 0.0)

        def first(r0, n):
            at = pl.ds(PAD + r0, n)
            wet = e_ref[side, at] > tall(level_of, n)
            number = jnp.where(e_ref[side, pl.ds(PAD + r0 - 1, n)] > tall(level_of, n), 1.0, 0.0)
            number += jnp.where(e_ref[side, pl.ds(PAD + r0 + 1, n)] > tall(level_of, n), 1.0, 0.0)
            number += jnp.where(west_ref[side, at] > tall(level_of, n), 1.0, 0.0)
            number += jnp.where(east_ref[side, at] > tall(level_of, n), 1.0, 0.0)
            n_ref[pl.ds(r0, n)] = number
            for c in range(2):
                x, around = neighbours(u_ref.at[c], r0, n)
                l_ref[c, at] = jnp.where(wet, around, 0.0) - number * x

        def density(r0, n):
            at = pl.ds(PAD + r0, n)
            wet = e_ref[side, at] > tall(level_of, n)
            number = n_ref[pl.ds(r0, n)]
            new = []
            for c in range(2):
                x, around = neighbours(l_ref.at[c], r0, n)
                second = jnp.where(wet, around, 0.0) - number * x
                new.append(f_ref[slot, c, pl.ds(r0, n)] - tall(mix[c], n) * second)
            rho_ref[at] = tall(thick, n) * (0.8 * new[1] - 0.2 * new[0])
            low, high = max(r0, HALO), min(r0 + n, HALO + ROWS)
            own = pl.ds(low - HALO, high - low)
            for c in range(2):
                value = new[c][low - r0 : high - r0]
                if side == 1:
                    value = jnp.where(first_half(high - low), value, new_ref[c, tile, own])
                new_ref[c, tile, own] = value

        def flux(r0, n):
            here = rho_ref[pl.ds(PAD + r0, n)]
            up = rho_ref[pl.ds(PAD + r0 - 1, n)]
            below_x = jnp.maximum(face_ref[side, 0, pl.ds(r0, n)] - tall(begin, n), 0.0)
            below_y = jnp.maximum(face_ref[side, 1, pl.ds(r0, n)] - tall(begin, n), 0.0)
            face_x = below_x * (here - up)
            face_y = below_y * (here - roll(here, 1))
            if tile > 0:
                face_x += fx_ref[side, pl.ds(PAD + r0, n)]
                face_y += fy_ref[side, pl.ds(r0, n)]
            fx_ref[side, pl.ds(PAD + r0, n)] = face_x
            fy_ref[side, pl.ds(r0, n)] = face_y

        return masked, first, density, flux

    for step in range(len(pieces) + 3):
        parts = [stages(step - late)[late] for late in (3, 2, 1, 0) if 0 <= step - late < len(pieces)]
        interleave(parts)

    halves = blocks(0, EXT, EXT // 2)
    for r0, n in halves:
        lane = lane_iota(n)
        at = pl.ds(PAD + r0, n)
        own = pl.ds(r0, n)
        sources = []
        for side in SIDES:
            fy = fy_ref[side, own]
            sources.append(fx_ref[side, at] - fx_ref[side, pl.ds(PAD + r0 + 1, n)] + (fy - roll(fy, -1)))
        for shift in (GROUP, 2 * GROUP, 4 * GROUP):
            sources = [x + roll(x, shift) for x in sources]
        west, east = (GRAVITY * roll(x, 8) for x in sources)
        v_ref[0, 0, at] = jnp.where(lane < 3, west, jnp.where(lane >= LANES - 3, east, source_ref[own]))
        v_ref[0, 1, at] = jnp.where(lane < 8, east, jnp.where(lane >= LANES - 8, west, 0.0))
    for r0, n in halves:
        lane = lane_iota(n)
        at = pl.ds(PAD + r0, n)
        west = roll(e_ref[0, at], 8)
        east = roll(e_ref[1, at], 8)
        beside = jnp.where(lane < 8, east, jnp.where(lane >= LANES - 8, west, 0))
        d_ref[0, at] = depth_in[pl.ds(r0, n)]
        d_ref[1, at] = look_up(table, beside)
    for r0, n in CHUNKS:
        here = pl.ds(PAD + r0, n)
        d_main, d_side = d_ref[0, here], d_ref[1, here]
        dl_ref[0, here], dl_ref[1, here] = lane_left(d_main, d_side)
        dr_ref[0, here], dr_ref[1, here] = lane_right(d_main, d_side)

    def weights(t, carry):
        for r0, n in CHUNKS:
            here = pl.ds(PAD + r0, n)
            above = pl.ds(PAD + r0 - 1, n)
            below = pl.ds(PAD + r0 + 1, n)
            d = d_ref[t, here]
            left, right = dl_ref[t, here], dr_ref[t, here]
            up, down = d_ref[t, above], d_ref[t, below]
            w_west, w_east = jnp.minimum(d, left), jnp.minimum(d, right)
            w_up, w_down = jnp.minimum(d, up), jnp.minimum(d, down)
            corners = (
                jnp.minimum(d, dl_ref[t, above])
                + jnp.minimum(d, dr_ref[t, below])
                + jnp.minimum(d, dr_ref[t, above])
                + jnp.minimum(d, dl_ref[t, below])
            )
            at = pl.ds(r0, n)
            w_ref[0, t, at] = 0.05 + w_up + w_down + w_west + w_east + 0.25 * corners
            w_ref[1, t, at] = w_west
            w_ref[2, t, at] = w_east
            w_ref[3, t, at] = w_down
            w_ref[4, t, at] = 0.25 * jnp.minimum(down, left)
            w_ref[5, t, at] = 0.25 * jnp.minimum(down, right)
            w_ref[6, t, at] = w_up
            w_ref[7, t, at] = 0.25 * jnp.minimum(up, left)
            w_ref[8, t, at] = 0.25 * jnp.minimum(up, right)
        return carry

    lax.fori_loop(0, 2, weights, 0)

    def power(step, carry):
        for r0, n in CHUNKS:
            here = pl.ds(PAD + r0, n)
            at = pl.ds(r0, n)
            v = (v_ref[step, 0, here], v_ref[step, 1, here])
            left = lane_left(*v)
            right = lane_right(*v)
            for t in range(2):
                w = [w_ref[m, t, at] for m in range(9)]
                p_ref[t, here] = w[3] * v[t] + w[4] * left[t] + w[5] * right[t]
                q_ref[t, here] = w[6] * v[t] + w[7] * left[t] + w[8] * right[t]
                v_ref[step + 1, t, here] = w[0] * v[t] - (w[1] * left[t] + w[2] * right[t])
        for r0, n in CHUNKS:
            here = pl.ds(PAD + r0, n)
            for t in range(2):
                beside = p_ref[t, pl.ds(PAD + r0 - 1, n)] + q_ref[t, pl.ds(PAD + r0 + 1, n)]
                v_ref[step + 1, t, here] -= beside
        return carry

    lax.fori_loop(0, 4, power, 0)

    for i in range(4):
        seen_ref[i] = v_ref[i, 0, pl.ds(PAD, SEEN)]
    depth_ref[...] = d_ref[0, pl.ds(PAD, SEEN)]
    for r0, n in blocks(HALO, HALO + ROWS, 128):
        lane = lane_iota(n)
        at = pl.ds(PAD + r0, n)
        beside = roll(d_ref[1, at], 5)
        for i in range(4):
            beside = jnp.where(lane == i, roll(v_ref[i, 1, at], i + 1), beside)
        beside_ref[pl.ds(r0 - HALO, n)] = beside

    def dots(step, carry):
        at = pl.ds(pl.multiple_of(PAD + HALO + 8 * step, 8), 8)
        v = [v_ref[i, 0, at] for i in range(5)]
        parts = [split(x) for x in v]
        out = []
        for m in range(MOMENTS):
            i, j = m // 2, (m + 1) // 2
            p, e = two_prod(v[i], v[j], parts[i], parts[j])
            s, f = two_sum(carry[2 * m], p)
            out += [s, carry[2 * m + 1] + (e + f)]
        return tuple(out)

    zero = jnp.zeros((8, LANES), F32)
    sums = lax.fori_loop(0, ROWS // 8, dots, (zero,) * (2 * MOMENTS), unroll=4)
    sub = lax.broadcasted_iota(I32, (8, LANES), 0)
    pairs = [(sums[2 * m], sums[2 * m + 1]) for m in range(MOMENTS)]
    for half in (4, 2, 1):
        merged = []
        for m in range(half):
            a, b = pairs[m], pairs[m + half]
            upper = (sub & half) == 0
            keep = tuple(jnp.where(upper, x, y) for x, y in zip(a, b))
            other = tuple(jnp.where(upper, pltpu.roll(x, 8 - half, 0), pltpu.roll(y, half, 0)) for x, y in zip(a, b))
            merged.append(loose_add(keep, other))
        pairs = merged
    wide = [jnp.concatenate([x, jnp.zeros((LANES - 8, LANES), F32)]).T for x in pairs[0]]
    rows = [tuple(x[at : at + 8] for x in wide) for at in range(0, LANES, 8)]
    while len(rows) > 1:
        rows = [loose_add(rows[i], rows[i + 1]) for i in range(0, len(rows), 2)]
    total = rows[0]
    for shift in (4, 2, 1):
        total = loose_add(total, tuple(pltpu.roll(x, shift, 0) for x in total))
    total = quick_sum(*total)
    row = total[0] + roll(total[1], MOMENTS)
    for at in range(0, sums_ref.shape[0], 8):
        sums_ref[pl.ds(at, 8)] = row


def finish_kernel(all_ref, seen_ref, beside_ref, depth_ref, surface_ref, flow_ref, s_ref):
    zero = jnp.zeros((8, LANES), F32)
    rows = [(all_ref[pl.ds(at, 8)], zero) for at in range(0, all_ref.shape[0], 8)]
    while len(rows) > 1:
        rows = [loose_add(rows[i], rows[i + 1]) for i in range(0, len(rows), 2)]
    total = rows[0]
    for shift in (4, 2, 1):
        total = loose_add(total, tuple(pltpu.roll(x, shift, 0) for x in total))
    total = pair_add(total, tuple(roll(x, -MOMENTS) for x in total))
    lane = lane_iota(8)

    def moment(m):
        return tuple(
            jnp.broadcast_to(jnp.sum(jnp.where(lane == m, x, 0.0), axis=1, keepdims=True), (8, LANES))
            for x in total
        )

    rho = [moment(m) for m in range(MOMENTS)]
    pi = list(rho)
    nought = (zero, zero)
    one = (zero + 1.0, zero)
    surface = [nought] * 4
    residual = [one] + [nought] * 3
    direction = list(residual)
    for step in range(4):
        alpha = pair_clip(pair_div(rho[step], pi[step + 1]), 20.0)
        for i in range(step + 1):
            surface[i] = pair_add(surface[i], pair_mul(alpha, direction[i]))
        if step == 3:
            break
        minus = pair_neg(alpha)
        new_rho = list(rho)
        for m in range(step + 1, MOMENTS - 1 - step):
            new_rho[m] = pair_add(rho[m], pair_mul(minus, pi[m + 1]))
        beta = pair_clip(pair_div(pair_mul(minus, new_rho[step + 1]), rho[step]), 400.0)
        for m in range(step + 2, MOMENTS - 1 - step):
            pi[m] = pair_add(new_rho[m], pair_mul(beta, pi[m]))
        rho = new_rho
        for i in range(step + 1, 0, -1):
            residual[i] = pair_add(residual[i], pair_mul(minus, direction[i - 1]))
        for i in range(step + 2):
            direction[i] = pair_add(residual[i], pair_mul(beta, direction[i]))
    weight = [s[0] for s in surface]
    lane = lane_iota(8)
    by_lane = zero
    for i in range(4):
        by_lane = jnp.where(lane == i, weight[i], by_lane)
    for r0, n in blocks(0, SEEN, 88):
        at = pl.ds(r0, n)
        total = tall(weight[0], n) * seen_ref[0, at]
        for i in range(1, 4):
            total = total + tall(weight[i], n) * seen_ref[i, at]
        s_ref[at] = total
    for r0, n in blocks(HALO, SEEN, 128):
        at = pl.ds(r0, n)
        above = pl.ds(r0 - 1, n)
        own = pl.ds(r0 - HALO, n)
        lane = lane_iota(n)
        s, d = s_ref[at], depth_ref[at]
        beside = beside_ref[own]
        d_west = jnp.where(lane == 0, roll(beside, -4), roll(d, 1))
        beside = tall(by_lane, n) * beside
        beside = beside + roll(beside, -1)
        west = jnp.where(lane == 0, beside + roll(beside, -2), roll(s, 1))
        surface_ref[own] = s
        flow_ref[0, own] = jnp.minimum(d, depth_ref[above]) * (s_ref[above] - s)
        flow_ref[1, own] = jnp.minimum(d, d_west) * (west - s)


VM = pl.BlockSpec(memory_space=pltpu.VMEM)
SM = pl.BlockSpec(memory_space=pltpu.SMEM)
HBM = pl.BlockSpec(memory_space=pltpu.HBM)


def params(limit):
    return pltpu.CompilerParams(vmem_limit_bytes=limit * MIB)


def cost(flops, moved):
    return pl.CostEstimate(flops=flops, bytes_accessed=moved, transcendentals=0)


def ring(x, axis, step):
    count = lax.axis_size(axis)
    return lax.ppermute(x, axis, [(i, (i + step) % count) for i in range(count)])


def shape(*sizes, dtype=F32):
    return jax.ShapeDtypeStruct(sizes, dtype)


def scratch(*lead, rows=BUF, dtype=F32):
    return pltpu.VMEM(lead + (rows, LANES), dtype)


def shards(tracers, mixing, thickness, levels, land):
    devices = lax.axis_size("bx") * lax.axis_size("by")
    planes = 2 * KL
    wet = wet_levels(levels, land).astype(F32)
    flat = tracers.reshape(planes, ROWS, LANES)
    with jax.named_scope("rows"):
        to_up = jnp.concatenate([flat[:, :HALO], wet[None, :HALO]])
        to_down = jnp.concatenate([flat[:, -HALO:], wet[None, -HALO:]])
        top = ring(to_down, "bx", 1)
        bottom = ring(to_up, "bx", -1)
    with jax.named_scope("columns"):
        edges = (shape(2, TILES, EXT, LANES), shape(TILES, EXT, LANES), shape(TILES, EXT, LANES))
        own = pl.pallas_call(
            own_edges_kernel,
            out_shape=edges,
            in_specs=[HBM, VM],
            out_specs=(VM,) * 3,
            scratch_shapes=[scratch(planes, rows=ROWS), pltpu.SemaphoreType.DMA((LOADS,))],
            compiler_params=params(48),
            cost_estimate=cost(10_000_000, 7_000_000),
        )(flat, wet)
        edge, to_right, to_left = pl.pallas_call(
            halo_edges_kernel,
            out_shape=edges,
            in_specs=[VM] * 5,
            out_specs=(VM,) * 3,
            input_output_aliases={i + 2: i for i in range(3)},
            compiler_params=params(16),
            cost_estimate=cost(1_000_000, 700_000),
        )(top, bottom, *own)
        from_left = ring(to_right, "by", 1)
        from_right = ring(to_left, "by", -1)
    with jax.named_scope("block"):
        new, source, depth = pl.pallas_call(
            block_kernel,
            out_shape=(shape(planes, ROWS, LANES), shape(EXT, LANES), shape(EXT, LANES)),
            in_specs=[SM, SM, HBM, VM, VM, VM],
            out_specs=(HBM, VM, VM),
            scratch_shapes=[
                scratch(planes, rows=EXT),
                scratch(dtype=I32),
                scratch(2, rows=EXT),
                scratch(3, rows=EXT, dtype=I32),
                scratch(2),
                scratch(2),
                scratch(rows=EXT),
                scratch(),
                scratch(),
                scratch(),
                pltpu.SMEM((KL,), F32),
                pltpu.SemaphoreType.DMA((KL,)),
                pltpu.SemaphoreType.DMA((KL,)),
            ],
            compiler_params=params(48),
            cost_estimate=cost(50_000_000, 12_000_000),
        )(mixing, thickness, flat, top, bottom, wet)
    with jax.named_scope("powers"):
        seen, beside, near_depth, sums, new_edge = pl.pallas_call(
            solve_kernel,
            out_shape=(
                shape(4, SEEN, LANES),
                shape(ROWS, LANES),
                shape(SEEN, LANES),
                shape(devices, LANES),
                shape(2, TILES, ROWS, LANES),
            ),
            in_specs=[SM, SM] + [VM] * 5,
            out_specs=(VM,) * 5,
            scratch_shapes=[
                scratch(5, 2),
                scratch(2),
                scratch(2, dtype=I32),
                scratch(2, dtype=I32),
                scratch(2, dtype=I32),
                scratch(3, 2, rows=EXT),
                scratch(2),
                scratch(2),
                scratch(rows=EXT),
                scratch(),
                scratch(2),
                scratch(2, rows=EXT),
                scratch(2, 2, rows=EXT),
                scratch(TILES, 4, rows=8),
                scratch(2),
                scratch(2),
                scratch(9, 2, rows=EXT),
                scratch(2),
                scratch(2),
            ],
            compiler_params=params(20),
            cost_estimate=cost(50_000_000, 6_000_000),
        )(mixing, thickness, source, depth, from_left, from_right, edge)
    with jax.named_scope("sums"):
        everyone = lax.all_to_all(sums, ("bx", "by"), 0, 0, tiled=True)
    with jax.named_scope("patch"):
        tracers_new = pl.pallas_call(
            patch_kernel,
            out_shape=shape(planes, ROWS, LANES),
            in_specs=[HBM, VM],
            out_specs=HBM,
            scratch_shapes=[
                scratch(planes, rows=ROWS),
                pltpu.SemaphoreType.DMA((KL // PATCH,)),
                pltpu.SemaphoreType.DMA((KL // PATCH,)),
            ],
            compiler_params=params(48),
            cost_estimate=cost(10_000_000, 12_000_000),
        )(new, new_edge)
    with jax.named_scope("surface"):
        surface, transports = pl.pallas_call(
            finish_kernel,
            out_shape=(shape(ROWS, LANES), shape(2, ROWS, LANES)),
            in_specs=[VM] * 4,
            out_specs=(VM, VM),
            scratch_shapes=[scratch(rows=SEEN)],
            compiler_params=params(8),
            cost_estimate=cost(1_000_000, 3_000_000),
        )(everyone, seen, beside, near_depth)
    return tracers_new.reshape(tracers.shape), surface, transports


def solution(mesh):
    in_specs = (P(None, None, "bx", "by"), P(), P(), P("bx", "by"), P("bx", "by"))
    out_specs = (P(None, None, "bx", "by"), P("bx", "by"), P(None, "bx", "by"))
    return jax.shard_map(shards, mesh=mesh, in_specs=in_specs, out_specs=out_specs, check_vma=False)
```

```python
import jax
import jax.numpy as jnp
from jax import lax
from jax.experimental import pallas as pl
from jax.experimental.pallas import tpu as pltpu
from jax.sharding import PartitionSpec as P

KL = 22
ROWS = 256
LANES = 128
HALO = 8
EXT = ROWS + 2 * HALO
PAD = 8
BUF = EXT + 2 * PAD
GROUP = 16
GROUPS = LANES // GROUP
TILES = 3
LOADS = 4
MOMENTS = 8
GRAVITY = 10.0
SEEN = HALO + ROWS
F32 = jnp.float32
I32 = jnp.int32
MIB = 1024 * 1024


def lane_iota(rows):
    return lax.broadcasted_iota(I32, (rows, LANES), 1)


def first_half(rows):
    return (lane_iota(rows) & 8) == 0


def tall(x, n):
    return jnp.concatenate([x] * (n // 8)) if n > 8 else x


def roll(x, shift):
    return pltpu.roll(x, shift % LANES, 1)


def blocks(start, stop, size):
    out = []
    while start < stop:
        out.append((start, min(size, stop - start)))
        start += size
    return out


CHUNKS = blocks(0, EXT, 32)
OWN_CHUNKS = blocks(HALO, HALO + ROWS, 32)


def interleave(parts):
    for turn in range(len(CHUNKS) + len(parts) - 1):
        for late, part in enumerate(parts):
            if 0 <= turn - late < len(CHUNKS):
                part(*CHUNKS[turn - late])


def wet_levels(levels, land):
    return jnp.where(land == 0, levels, 0)


def tops(thick_ref):
    out = [jnp.float32(0.0)]
    for k in range(KL):
        out.append(out[-1] + thick_ref[k])
    return out


def depth_table(levels):
    table = jnp.zeros((8, LANES), F32)
    for k, top in enumerate(levels):
        table = jnp.where(lane_iota(8) == k, top, table)
    return table


def look_up(table, index):
    rows = [jnp.take_along_axis(table, index[i : i + 8], axis=1) for i in range(0, index.shape[0], 8)]
    return jnp.concatenate(rows) if len(rows) > 1 else rows[0]


def edge_slot(k):
    return k % TILES, k // TILES


def place(x, k, old):
    _, g = edge_slot(k)
    return jnp.where(lane_iota(x.shape[0]) // GROUP == g, roll(x, 8 + GROUP * g), old)


def to_neighbours(a, b):
    first = first_half(a.shape[0])
    return jnp.where(first, a, roll(b, 8)), jnp.where(first, roll(b, -8), a)


def own_edges_kernel(t_ref, wet_ref, edge_ref, right_ref, left_ref, own_ref, sems):
    parts = blocks(0, KL, -(-KL // LOADS))

    def copy(i):
        start, count = parts[i]
        planes = pl.ds(2 * start, 2 * count)
        return pltpu.make_async_copy(t_ref.at[planes], own_ref.at[planes], sems.at[i])

    for i in range(len(parts)):
        copy(i).start()
    size = ROWS
    tile_eff, _ = edge_slot(KL)

    def rows_of(step):
        own = pl.ds(pl.multiple_of(size * step, 8), size)
        return own, pl.ds(pl.multiple_of(HALO + size * step, 8), size)

    def clear(step, carry):
        own, at = rows_of(step)
        zero = jnp.zeros((size, LANES), F32)
        for c in range(2):
            for tile in range(TILES):
                edge_ref[c, tile, at] = zero
            edge_ref[c, tile_eff, at] = place(wet_ref[own], KL, zero)
        return carry

    lax.fori_loop(0, ROWS // size, clear, 0)
    for i, (start, count) in enumerate(parts):
        copy(i).wait()

        def rows(step, carry):
            own, at = rows_of(step)
            for k in range(start, start + count):
                tile, _ = edge_slot(k)
                for c in range(2):
                    edge_ref[c, tile, at] = place(own_ref[2 * k + c, own], k, edge_ref[c, tile, at])
            return carry

        lax.fori_loop(0, ROWS // size, rows, 0)

    def send(step, carry):
        _, at = rows_of(step)
        for tile in range(TILES):
            right_ref[tile, at], left_ref[tile, at] = to_neighbours(edge_ref[0, tile, at], edge_ref[1, tile, at])
        return carry

    lax.fori_loop(0, ROWS // size, send, 0)


def halo_edges_kernel(top_ref, bottom_ref, edge_in, right_in, left_in, edge_ref, right_ref, left_ref, near_ref):
    after = lax.broadcasted_iota(I32, (HALO, LANES), 0) < HALO // 2
    for i in range(2 * KL + 1):
        near_ref[i] = jnp.where(after, bottom_ref[i], top_ref[i])
    for r0, ref in ((0, top_ref), (HALO + ROWS, bottom_ref)):
        at = pl.ds(r0, HALO)
        held = [[jnp.zeros((HALO, LANES), F32) for _ in range(TILES)] for _ in range(2)]
        for k in range(KL + 1):
            tile, _ = edge_slot(k)
            for c in range(2):
                x = ref[2 * k + c] if k < KL else ref[2 * KL]
                held[c][tile] = place(x, k, held[c][tile])
        for tile in range(TILES):
            for c in range(2):
                edge_ref[c, tile, at] = held[c][tile]
            right_ref[tile, at], left_ref[tile, at] = to_neighbours(held[0][tile], held[1][tile])


def count_word(effs, word):
    total = None
    for eff in effs:
        bits = jnp.clip(eff - 10 * word, 0, 10) * 3
        mask = (lax.shift_left(jnp.full_like(bits, 1), bits) - 1) & 0o1111111111
        total = mask if total is None else total + mask
    return total


def neighbours(ref, r0, n):
    x = ref[pl.ds(PAD + r0, n)]
    around = ref[pl.ds(PAD + r0 - 1, n)] + ref[pl.ds(PAD + r0 + 1, n)]
    return x, around + (roll(x, 1) + roll(x, -1))


def wet_count(word_ref, k, r0, n):
    words = word_ref[k // 10, pl.ds(r0, n)]
    shift = jnp.full((n, LANES), 3 * (k % 10), I32)
    return (lax.shift_right_logical(words, shift) & 7).astype(F32)


def level_copies(t_ref, out_ref, ext_ref, in_sems, out_sems):
    def held(k):
        return ext_ref.at[pl.ds(2 * k, 2), pl.ds(HALO, ROWS)]

    def load(k):
        return pltpu.make_async_copy(t_ref.at[pl.ds(2 * k, 2)], held(k), in_sems.at[k])

    def store(k):
        return pltpu.make_async_copy(held(k), out_ref.at[pl.ds(2 * k, 2)], out_sems.at[k])

    def each(body):
        def step(k, carry):
            body(k)
            return carry

        lax.fori_loop(0, KL, step, 0)

    return load, store, each


def block_kernel(
    mixing_ref,
    thick_ref,
    t_ref,
    top_ref,
    bottom_ref,
    wet_ref,
    source_ref,
    depth_ref,
    ext_ref,
    eff_ref,
    face_ref,
    word_ref,
    u_ref,
    l_ref,
    n_ref,
    rho_ref,
    fx_ref,
    fy_ref,
    begin_ref,
    in_sems,
):
    load, _, each = level_copies(t_ref, None, ext_ref, in_sems, None)
    each(lambda k: load(k).start())
    eff_ref[pl.ds(PAD, HALO)] = top_ref[2 * KL].astype(I32)
    eff_ref[pl.ds(PAD + HALO, ROWS)] = wet_ref[...].astype(I32)
    eff_ref[pl.ds(PAD + HALO + ROWS, HALO)] = bottom_ref[2 * KL].astype(I32)
    ext_ref[:, pl.ds(0, HALO)] = top_ref[pl.ds(0, 2 * KL)]
    ext_ref[:, pl.ds(HALO + ROWS, HALO)] = bottom_ref[pl.ds(0, 2 * KL)]
    for ref in (u_ref, l_ref, rho_ref, fx_ref, fy_ref):
        ref[...] = jnp.zeros(ref.shape, F32)
    levels = tops(thick_ref)
    table = depth_table(levels)
    for k in range(KL):
        begin_ref[k] = levels[k]
    for r0, n in CHUNKS:
        e = eff_ref[pl.ds(PAD + r0, n)]
        up = eff_ref[pl.ds(PAD + r0 - 1, n)]
        west = roll(e, 1)
        depth_ref[pl.ds(r0, n)] = look_up(table, e)
        face_ref[0, pl.ds(r0, n)] = look_up(table, jnp.minimum(e, up))
        face_ref[1, pl.ds(r0, n)] = look_up(table, jnp.minimum(e, west))
        effs = (up, eff_ref[pl.ds(PAD + r0 + 1, n)], west, roll(e, -1))
        for word in range(3):
            word_ref[word, pl.ds(r0, n)] = count_word(effs, word)

    def body(step, stages):
        if 0 in stages:
            load(step).wait()
        ku, kl, kd, kf = (step - late for late in range(4))

        def flux(r0, n):
            here = rho_ref[pl.ds(PAD + r0, n)]
            up = rho_ref[pl.ds(PAD + r0 - 1, n)]
            below_x = jnp.maximum(face_ref[0, pl.ds(r0, n)] - begin_ref[kf], 0.0)
            below_y = jnp.maximum(face_ref[1, pl.ds(r0, n)] - begin_ref[kf], 0.0)
            fx_ref[pl.ds(PAD + r0, n)] += below_x * (here - up)
            fy_ref[pl.ds(PAD + r0, n)] += below_y * (here - roll(here, 1))

        def density(r0, n):
            wet = eff_ref[pl.ds(PAD + r0, n)] > kd
            x, around = neighbours(l_ref, r0, n)
            second = jnp.where(wet, around, 0.0) - n_ref[pl.ds(r0, n)] * x
            a, b = (ext_ref[2 * kd + c, pl.ds(r0, n)] for c in range(2))
            rho_ref[pl.ds(PAD + r0, n)] = thick_ref[kd] * ((0.8 * b - 0.2 * a) - second)

        def first(r0, n):
            wet = eff_ref[pl.ds(PAD + r0, n)] > kl
            number = wet_count(word_ref, kl, r0, n)
            n_ref[pl.ds(r0, n)] = number
            x, around = neighbours(u_ref, r0, n)
            l_ref[pl.ds(PAD + r0, n)] = jnp.where(wet, around, 0.0) - number * x

        def masked(r0, n):
            wet = eff_ref[pl.ds(PAD + r0, n)] > ku
            a, b = (ext_ref[2 * ku + c, pl.ds(r0, n)] for c in range(2))
            mixed = (0.8 * mixing_ref[ku, 1]) * b - (0.2 * mixing_ref[ku, 0]) * a
            u_ref[pl.ds(PAD + r0, n)] = jnp.where(wet, mixed, 0.0)

        work = ((3, flux), (2, density), (1, first), (0, masked))
        interleave([part for late, part in work if late in stages])

    def all_stages(step, carry):
        body(step, range(4))
        return carry

    for step in range(3):
        body(step, range(step + 1))
    lax.fori_loop(3, KL, all_stages, 0)
    for step in range(KL, KL + 3):
        body(step, range(step - KL + 1, 4))
    for r0, n in CHUNKS:
        fx = fx_ref[pl.ds(PAD + r0, n)] - fx_ref[pl.ds(PAD + r0 + 1, n)]
        fy = fy_ref[pl.ds(PAD + r0, n)]
        source_ref[pl.ds(r0, n)] = GRAVITY * (fx + (fy - roll(fy, -1)))


def tracer_kernel(
    mixing_ref,
    t_ref,
    near_ref,
    wet_ref,
    edge_ref,
    out_ref,
    ext_ref,
    eff_ref,
    word_ref,
    u_ref,
    l_ref,
    n_ref,
    in_sems,
    out_sems,
):
    load, store, each = level_copies(t_ref, out_ref, ext_ref, in_sems, out_sems)
    each(lambda k: load(k).start())
    eff_ref[...] = jnp.zeros(eff_ref.shape, I32)
    eff_ref[pl.ds(PAD, HALO)] = near_ref[2 * KL].astype(I32)
    eff_ref[pl.ds(PAD + HALO, ROWS)] = wet_ref[...].astype(I32)
    eff_ref[pl.ds(PAD + HALO + ROWS, HALO)] = near_ref[2 * KL].astype(I32)
    ext_ref[:, pl.ds(0, HALO)] = near_ref[pl.ds(0, 2 * KL)]
    ext_ref[:, pl.ds(HALO + ROWS, HALO)] = near_ref[pl.ds(0, 2 * KL)]
    for ref in (u_ref, l_ref):
        ref[...] = jnp.zeros(ref.shape, F32)
    for r0, n in CHUNKS:
        e = eff_ref[pl.ds(PAD + r0, n)]
        effs = (eff_ref[pl.ds(PAD + r0 - 1, n)], eff_ref[pl.ds(PAD + r0 + 1, n)], roll(e, 1), roll(e, -1))
        for word in range(3):
            word_ref[word, pl.ds(r0, n)] = count_word(effs, word)

    def body(step, stages, ready):
        if 0 in stages:
            load(step).wait()
        if ready:
            store(step - 3).start()
        ku, kl, kd = (step - late for late in range(3))
        tile = kd % TILES
        back = (2 * LANES - 8 - GROUP * (kd // TILES)) % LANES

        def second(r0, n):
            low, high = max(r0, HALO), min(r0 + n, HALO + ROWS)
            size = high - low
            lane = lane_iota(size)
            middle = jnp.logical_and(lane >= 4, lane < LANES - 4)
            wet = eff_ref[pl.ds(PAD + low, size)] > kd
            number = n_ref[pl.ds(low, size)]
            for c in range(2):
                x, around = neighbours(l_ref.at[c], low, size)
                twice = jnp.where(wet, around, 0.0) - number * x
                value = ext_ref[2 * kd + c, pl.ds(low, size)] - mixing_ref[kd, c] * twice
                edge = pltpu.roll(edge_ref[c, tile, pl.ds(low - HALO, size)], back, 1)
                ext_ref[2 * kd + c, pl.ds(low, size)] = jnp.where(middle, value, edge)

        def first(r0, n):
            wet = eff_ref[pl.ds(PAD + r0, n)] > kl
            number = wet_count(word_ref, kl, r0, n)
            n_ref[pl.ds(r0, n)] = number
            for c in range(2):
                x, around = neighbours(u_ref.at[c], r0, n)
                l_ref[c, pl.ds(PAD + r0, n)] = jnp.where(wet, around, 0.0) - number * x

        def masked(r0, n):
            wet = eff_ref[pl.ds(PAD + r0, n)] > ku
            for c in range(2):
                u_ref[c, pl.ds(PAD + r0, n)] = jnp.where(wet, ext_ref[2 * ku + c, pl.ds(r0, n)], 0.0)

        work = ((2, second), (1, first), (0, masked))
        interleave([part for late, part in work if late in stages])

    def all_stages(step, carry):
        body(step, range(3), True)
        return carry

    for step in range(3):
        body(step, range(step + 1), False)
    lax.fori_loop(3, KL, all_stages, 0)
    for step in range(KL, KL + 2):
        body(step, range(step - KL + 1, 3), True)
    store(KL - 1).start()
    each(lambda k: store(k).wait())


def two_sum(a, b):
    s = a + b
    v = s - a
    return s, (a - (s - v)) + (b - v)


def quick_sum(a, b):
    s = a + b
    return s, b - (s - a)


def split(a):
    t = a * 4097.0
    high = t - (t - a)
    return high, a - high


def two_prod(a, b, parts_a, parts_b):
    p = a * b
    ah, al = parts_a
    bh, bl = parts_b
    return p, ((ah * bh - p) + ah * bl + al * bh) + al * bl


def pair_add(x, y):
    s, e = two_sum(x[0], y[0])
    return quick_sum(s, e + (x[1] + y[1]))


def loose_add(x, y):
    s, e = two_sum(x[0], y[0])
    return s, e + (x[1] + y[1])


def pair_mul(x, y):
    p, e = two_prod(x[0], y[0], split(x[0]), split(y[0]))
    return quick_sum(p, e + (x[0] * y[1] + x[1] * y[0]))


def pair_neg(x):
    return -x[0], -x[1]


def pair_div(x, y):
    q = x[0] / y[0]
    rest = pair_add(x, pair_neg(pair_mul(y, (q, jnp.zeros_like(q)))))
    return quick_sum(q, rest[0] / y[0])


def pair_clip(x, top):
    inside = jnp.logical_and(x[0] >= 0.0, x[0] <= top)
    high = jnp.where(inside, x[0], jnp.where(x[0] > top, top, 0.0))
    return high, jnp.where(inside, x[1], 0.0)


def group_totals(x):
    x = x + roll(x, GROUP)
    x = x + roll(x, 2 * GROUP)
    return x + roll(x, 4 * GROUP)


def lane_left(main, side):
    lane = lane_iota(main.shape[0])
    a, b = roll(main, 1), roll(side, 1)
    return jnp.where(lane == 0, b, a), jnp.where(lane == 0, a, b)


def lane_right(main, side):
    lane = lane_iota(main.shape[0])
    a, b = roll(main, -1), roll(side, -1)
    return jnp.where(lane == LANES - 1, b, a), jnp.where(lane == LANES - 1, a, b)


SIDES = (0, 1)


def solve_kernel(
    mixing_ref,
    thick_ref,
    source_ref,
    depth_in,
    from_left_ref,
    from_right_ref,
    edge_ref,
    seen_ref,
    beside_ref,
    sums_ref,
    new_ref,
    v_ref,
    d_ref,
    e_ref,
    west_ref,
    east_ref,
    f_ref,
    u_ref,
    l_ref,
    n_ref,
    rho_ref,
    fx_ref,
    fy_ref,
    face_ref,
    lanes_ref,
    dl_ref,
    dr_ref,
    w_ref,
    p_ref,
    q_ref,
):
    by = lax.axis_index("by")
    open_side = (by != 0, by != lax.axis_size("by") - 1)

    def clear(ref):
        ref[...] = jnp.zeros(ref.shape, ref.dtype)

    for ref in (e_ref, west_ref, east_ref):
        clear(ref)
    for ref in (u_ref, l_ref, rho_ref, d_ref, v_ref, dl_ref, dr_ref, p_ref, q_ref, fx_ref):
        rank = len(ref.shape) - 2
        lead = [()]
        for size in ref.shape[:rank]:
            lead = [i + (j,) for i in lead for j in range(size)]
        for i in lead:
            for r0 in (0, BUF - PAD):
                ref[i + (pl.ds(r0, PAD),)] = jnp.zeros((PAD, LANES), F32)

    def field(side, c, tile, r0, n):
        own = edge_ref[c, tile, pl.ds(r0, n)]
        first = first_half(n)
        if side == 0:
            far = from_left_ref[tile, pl.ds(r0, n)]
            return jnp.where(first, roll(far, -8) if c else far, own)
        far = from_right_ref[tile, pl.ds(r0, n)]
        return jnp.where(first, own, roll(far, 8) if c else far)

    tile_eff, slot = edge_slot(KL)
    for side in SIDES:
        for r0, n in CHUNKS:
            lane = lane_iota(n)
            x = field(side, 0, tile_eff, r0, n)
            inner = (lane & 8) == (8 if side == 0 else 0)
            keep = jnp.logical_and(lane // GROUP == slot, jnp.logical_or(inner, open_side[side]))
            e = group_totals(jnp.where(keep, x, 0.0)).astype(I32)
            at = pl.ds(PAD + r0, n)
            e_ref[side, at] = e
            west_ref[side, at] = roll(e, 1)
            east_ref[side, at] = roll(e, -1)

    levels = tops(thick_ref)
    table = depth_table(levels)
    group8 = lane_iota(8) // GROUP
    for tile in range(TILES):
        held = [jnp.zeros((8, LANES), F32) for _ in range(4)]
        for g in range(GROUPS):
            k = TILES * g + tile
            if k < KL:
                values = (mixing_ref[k, 0], mixing_ref[k, 1], thick_ref[k], levels[k])
            else:
                values = (0.0, 0.0, 0.0, levels[KL])
            held = [jnp.where(group8 == g, x, old) for x, old in zip(values, held)]
        for i in range(4):
            lanes_ref[tile, i] = held[i]
    for side in SIDES:
        for r0, n in CHUNKS:
            e = e_ref[side, pl.ds(PAD + r0, n)]
            face_ref[side, 0, pl.ds(r0, n)] = look_up(table, jnp.minimum(e, e_ref[side, pl.ds(PAD + r0 - 1, n)]))
            face_ref[side, 1, pl.ds(r0, n)] = look_up(table, jnp.minimum(e, west_ref[side, pl.ds(PAD + r0, n)]))
    pieces = [(tile, side) for tile in range(TILES) for side in SIDES]

    def stages(piece):
        tile, side = pieces[piece]
        slot = piece % 3
        level_of = group8 * TILES + tile
        mix = [lanes_ref[tile, c] for c in range(2)]
        thick = lanes_ref[tile, 2]
        begin = lanes_ref[tile, 3]

        def masked(r0, n):
            at = pl.ds(PAD + r0, n)
            wet = e_ref[side, at] > tall(level_of, n)
            for c in range(2):
                x = field(side, c, tile, r0, n)
                f_ref[slot, c, pl.ds(r0, n)] = x
                u_ref[c, at] = jnp.where(wet, x, 0.0)

        def first(r0, n):
            at = pl.ds(PAD + r0, n)
            wet = e_ref[side, at] > tall(level_of, n)
            number = jnp.where(e_ref[side, pl.ds(PAD + r0 - 1, n)] > tall(level_of, n), 1.0, 0.0)
            number += jnp.where(e_ref[side, pl.ds(PAD + r0 + 1, n)] > tall(level_of, n), 1.0, 0.0)
            number += jnp.where(west_ref[side, at] > tall(level_of, n), 1.0, 0.0)
            number += jnp.where(east_ref[side, at] > tall(level_of, n), 1.0, 0.0)
            n_ref[pl.ds(r0, n)] = number
            for c in range(2):
                x, around = neighbours(u_ref.at[c], r0, n)
                l_ref[c, at] = jnp.where(wet, around, 0.0) - number * x

        def density(r0, n):
            at = pl.ds(PAD + r0, n)
            wet = e_ref[side, at] > tall(level_of, n)
            number = n_ref[pl.ds(r0, n)]
            new = []
            for c in range(2):
                x, around = neighbours(l_ref.at[c], r0, n)
                second = jnp.where(wet, around, 0.0) - number * x
                new.append(f_ref[slot, c, pl.ds(r0, n)] - tall(mix[c], n) * second)
            rho_ref[at] = tall(thick, n) * (0.8 * new[1] - 0.2 * new[0])
            low, high = max(r0, HALO), min(r0 + n, HALO + ROWS)
            own = pl.ds(low - HALO, high - low)
            for c in range(2):
                value = new[c][low - r0 : high - r0]
                if side == 1:
                    value = jnp.where(first_half(high - low), value, new_ref[c, tile, own])
                new_ref[c, tile, own] = value

        def flux(r0, n):
            here = rho_ref[pl.ds(PAD + r0, n)]
            up = rho_ref[pl.ds(PAD + r0 - 1, n)]
            below_x = jnp.maximum(face_ref[side, 0, pl.ds(r0, n)] - tall(begin, n), 0.0)
            below_y = jnp.maximum(face_ref[side, 1, pl.ds(r0, n)] - tall(begin, n), 0.0)
            face_x = below_x * (here - up)
            face_y = below_y * (here - roll(here, 1))
            if tile > 0:
                face_x += fx_ref[side, pl.ds(PAD + r0, n)]
                face_y += fy_ref[side, pl.ds(r0, n)]
            fx_ref[side, pl.ds(PAD + r0, n)] = face_x
            fy_ref[side, pl.ds(r0, n)] = face_y

        return masked, first, density, flux

    for step in range(len(pieces) + 3):
        parts = [stages(step - late)[late] for late in (3, 2, 1, 0) if 0 <= step - late < len(pieces)]
        interleave(parts)

    halves = blocks(0, EXT, EXT // 2)
    for r0, n in halves:
        lane = lane_iota(n)
        at = pl.ds(PAD + r0, n)
        own = pl.ds(r0, n)
        sources = []
        for side in SIDES:
            fy = fy_ref[side, own]
            sources.append(fx_ref[side, at] - fx_ref[side, pl.ds(PAD + r0 + 1, n)] + (fy - roll(fy, -1)))
        for shift in (GROUP, 2 * GROUP, 4 * GROUP):
            sources = [x + roll(x, shift) for x in sources]
        west, east = (GRAVITY * roll(x, 8) for x in sources)
        v_ref[0, 0, at] = jnp.where(lane < 3, west, jnp.where(lane >= LANES - 3, east, source_ref[own]))
        v_ref[0, 1, at] = jnp.where(lane < 8, east, jnp.where(lane >= LANES - 8, west, 0.0))
    for r0, n in halves:
        lane = lane_iota(n)
        at = pl.ds(PAD + r0, n)
        west = roll(e_ref[0, at], 8)
        east = roll(e_ref[1, at], 8)
        beside = jnp.where(lane < 8, east, jnp.where(lane >= LANES - 8, west, 0))
        d_ref[0, at] = depth_in[pl.ds(r0, n)]
        d_ref[1, at] = look_up(table, beside)
    for r0, n in CHUNKS:
        here = pl.ds(PAD + r0, n)
        d_main, d_side = d_ref[0, here], d_ref[1, here]
        dl_ref[0, here], dl_ref[1, here] = lane_left(d_main, d_side)
        dr_ref[0, here], dr_ref[1, here] = lane_right(d_main, d_side)

    def weights(t, carry):
        for r0, n in CHUNKS:
            here = pl.ds(PAD + r0, n)
            above = pl.ds(PAD + r0 - 1, n)
            below = pl.ds(PAD + r0 + 1, n)
            d = d_ref[t, here]
            left, right = dl_ref[t, here], dr_ref[t, here]
            up, down = d_ref[t, above], d_ref[t, below]
            w_west, w_east = jnp.minimum(d, left), jnp.minimum(d, right)
            w_up, w_down = jnp.minimum(d, up), jnp.minimum(d, down)
            corners = (
                jnp.minimum(d, dl_ref[t, above])
                + jnp.minimum(d, dr_ref[t, below])
                + jnp.minimum(d, dr_ref[t, above])
                + jnp.minimum(d, dl_ref[t, below])
            )
            at = pl.ds(r0, n)
            w_ref[0, t, at] = 0.05 + w_up + w_down + w_west + w_east + 0.25 * corners
            w_ref[1, t, at] = w_west
            w_ref[2, t, at] = w_east
            w_ref[3, t, at] = w_down
            w_ref[4, t, at] = 0.25 * jnp.minimum(down, left)
            w_ref[5, t, at] = 0.25 * jnp.minimum(down, right)
            w_ref[6, t, at] = w_up
            w_ref[7, t, at] = 0.25 * jnp.minimum(up, left)
            w_ref[8, t, at] = 0.25 * jnp.minimum(up, right)
        return carry

    lax.fori_loop(0, 2, weights, 0)

    def power(step, carry):
        for r0, n in CHUNKS:
            here = pl.ds(PAD + r0, n)
            at = pl.ds(r0, n)
            v = (v_ref[step, 0, here], v_ref[step, 1, here])
            left = lane_left(*v)
            right = lane_right(*v)
            for t in range(2):
                w = [w_ref[m, t, at] for m in range(9)]
                p_ref[t, here] = w[3] * v[t] + w[4] * left[t] + w[5] * right[t]
                q_ref[t, here] = w[6] * v[t] + w[7] * left[t] + w[8] * right[t]
                v_ref[step + 1, t, here] = w[0] * v[t] - (w[1] * left[t] + w[2] * right[t])
        for r0, n in CHUNKS:
            here = pl.ds(PAD + r0, n)
            for t in range(2):
                beside = p_ref[t, pl.ds(PAD + r0 - 1, n)] + q_ref[t, pl.ds(PAD + r0 + 1, n)]
                v_ref[step + 1, t, here] -= beside
        return carry

    lax.fori_loop(0, 4, power, 0)

    for i in range(4):
        seen_ref[i] = v_ref[i, 0, pl.ds(PAD, SEEN)]
    for r0, n in blocks(HALO, HALO + ROWS, 128):
        lane = lane_iota(n)
        at = pl.ds(PAD + r0, n)
        beside = roll(d_ref[1, at], 5)
        for i in range(4):
            beside = jnp.where(lane == i, roll(v_ref[i, 1, at], i + 1), beside)
        beside_ref[pl.ds(r0 - HALO, n)] = beside

    def dots(step, carry):
        at = pl.ds(pl.multiple_of(PAD + HALO + 8 * step, 8), 8)
        v = [v_ref[i, 0, at] for i in range(5)]
        parts = [split(x) for x in v]
        out = []
        for m in range(MOMENTS):
            i, j = m // 2, (m + 1) // 2
            p, e = two_prod(v[i], v[j], parts[i], parts[j])
            s, f = two_sum(carry[2 * m], p)
            out += [s, carry[2 * m + 1] + (e + f)]
        return tuple(out)

    zero = jnp.zeros((8, LANES), F32)
    sums = lax.fori_loop(0, ROWS // 8, dots, (zero,) * (2 * MOMENTS), unroll=4)
    sub = lax.broadcasted_iota(I32, (8, LANES), 0)
    pairs = [(sums[2 * m], sums[2 * m + 1]) for m in range(MOMENTS)]
    for half in (4, 2, 1):
        merged = []
        for m in range(half):
            a, b = pairs[m], pairs[m + half]
            upper = (sub & half) == 0
            keep = tuple(jnp.where(upper, x, y) for x, y in zip(a, b))
            other = tuple(jnp.where(upper, pltpu.roll(x, 8 - half, 0), pltpu.roll(y, half, 0)) for x, y in zip(a, b))
            merged.append(loose_add(keep, other))
        pairs = merged
    wide = [jnp.concatenate([x, jnp.zeros((LANES - 8, LANES), F32)]).T for x in pairs[0]]
    rows = [tuple(x[at : at + 8] for x in wide) for at in range(0, LANES, 8)]
    while len(rows) > 1:
        rows = [loose_add(rows[i], rows[i + 1]) for i in range(0, len(rows), 2)]
    total = rows[0]
    for shift in (4, 2, 1):
        total = loose_add(total, tuple(pltpu.roll(x, shift, 0) for x in total))
    total = quick_sum(*total)
    row = total[0] + roll(total[1], MOMENTS)
    for at in range(0, sums_ref.shape[0], 8):
        sums_ref[pl.ds(at, 8)] = row


def finish_kernel(thick_ref, all_ref, seen_ref, beside_ref, near_ref, wet_ref, surface_ref, flow_ref, s_ref, depth_ref):
    zero = jnp.zeros((8, LANES), F32)
    rows = [(all_ref[pl.ds(at, 8)], zero) for at in range(0, all_ref.shape[0], 8)]
    while len(rows) > 1:
        rows = [loose_add(rows[i], rows[i + 1]) for i in range(0, len(rows), 2)]
    total = rows[0]
    for shift in (4, 2, 1):
        total = loose_add(total, tuple(pltpu.roll(x, shift, 0) for x in total))
    total = pair_add(total, tuple(roll(x, -MOMENTS) for x in total))
    lane = lane_iota(8)

    def moment(m):
        return tuple(
            jnp.broadcast_to(jnp.sum(jnp.where(lane == m, x, 0.0), axis=1, keepdims=True), (8, LANES))
            for x in total
        )

    rho = [moment(m) for m in range(MOMENTS)]
    pi = list(rho)
    nought = (zero, zero)
    one = (zero + 1.0, zero)
    surface = [nought] * 4
    residual = [one] + [nought] * 3
    direction = list(residual)
    for step in range(4):
        alpha = pair_clip(pair_div(rho[step], pi[step + 1]), 20.0)
        for i in range(step + 1):
            surface[i] = pair_add(surface[i], pair_mul(alpha, direction[i]))
        if step == 3:
            break
        minus = pair_neg(alpha)
        new_rho = list(rho)
        for m in range(step + 1, MOMENTS - 1 - step):
            new_rho[m] = pair_add(rho[m], pair_mul(minus, pi[m + 1]))
        beta = pair_clip(pair_div(pair_mul(minus, new_rho[step + 1]), rho[step]), 400.0)
        for m in range(step + 2, MOMENTS - 1 - step):
            pi[m] = pair_add(new_rho[m], pair_mul(beta, pi[m]))
        rho = new_rho
        for i in range(step + 1, 0, -1):
            residual[i] = pair_add(residual[i], pair_mul(minus, direction[i - 1]))
        for i in range(step + 2):
            direction[i] = pair_add(residual[i], pair_mul(beta, direction[i]))
    table = depth_table(tops(thick_ref))
    depth_ref[pl.ds(0, HALO)] = look_up(table, near_ref[2 * KL].astype(I32))
    depth_ref[pl.ds(HALO, ROWS)] = look_up(table, wet_ref[...].astype(I32))
    weight = [s[0] for s in surface]
    lane = lane_iota(8)
    by_lane = zero
    for i in range(4):
        by_lane = jnp.where(lane == i, weight[i], by_lane)
    for r0, n in blocks(0, SEEN, 88):
        at = pl.ds(r0, n)
        total = tall(weight[0], n) * seen_ref[0, at]
        for i in range(1, 4):
            total = total + tall(weight[i], n) * seen_ref[i, at]
        s_ref[at] = total
    for r0, n in blocks(HALO, SEEN, 128):
        at = pl.ds(r0, n)
        above = pl.ds(r0 - 1, n)
        own = pl.ds(r0 - HALO, n)
        lane = lane_iota(n)
        s, d = s_ref[at], depth_ref[at]
        beside = beside_ref[own]
        d_west = jnp.where(lane == 0, roll(beside, -4), roll(d, 1))
        beside = tall(by_lane, n) * beside
        beside = beside + roll(beside, -1)
        west = jnp.where(lane == 0, beside + roll(beside, -2), roll(s, 1))
        surface_ref[own] = s
        flow_ref[0, own] = jnp.minimum(d, depth_ref[above]) * (s_ref[above] - s)
        flow_ref[1, own] = jnp.minimum(d, d_west) * (west - s)


VM = pl.BlockSpec(memory_space=pltpu.VMEM)
SM = pl.BlockSpec(memory_space=pltpu.SMEM)
HBM = pl.BlockSpec(memory_space=pltpu.HBM)


def params(limit):
    return pltpu.CompilerParams(vmem_limit_bytes=limit * MIB)


def cost(flops, moved):
    return pl.CostEstimate(flops=flops, bytes_accessed=moved, transcendentals=0)


def ring(x, axis, step):
    count = lax.axis_size(axis)
    return lax.ppermute(x, axis, [(i, (i + step) % count) for i in range(count)])


def shape(*sizes, dtype=F32):
    return jax.ShapeDtypeStruct(sizes, dtype)


def scratch(*lead, rows=BUF, dtype=F32):
    return pltpu.VMEM(lead + (rows, LANES), dtype)


def shards(tracers, mixing, thickness, levels, land):
    devices = lax.axis_size("bx") * lax.axis_size("by")
    planes = 2 * KL
    wet = wet_levels(levels, land).astype(F32)
    flat = tracers.reshape(planes, ROWS, LANES)
    with jax.named_scope("rows"):
        to_up = jnp.concatenate([flat[:, :HALO], wet[None, :HALO]])
        to_down = jnp.concatenate([flat[:, -HALO:], wet[None, -HALO:]])
        top = ring(to_down, "bx", 1)
        bottom = ring(to_up, "bx", -1)
    with jax.named_scope("columns"):
        edges = (shape(2, TILES, EXT, LANES), shape(TILES, EXT, LANES), shape(TILES, EXT, LANES))
        own = pl.pallas_call(
            own_edges_kernel,
            out_shape=edges,
            in_specs=[HBM, VM],
            out_specs=(VM,) * 3,
            scratch_shapes=[scratch(planes, rows=ROWS), pltpu.SemaphoreType.DMA((LOADS,))],
            compiler_params=params(48),
            cost_estimate=cost(10_000_000, 7_000_000),
        )(flat, wet)
        edge, to_right, to_left, near = pl.pallas_call(
            halo_edges_kernel,
            out_shape=edges + (shape(planes + 1, HALO, LANES),),
            in_specs=[VM] * 5,
            out_specs=(VM,) * 4,
            input_output_aliases={i + 2: i for i in range(3)},
            compiler_params=params(16),
            cost_estimate=cost(1_000_000, 700_000),
        )(top, bottom, *own)
        from_left = ring(to_right, "by", 1)
        from_right = ring(to_left, "by", -1)
    with jax.named_scope("block"):
        source, depth = pl.pallas_call(
            block_kernel,
            out_shape=(shape(EXT, LANES), shape(EXT, LANES)),
            in_specs=[SM, SM, HBM, VM, VM, VM],
            out_specs=(VM, VM),
            scratch_shapes=[
                scratch(planes, rows=EXT),
                scratch(dtype=I32),
                scratch(2, rows=EXT),
                scratch(3, rows=EXT, dtype=I32),
                scratch(),
                scratch(),
                scratch(rows=EXT),
                scratch(),
                scratch(),
                scratch(),
                pltpu.SMEM((KL,), F32),
                pltpu.SemaphoreType.DMA((KL,)),
            ],
            compiler_params=params(48),
            cost_estimate=cost(50_000_000, 12_000_000),
        )(mixing, thickness, flat, top, bottom, wet)
    with jax.named_scope("powers"):
        seen, beside, sums, new_edge = pl.pallas_call(
            solve_kernel,
            out_shape=(
                shape(4, SEEN, LANES),
                shape(ROWS, LANES),
                shape(devices, LANES),
                shape(2, TILES, ROWS, LANES),
            ),
            in_specs=[SM, SM] + [VM] * 5,
            out_specs=(VM,) * 4,
            scratch_shapes=[
                scratch(5, 2),
                scratch(2),
                scratch(2, dtype=I32),
                scratch(2, dtype=I32),
                scratch(2, dtype=I32),
                scratch(3, 2, rows=EXT),
                scratch(2),
                scratch(2),
                scratch(rows=EXT),
                scratch(),
                scratch(2),
                scratch(2, rows=EXT),
                scratch(2, 2, rows=EXT),
                scratch(TILES, 4, rows=8),
                scratch(2),
                scratch(2),
                scratch(9, 2, rows=EXT),
                scratch(2),
                scratch(2),
            ],
            compiler_params=params(20),
            cost_estimate=cost(50_000_000, 6_000_000),
        )(mixing, thickness, source, depth, from_left, from_right, edge)
    with jax.named_scope("sums"):
        everyone = lax.all_to_all(sums, ("bx", "by"), 0, 0, tiled=True)
    with jax.named_scope("tracers"):
        tracers_new = pl.pallas_call(
            tracer_kernel,
            out_shape=shape(planes, ROWS, LANES),
            in_specs=[SM, HBM, VM, VM, VM],
            out_specs=HBM,
            scratch_shapes=[
                scratch(planes, rows=EXT),
                scratch(dtype=I32),
                scratch(3, rows=EXT, dtype=I32),
                scratch(2),
                scratch(2),
                scratch(rows=EXT),
                pltpu.SemaphoreType.DMA((KL,)),
                pltpu.SemaphoreType.DMA((KL,)),
            ],
            compiler_params=params(48),
            cost_estimate=cost(80_000_000, 12_000_000),
        )(mixing, flat, near, wet, new_edge)
    with jax.named_scope("surface"):
        surface, transports = pl.pallas_call(
            finish_kernel,
            out_shape=(shape(ROWS, LANES), shape(2, ROWS, LANES)),
            in_specs=[SM] + [VM] * 5,
            out_specs=(VM, VM),
            scratch_shapes=[scratch(rows=SEEN), scratch(rows=SEEN)],
            compiler_params=params(8),
            cost_estimate=cost(1_000_000, 3_000_000),
        )(thickness, everyone, seen, beside, near, wet)
    return tracers_new.reshape(tracers.shape), surface, transports


def solution(mesh):
    in_specs = (P(None, None, "bx", "by"), P(), P(), P("bx", "by"), P("bx", "by"))
    out_specs = (P(None, None, "bx", "by"), P("bx", "by"), P(None, "bx", "by"))
    return jax.shard_map(shards, mesh=mesh, in_specs=in_specs, out_specs=out_specs, check_vma=False)
```

```python
import jax
import jax.numpy as jnp
from jax import lax
from jax.experimental import pallas as pl
from jax.experimental.pallas import tpu as pltpu
from jax.sharding import PartitionSpec as P

KL = 22
ROWS = 256
LANES = 128
HALO = 8
EXT = ROWS + 2 * HALO
PAD = 8
BUF = EXT + 2 * PAD
GROUP = 16
GROUPS = LANES // GROUP
TILES = 3
LOADS = 4
MOMENTS = 8
PATCH = 2
GRAVITY = 10.0
SEEN = HALO + ROWS
F32 = jnp.float32
I32 = jnp.int32
MIB = 1024 * 1024


def lane_iota(rows):
    return lax.broadcasted_iota(I32, (rows, LANES), 1)


def first_half(rows):
    return (lane_iota(rows) & 8) == 0


def tall(x, n):
    return jnp.concatenate([x] * (n // 8)) if n > 8 else x


def roll(x, shift):
    return pltpu.roll(x, shift % LANES, 1)


def blocks(start, stop, size):
    out = []
    while start < stop:
        out.append((start, min(size, stop - start)))
        start += size
    return out


CHUNKS = blocks(0, EXT, 32)
OWN_CHUNKS = blocks(HALO, HALO + ROWS, 32)


def interleave(parts):
    for turn in range(len(CHUNKS) + len(parts) - 1):
        for late, part in enumerate(parts):
            if 0 <= turn - late < len(CHUNKS):
                part(*CHUNKS[turn - late])


def wet_levels(levels, land):
    return jnp.where(land == 0, levels, 0)


def tops(thick_ref):
    out = [jnp.float32(0.0)]
    for k in range(KL):
        out.append(out[-1] + thick_ref[k])
    return out


def depth_table(levels):
    table = jnp.zeros((8, LANES), F32)
    for k, top in enumerate(levels):
        table = jnp.where(lane_iota(8) == k, top, table)
    return table


def look_up(table, index):
    rows = [jnp.take_along_axis(table, index[i : i + 8], axis=1) for i in range(0, index.shape[0], 8)]
    return jnp.concatenate(rows) if len(rows) > 1 else rows[0]


def edge_slot(k):
    return k % TILES, k // TILES


def place(x, k, old):
    _, g = edge_slot(k)
    return jnp.where(lane_iota(x.shape[0]) // GROUP == g, roll(x, 8 + GROUP * g), old)


def to_neighbours(a, b):
    first = first_half(a.shape[0])
    return jnp.where(first, a, roll(b, 8)), jnp.where(first, roll(b, -8), a)


def own_edges_kernel(t_ref, wet_ref, edge_ref, right_ref, left_ref, own_ref, sems):
    parts = blocks(0, KL, -(-KL // LOADS))

    def copy(i):
        start, count = parts[i]
        planes = pl.ds(2 * start, 2 * count)
        return pltpu.make_async_copy(t_ref.at[planes], own_ref.at[planes], sems.at[i])

    for i in range(len(parts)):
        copy(i).start()
    size = ROWS
    tile_eff, _ = edge_slot(KL)

    def rows_of(step):
        own = pl.ds(pl.multiple_of(size * step, 8), size)
        return own, pl.ds(pl.multiple_of(HALO + size * step, 8), size)

    def clear(step, carry):
        own, at = rows_of(step)
        zero = jnp.zeros((size, LANES), F32)
        for c in range(2):
            for tile in range(TILES):
                edge_ref[c, tile, at] = zero
            edge_ref[c, tile_eff, at] = place(wet_ref[own], KL, zero)
        return carry

    lax.fori_loop(0, ROWS // size, clear, 0)
    for i, (start, count) in enumerate(parts):
        copy(i).wait()

        def rows(step, carry):
            own, at = rows_of(step)
            for k in range(start, start + count):
                tile, _ = edge_slot(k)
                for c in range(2):
                    edge_ref[c, tile, at] = place(own_ref[2 * k + c, own], k, edge_ref[c, tile, at])
            return carry

        lax.fori_loop(0, ROWS // size, rows, 0)

    def send(step, carry):
        _, at = rows_of(step)
        for tile in range(TILES):
            right_ref[tile, at], left_ref[tile, at] = to_neighbours(edge_ref[0, tile, at], edge_ref[1, tile, at])
        return carry

    lax.fori_loop(0, ROWS // size, send, 0)


def halo_edges_kernel(top_ref, bottom_ref, edge_in, right_in, left_in, edge_ref, right_ref, left_ref):
    for r0, ref in ((0, top_ref), (HALO + ROWS, bottom_ref)):
        at = pl.ds(r0, HALO)
        held = [[jnp.zeros((HALO, LANES), F32) for _ in range(TILES)] for _ in range(2)]
        for k in range(KL + 1):
            tile, _ = edge_slot(k)
            for c in range(2):
                x = ref[2 * k + c] if k < KL else ref[2 * KL]
                held[c][tile] = place(x, k, held[c][tile])
        for tile in range(TILES):
            for c in range(2):
                edge_ref[c, tile, at] = held[c][tile]
            right_ref[tile, at], left_ref[tile, at] = to_neighbours(held[0][tile], held[1][tile])


def count_word(effs, word):
    total = None
    for eff in effs:
        bits = jnp.clip(eff - 10 * word, 0, 10) * 3
        mask = (lax.shift_left(jnp.full_like(bits, 1), bits) - 1) & 0o1111111111
        total = mask if total is None else total + mask
    return total


def neighbours(ref, r0, n):
    x = ref[pl.ds(PAD + r0, n)]
    around = ref[pl.ds(PAD + r0 - 1, n)] + ref[pl.ds(PAD + r0 + 1, n)]
    return x, around + (roll(x, 1) + roll(x, -1))


def block_kernel(
    mixing_ref,
    thick_ref,
    t_ref,
    top_ref,
    bottom_ref,
    wet_ref,
    new_ref,
    source_ref,
    depth_ref,
    ext_ref,
    eff_ref,
    face_ref,
    word_ref,
    u_ref,
    l_ref,
    n_ref,
    rho_ref,
    fx_ref,
    fy_ref,
    begin_ref,
    in_sems,
    out_sems,
):
    def held(k):
        return ext_ref.at[pl.ds(2 * k, 2), pl.ds(HALO, ROWS)]

    def load(k):
        return pltpu.make_async_copy(t_ref.at[pl.ds(2 * k, 2)], held(k), in_sems.at[k])

    def store(k):
        return pltpu.make_async_copy(held(k), new_ref.at[pl.ds(2 * k, 2)], out_sems.at[k])

    def each(body):
        def step(k, carry):
            body(k)
            return carry

        lax.fori_loop(0, KL, step, 0)

    each(lambda k: load(k).start())
    eff_ref[...] = jnp.zeros(eff_ref.shape, I32)
    eff_ref[pl.ds(PAD, HALO)] = top_ref[2 * KL].astype(I32)
    eff_ref[pl.ds(PAD + HALO, ROWS)] = wet_ref[...].astype(I32)
    eff_ref[pl.ds(PAD + HALO + ROWS, HALO)] = bottom_ref[2 * KL].astype(I32)
    ext_ref[:, pl.ds(0, HALO)] = top_ref[pl.ds(0, 2 * KL)]
    ext_ref[:, pl.ds(HALO + ROWS, HALO)] = bottom_ref[pl.ds(0, 2 * KL)]
    for ref in (u_ref, l_ref, rho_ref, fx_ref, fy_ref):
        ref[...] = jnp.zeros(ref.shape, F32)
    levels = tops(thick_ref)
    table = depth_table(levels)
    for k in range(KL):
        begin_ref[k] = levels[k]
    for r0, n in CHUNKS:
        e = eff_ref[pl.ds(PAD + r0, n)]
        up = eff_ref[pl.ds(PAD + r0 - 1, n)]
        west = roll(e, 1)
        depth_ref[pl.ds(r0, n)] = look_up(table, e)
        face_ref[0, pl.ds(r0, n)] = look_up(table, jnp.minimum(e, up))
        face_ref[1, pl.ds(r0, n)] = look_up(table, jnp.minimum(e, west))
        effs = (up, eff_ref[pl.ds(PAD + r0 + 1, n)], west, roll(e, -1))
        for word in range(3):
            word_ref[word, pl.ds(r0, n)] = count_word(effs, word)

    def count(k, r0, n):
        words = word_ref[k // 10, pl.ds(r0, n)]
        shift = jnp.full((n, LANES), 3 * (k % 10), I32)
        return (lax.shift_right_logical(words, shift) & 7).astype(F32)

    def body(step, stages):
        if 0 in stages:
            load(step).wait()
        if 3 in stages:
            store(step - 3).start()
        ku, kl, kd, kf = (step - late for late in range(4))

        def flux(r0, n):
            here = rho_ref[pl.ds(PAD + r0, n)]
            up = rho_ref[pl.ds(PAD + r0 - 1, n)]
            below_x = jnp.maximum(face_ref[0, pl.ds(r0, n)] - begin_ref[kf], 0.0)
            below_y = jnp.maximum(face_ref[1, pl.ds(r0, n)] - begin_ref[kf], 0.0)
            fx_ref[pl.ds(PAD + r0, n)] += below_x * (here - up)
            fy_ref[pl.ds(PAD + r0, n)] += below_y * (here - roll(here, 1))

        def density(r0, n):
            wet = eff_ref[pl.ds(PAD + r0, n)] > kd
            number = n_ref[pl.ds(r0, n)]
            new = []
            for c in range(2):
                x, around = neighbours(l_ref.at[c], r0, n)
                second = jnp.where(wet, around, 0.0) - number * x
                value = ext_ref[2 * kd + c, pl.ds(r0, n)] - mixing_ref[kd, c] * second
                low, high = max(r0, HALO), min(r0 + n, HALO + ROWS)
                ext_ref[2 * kd + c, pl.ds(low, high - low)] = value[low - r0 : high - r0]
                new.append(value)
            rho_ref[pl.ds(PAD + r0, n)] = (0.8 * thick_ref[kd]) * new[1] - (0.2 * thick_ref[kd]) * new[0]

        def first(r0, n):
            wet = eff_ref[pl.ds(PAD + r0, n)] > kl
            number = count(kl, r0, n)
            n_ref[pl.ds(r0, n)] = number
            for c in range(2):
                x, around = neighbours(u_ref.at[c], r0, n)
                l_ref[c, pl.ds(PAD + r0, n)] = jnp.where(wet, around, 0.0) - number * x

        def masked(r0, n):
            wet = eff_ref[pl.ds(PAD + r0, n)] > ku
            for c in range(2):
                u_ref[c, pl.ds(PAD + r0, n)] = jnp.where(wet, ext_ref[2 * ku + c, pl.ds(r0, n)], 0.0)

        work = ((3, flux), (2, density), (1, first), (0, masked))
        interleave([part for late, part in work if late in stages])

    def all_stages(step, carry):
        body(step, range(4))
        return carry

    for step in range(3):
        body(step, range(step + 1))
    lax.fori_loop(3, KL, all_stages, 0)
    for step in range(KL, KL + 3):
        body(step, range(step - KL + 1, 4))
    for r0, n in CHUNKS:
        fx = fx_ref[pl.ds(PAD + r0, n)] - fx_ref[pl.ds(PAD + r0 + 1, n)]
        fy = fy_ref[pl.ds(PAD + r0, n)]
        source_ref[pl.ds(r0, n)] = GRAVITY * (fx + (fy - roll(fy, -1)))
    each(lambda k: store(k).wait())


def patch_kernel(new_ref, edge_ref, out_ref, held_ref, in_sems, out_sems):
    def planes(k):
        return pl.ds(2 * PATCH * k, 2 * PATCH)

    def load(k):
        return pltpu.make_async_copy(new_ref.at[planes(k)], held_ref.at[planes(k)], in_sems.at[k])

    def store(k):
        return pltpu.make_async_copy(held_ref.at[planes(k)], out_ref.at[planes(k)], out_sems.at[k])

    def each(body):
        def step(k, carry):
            body(k)
            return carry

        lax.fori_loop(0, KL // PATCH, step, 0)

    def levels(part):
        load(part).wait()
        for i in range(PATCH):
            k = part * PATCH + i
            tile = k % TILES
            back = (2 * LANES - 8 - GROUP * (k // TILES)) % LANES
            for c in range(2):
                for r0, n in blocks(0, ROWS, 64):
                    lane = lane_iota(n)
                    middle = jnp.logical_and(lane >= 4, lane < LANES - 4)
                    own = pl.ds(r0, n)
                    edge = pltpu.roll(edge_ref[c, tile, own], back, 1)
                    held_ref[2 * k + c, own] = jnp.where(middle, held_ref[2 * k + c, own], edge)
        store(part).start()

    each(lambda k: load(k).start())
    each(levels)
    each(lambda k: store(k).wait())


def two_sum(a, b):
    s = a + b
    v = s - a
    return s, (a - (s - v)) + (b - v)


def quick_sum(a, b):
    s = a + b
    return s, b - (s - a)


def split(a):
    t = a * 4097.0
    high = t - (t - a)
    return high, a - high


def two_prod(a, b, parts_a, parts_b):
    p = a * b
    ah, al = parts_a
    bh, bl = parts_b
    return p, ((ah * bh - p) + ah * bl + al * bh) + al * bl


def pair_add(x, y):
    s, e = two_sum(x[0], y[0])
    return quick_sum(s, e + (x[1] + y[1]))


def loose_add(x, y):
    s, e = two_sum(x[0], y[0])
    return s, e + (x[1] + y[1])


def pair_mul(x, y):
    p, e = two_prod(x[0], y[0], split(x[0]), split(y[0]))
    return quick_sum(p, e + (x[0] * y[1] + x[1] * y[0]))


def pair_neg(x):
    return -x[0], -x[1]


def pair_div(x, y):
    q = x[0] / y[0]
    rest = pair_add(x, pair_neg(pair_mul(y, (q, jnp.zeros_like(q)))))
    return quick_sum(q, rest[0] / y[0])


def pair_clip(x, top):
    inside = jnp.logical_and(x[0] >= 0.0, x[0] <= top)
    high = jnp.where(inside, x[0], jnp.where(x[0] > top, top, 0.0))
    return high, jnp.where(inside, x[1], 0.0)


def group_totals(x):
    x = x + roll(x, GROUP)
    x = x + roll(x, 2 * GROUP)
    return x + roll(x, 4 * GROUP)


def lane_left(main, side):
    lane = lane_iota(main.shape[0])
    a, b = roll(main, 1), roll(side, 1)
    return jnp.where(lane == 0, b, a), jnp.where(lane == 0, a, b)


def lane_right(main, side):
    lane = lane_iota(main.shape[0])
    a, b = roll(main, -1), roll(side, -1)
    return jnp.where(lane == LANES - 1, b, a), jnp.where(lane == LANES - 1, a, b)


SIDES = (0, 1)


def solve_kernel(
    mixing_ref,
    thick_ref,
    source_ref,
    depth_in,
    from_left_ref,
    from_right_ref,
    edge_ref,
    seen_ref,
    beside_ref,
    depth_ref,
    sums_ref,
    new_ref,
    v_ref,
    d_ref,
    e_ref,
    west_ref,
    east_ref,
    f_ref,
    u_ref,
    l_ref,
    n_ref,
    rho_ref,
    fx_ref,
    fy_ref,
    face_ref,
    lanes_ref,
    dl_ref,
    dr_ref,
    w_ref,
    p_ref,
    q_ref,
):
    by = lax.axis_index("by")
    open_side = (by != 0, by != lax.axis_size("by") - 1)

    def clear(ref):
        ref[...] = jnp.zeros(ref.shape, ref.dtype)

    for ref in (e_ref, west_ref, east_ref):
        clear(ref)
    for ref in (u_ref, l_ref, rho_ref, d_ref, v_ref, dl_ref, dr_ref, p_ref, q_ref, fx_ref):
        rank = len(ref.shape) - 2
        lead = [()]
        for size in ref.shape[:rank]:
            lead = [i + (j,) for i in lead for j in range(size)]
        for i in lead:
            for r0 in (0, BUF - PAD):
                ref[i + (pl.ds(r0, PAD),)] = jnp.zeros((PAD, LANES), F32)

    def field(side, c, tile, r0, n):
        own = edge_ref[c, tile, pl.ds(r0, n)]
        first = first_half(n)
        if side == 0:
            far = from_left_ref[tile, pl.ds(r0, n)]
            return jnp.where(first, roll(far, -8) if c else far, own)
        far = from_right_ref[tile, pl.ds(r0, n)]
        return jnp.where(first, own, roll(far, 8) if c else far)

    tile_eff, slot = edge_slot(KL)
    for side in SIDES:
        for r0, n in CHUNKS:
            lane = lane_iota(n)
            x = field(side, 0, tile_eff, r0, n)
            inner = (lane & 8) == (8 if side == 0 else 0)
            keep = jnp.logical_and(lane // GROUP == slot, jnp.logical_or(inner, open_side[side]))
            e = group_totals(jnp.where(keep, x, 0.0)).astype(I32)
            at = pl.ds(PAD + r0, n)
            e_ref[side, at] = e
            west_ref[side, at] = roll(e, 1)
            east_ref[side, at] = roll(e, -1)

    levels = tops(thick_ref)
    table = depth_table(levels)
    group8 = lane_iota(8) // GROUP
    for tile in range(TILES):
        held = [jnp.zeros((8, LANES), F32) for _ in range(4)]
        for g in range(GROUPS):
            k = TILES * g + tile
            if k < KL:
                values = (mixing_ref[k, 0], mixing_ref[k, 1], thick_ref[k], levels[k])
            else:
                values = (0.0, 0.0, 0.0, levels[KL])
            held = [jnp.where(group8 == g, x, old) for x, old in zip(values, held)]
        for i in range(4):
            lanes_ref[tile, i] = held[i]
    for side in SIDES:
        for r0, n in CHUNKS:
            e = e_ref[side, pl.ds(PAD + r0, n)]
            face_ref[side, 0, pl.ds(r0, n)] = look_up(table, jnp.minimum(e, e_ref[side, pl.ds(PAD + r0 - 1, n)]))
            face_ref[side, 1, pl.ds(r0, n)] = look_up(table, jnp.minimum(e, west_ref[side, pl.ds(PAD + r0, n)]))
    pieces = [(tile, side) for tile in range(TILES) for side in SIDES]

    def stages(piece):
        tile, side = pieces[piece]
        slot = piece % 3
        level_of = group8 * TILES + tile
        mix = [lanes_ref[tile, c] for c in range(2)]
        thick = lanes_ref[tile, 2]
        begin = lanes_ref[tile, 3]

        def masked(r0, n):
            at = pl.ds(PAD + r0, n)
            wet = e_ref[side, at] > tall(level_of, n)
            for c in range(2):
                x = field(side, c, tile, r0, n)
                f_ref[slot, c, pl.ds(r0, n)] = x
                u_ref[c, at] = jnp.where(wet, x, 0.0)

        def first(r0, n):
            at = pl.ds(PAD + r0, n)
            wet = e_ref[side, at] > tall(level_of, n)
            number = jnp.where(e_ref[side, pl.ds(PAD + r0 - 1, n)] > tall(level_of, n), 1.0, 0.0)
            number += jnp.where(e_ref[side, pl.ds(PAD + r0 + 1, n)] > tall(level_of, n), 1.0, 0.0)
            number += jnp.where(west_ref[side, at] > tall(level_of, n), 1.0, 0.0)
            number += jnp.where(east_ref[side, at] > tall(level_of, n), 1.0, 0.0)
            n_ref[pl.ds(r0, n)] = number
            for c in range(2):
                x, around = neighbours(u_ref.at[c], r0, n)
                l_ref[c, at] = jnp.where(wet, around, 0.0) - number * x

        def density(r0, n):
            at = pl.ds(PAD + r0, n)
            wet = e_ref[side, at] > tall(level_of, n)
            number = n_ref[pl.ds(r0, n)]
            new = []
            for c in range(2):
                x, around = neighbours(l_ref.at[c], r0, n)
                second = jnp.where(wet, around, 0.0) - number * x
                new.append(f_ref[slot, c, pl.ds(r0, n)] - tall(mix[c], n) * second)
            rho_ref[at] = tall(thick, n) * (0.8 * new[1] - 0.2 * new[0])
            low, high = max(r0, HALO), min(r0 + n, HALO + ROWS)
            own = pl.ds(low - HALO, high - low)
            for c in range(2):
                value = new[c][low - r0 : high - r0]
                if side == 1:
                    value = jnp.where(first_half(high - low), value, new_ref[c, tile, own])
                new_ref[c, tile, own] = value

        def flux(r0, n):
            here = rho_ref[pl.ds(PAD + r0, n)]
            up = rho_ref[pl.ds(PAD + r0 - 1, n)]
            below_x = jnp.maximum(face_ref[side, 0, pl.ds(r0, n)] - tall(begin, n), 0.0)
            below_y = jnp.maximum(face_ref[side, 1, pl.ds(r0, n)] - tall(begin, n), 0.0)
            face_x = below_x * (here - up)
            face_y = below_y * (here - roll(here, 1))
            if tile > 0:
                face_x += fx_ref[side, pl.ds(PAD + r0, n)]
                face_y += fy_ref[side, pl.ds(r0, n)]
            fx_ref[side, pl.ds(PAD + r0, n)] = face_x
            fy_ref[side, pl.ds(r0, n)] = face_y

        return masked, first, density, flux

    for step in range(len(pieces) + 3):
        parts = [stages(step - late)[late] for late in (3, 2, 1, 0) if 0 <= step - late < len(pieces)]
        interleave(parts)

    halves = blocks(0, EXT, EXT // 2)
    for r0, n in halves:
        lane = lane_iota(n)
        at = pl.ds(PAD + r0, n)
        own = pl.ds(r0, n)
        sources = []
        for side in SIDES:
            fy = fy_ref[side, own]
            sources.append(fx_ref[side, at] - fx_ref[side, pl.ds(PAD + r0 + 1, n)] + (fy - roll(fy, -1)))
        for shift in (GROUP, 2 * GROUP, 4 * GROUP):
            sources = [x + roll(x, shift) for x in sources]
        west, east = (GRAVITY * roll(x, 8) for x in sources)
        v_ref[0, 0, at] = jnp.where(lane < 3, west, jnp.where(lane >= LANES - 3, east, source_ref[own]))
        v_ref[0, 1, at] = jnp.where(lane < 8, east, jnp.where(lane >= LANES - 8, west, 0.0))
    for r0, n in halves:
        lane = lane_iota(n)
        at = pl.ds(PAD + r0, n)
        west = roll(e_ref[0, at], 8)
        east = roll(e_ref[1, at], 8)
        beside = jnp.where(lane < 8, east, jnp.where(lane >= LANES - 8, west, 0))
        d_ref[0, at] = depth_in[pl.ds(r0, n)]
        d_ref[1, at] = look_up(table, beside)
    for r0, n in CHUNKS:
        here = pl.ds(PAD + r0, n)
        d_main, d_side = d_ref[0, here], d_ref[1, here]
        dl_ref[0, here], dl_ref[1, here] = lane_left(d_main, d_side)
        dr_ref[0, here], dr_ref[1, here] = lane_right(d_main, d_side)

    def weights(t, carry):
        for r0, n in CHUNKS:
            here = pl.ds(PAD + r0, n)
            above = pl.ds(PAD + r0 - 1, n)
            below = pl.ds(PAD + r0 + 1, n)
            d = d_ref[t, here]
            left, right = dl_ref[t, here], dr_ref[t, here]
            up, down = d_ref[t, above], d_ref[t, below]
            w_west, w_east = jnp.minimum(d, left), jnp.minimum(d, right)
            w_up, w_down = jnp.minimum(d, up), jnp.minimum(d, down)
            corners = (
                jnp.minimum(d, dl_ref[t, above])
                + jnp.minimum(d, dr_ref[t, below])
                + jnp.minimum(d, dr_ref[t, above])
                + jnp.minimum(d, dl_ref[t, below])
            )
            at = pl.ds(r0, n)
            w_ref[0, t, at] = 0.05 + w_up + w_down + w_west + w_east + 0.25 * corners
            w_ref[1, t, at] = w_west
            w_ref[2, t, at] = w_east
            w_ref[3, t, at] = w_down
            w_ref[4, t, at] = 0.25 * jnp.minimum(down, left)
            w_ref[5, t, at] = 0.25 * jnp.minimum(down, right)
            w_ref[6, t, at] = w_up
            w_ref[7, t, at] = 0.25 * jnp.minimum(up, left)
            w_ref[8, t, at] = 0.25 * jnp.minimum(up, right)
        return carry

    lax.fori_loop(0, 2, weights, 0)

    def power(step, carry):
        for r0, n in CHUNKS:
            here = pl.ds(PAD + r0, n)
            at = pl.ds(r0, n)
            v = (v_ref[step, 0, here], v_ref[step, 1, here])
            left = lane_left(*v)
            right = lane_right(*v)
            for t in range(2):
                w = [w_ref[m, t, at] for m in range(9)]
                p_ref[t, here] = w[3] * v[t] + w[4] * left[t] + w[5] * right[t]
                q_ref[t, here] = w[6] * v[t] + w[7] * left[t] + w[8] * right[t]
                v_ref[step + 1, t, here] = w[0] * v[t] - (w[1] * left[t] + w[2] * right[t])
        for r0, n in CHUNKS:
            here = pl.ds(PAD + r0, n)
            for t in range(2):
                beside = p_ref[t, pl.ds(PAD + r0 - 1, n)] + q_ref[t, pl.ds(PAD + r0 + 1, n)]
                v_ref[step + 1, t, here] -= beside
        return carry

    lax.fori_loop(0, 4, power, 0)

    for i in range(4):
        seen_ref[i] = v_ref[i, 0, pl.ds(PAD, SEEN)]
    depth_ref[...] = d_ref[0, pl.ds(PAD, SEEN)]
    for r0, n in blocks(HALO, HALO + ROWS, 128):
        lane = lane_iota(n)
        at = pl.ds(PAD + r0, n)
        beside = roll(d_ref[1, at], 5)
        for i in range(4):
            beside = jnp.where(lane == i, roll(v_ref[i, 1, at], i + 1), beside)
        beside_ref[pl.ds(r0 - HALO, n)] = beside

    def dots(step, carry):
        at = pl.ds(pl.multiple_of(PAD + HALO + 8 * step, 8), 8)
        v = [v_ref[i, 0, at] for i in range(5)]
        parts = [split(x) for x in v]
        out = []
        for m in range(MOMENTS):
            i, j = m // 2, (m + 1) // 2
            p, e = two_prod(v[i], v[j], parts[i], parts[j])
            s, f = two_sum(carry[2 * m], p)
            out += [s, carry[2 * m + 1] + (e + f)]
        return tuple(out)

    zero = jnp.zeros((8, LANES), F32)
    sums = lax.fori_loop(0, ROWS // 8, dots, (zero,) * (2 * MOMENTS), unroll=4)
    sub = lax.broadcasted_iota(I32, (8, LANES), 0)
    pairs = [(sums[2 * m], sums[2 * m + 1]) for m in range(MOMENTS)]
    for half in (4, 2, 1):
        merged = []
        for m in range(half):
            a, b = pairs[m], pairs[m + half]
            upper = (sub & half) == 0
            keep = tuple(jnp.where(upper, x, y) for x, y in zip(a, b))
            other = tuple(jnp.where(upper, pltpu.roll(x, 8 - half, 0), pltpu.roll(y, half, 0)) for x, y in zip(a, b))
            merged.append(loose_add(keep, other))
        pairs = merged
    wide = [jnp.concatenate([x, jnp.zeros((LANES - 8, LANES), F32)]).T for x in pairs[0]]
    rows = [tuple(x[at : at + 8] for x in wide) for at in range(0, LANES, 8)]
    while len(rows) > 1:
        rows = [loose_add(rows[i], rows[i + 1]) for i in range(0, len(rows), 2)]
    total = rows[0]
    for shift in (4, 2, 1):
        total = loose_add(total, tuple(pltpu.roll(x, shift, 0) for x in total))
    total = quick_sum(*total)
    row = total[0] + roll(total[1], MOMENTS)
    for at in range(0, sums_ref.shape[0], 8):
        sums_ref[pl.ds(at, 8)] = row


def finish_kernel(all_ref, seen_ref, beside_ref, depth_ref, surface_ref, flow_ref, s_ref):
    zero = jnp.zeros((8, LANES), F32)
    rows = [(all_ref[pl.ds(at, 8)], zero) for at in range(0, all_ref.shape[0], 8)]
    while len(rows) > 1:
        rows = [loose_add(rows[i], rows[i + 1]) for i in range(0, len(rows), 2)]
    total = rows[0]
    for shift in (4, 2, 1):
        total = loose_add(total, tuple(pltpu.roll(x, shift, 0) for x in total))
    total = pair_add(total, tuple(roll(x, -MOMENTS) for x in total))
    lane = lane_iota(8)

    def moment(m):
        return tuple(
            jnp.broadcast_to(jnp.sum(jnp.where(lane == m, x, 0.0), axis=1, keepdims=True), (8, LANES))
            for x in total
        )

    rho = [moment(m) for m in range(MOMENTS)]
    pi = list(rho)
    nought = (zero, zero)
    one = (zero + 1.0, zero)
    surface = [nought] * 4
    residual = [one] + [nought] * 3
    direction = list(residual)
    for step in range(4):
        alpha = pair_clip(pair_div(rho[step], pi[step + 1]), 20.0)
        for i in range(step + 1):
            surface[i] = pair_add(surface[i], pair_mul(alpha, direction[i]))
        if step == 3:
            break
        minus = pair_neg(alpha)
        new_rho = list(rho)
        for m in range(step + 1, MOMENTS - 1 - step):
            new_rho[m] = pair_add(rho[m], pair_mul(minus, pi[m + 1]))
        beta = pair_clip(pair_div(pair_mul(minus, new_rho[step + 1]), rho[step]), 400.0)
        for m in range(step + 2, MOMENTS - 1 - step):
            pi[m] = pair_add(new_rho[m], pair_mul(beta, pi[m]))
        rho = new_rho
        for i in range(step + 1, 0, -1):
            residual[i] = pair_add(residual[i], pair_mul(minus, direction[i - 1]))
        for i in range(step + 2):
            direction[i] = pair_add(residual[i], pair_mul(beta, direction[i]))
    weight = [s[0] for s in surface]
    lane = lane_iota(8)
    by_lane = zero
    for i in range(4):
        by_lane = jnp.where(lane == i, weight[i], by_lane)
    for r0, n in blocks(0, SEEN, 88):
        at = pl.ds(r0, n)
        total = tall(weight[0], n) * seen_ref[0, at]
        for i in range(1, 4):
            total = total + tall(weight[i], n) * seen_ref[i, at]
        s_ref[at] = total
    for r0, n in blocks(HALO, SEEN, 128):
        at = pl.ds(r0, n)
        above = pl.ds(r0 - 1, n)
        own = pl.ds(r0 - HALO, n)
        lane = lane_iota(n)
        s, d = s_ref[at], depth_ref[at]
        beside = beside_ref[own]
        d_west = jnp.where(lane == 0, roll(beside, -4), roll(d, 1))
        beside = tall(by_lane, n) * beside
        beside = beside + roll(beside, -1)
        west = jnp.where(lane == 0, beside + roll(beside, -2), roll(s, 1))
        surface_ref[own] = s
        flow_ref[0, own] = jnp.minimum(d, depth_ref[above]) * (s_ref[above] - s)
        flow_ref[1, own] = jnp.minimum(d, d_west) * (west - s)


VM = pl.BlockSpec(memory_space=pltpu.VMEM)
SM = pl.BlockSpec(memory_space=pltpu.SMEM)
HBM = pl.BlockSpec(memory_space=pltpu.HBM)


def params(limit):
    return pltpu.CompilerParams(vmem_limit_bytes=limit * MIB)


def cost(flops, moved):
    return pl.CostEstimate(flops=flops, bytes_accessed=moved, transcendentals=0)


def ring(x, axis, step):
    count = lax.axis_size(axis)
    return lax.ppermute(x, axis, [(i, (i + step) % count) for i in range(count)])


def shape(*sizes, dtype=F32):
    return jax.ShapeDtypeStruct(sizes, dtype)


def scratch(*lead, rows=BUF, dtype=F32):
    return pltpu.VMEM(lead + (rows, LANES), dtype)


def shards(tracers, mixing, thickness, levels, land):
    devices = lax.axis_size("bx") * lax.axis_size("by")
    planes = 2 * KL
    wet = wet_levels(levels, land).astype(F32)
    flat = tracers.reshape(planes, ROWS, LANES)
    with jax.named_scope("rows"):
        to_up = jnp.concatenate([flat[:, :HALO], wet[None, :HALO]])
        to_down = jnp.concatenate([flat[:, -HALO:], wet[None, -HALO:]])
        top = ring(to_down, "bx", 1)
        bottom = ring(to_up, "bx", -1)
    with jax.named_scope("columns"):
        edges = (shape(2, TILES, EXT, LANES), shape(TILES, EXT, LANES), shape(TILES, EXT, LANES))
        own = pl.pallas_call(
            own_edges_kernel,
            out_shape=edges,
            in_specs=[HBM, VM],
            out_specs=(VM,) * 3,
            scratch_shapes=[scratch(planes, rows=ROWS), pltpu.SemaphoreType.DMA((LOADS,))],
            compiler_params=params(48),
            cost_estimate=cost(10_000_000, 7_000_000),
        )(flat, wet)
        edge, to_right, to_left = pl.pallas_call(
            halo_edges_kernel,
            out_shape=edges,
            in_specs=[VM] * 5,
            out_specs=(VM,) * 3,
            input_output_aliases={i + 2: i for i in range(3)},
            compiler_params=params(16),
            cost_estimate=cost(1_000_000, 700_000),
        )(top, bottom, *own)
        from_left = ring(to_right, "by", 1)
        from_right = ring(to_left, "by", -1)
    with jax.named_scope("block"):
        new, source, depth = pl.pallas_call(
            block_kernel,
            out_shape=(shape(planes, ROWS, LANES), shape(EXT, LANES), shape(EXT, LANES)),
            in_specs=[SM, SM, HBM, VM, VM, VM],
            out_specs=(HBM, VM, VM),
            scratch_shapes=[
                scratch(planes, rows=EXT),
                scratch(dtype=I32),
                scratch(2, rows=EXT),
                scratch(3, rows=EXT, dtype=I32),
                scratch(2),
                scratch(2),
                scratch(rows=EXT),
                scratch(),
                scratch(),
                scratch(),
                pltpu.SMEM((KL,), F32),
                pltpu.SemaphoreType.DMA((KL,)),
                pltpu.SemaphoreType.DMA((KL,)),
            ],
            compiler_params=params(48),
            cost_estimate=cost(50_000_000, 12_000_000),
        )(mixing, thickness, flat, top, bottom, wet)
    with jax.named_scope("powers"):
        seen, beside, near_depth, sums, new_edge = pl.pallas_call(
            solve_kernel,
            out_shape=(
                shape(4, SEEN, LANES),
                shape(ROWS, LANES),
                shape(SEEN, LANES),
                shape(devices, LANES),
                shape(2, TILES, ROWS, LANES),
            ),
            in_specs=[SM, SM] + [VM] * 5,
            out_specs=(VM,) * 5,
            scratch_shapes=[
                scratch(5, 2),
                scratch(2),
                scratch(2, dtype=I32),
                scratch(2, dtype=I32),
                scratch(2, dtype=I32),
                scratch(3, 2, rows=EXT),
                scratch(2),
                scratch(2),
                scratch(rows=EXT),
                scratch(),
                scratch(2),
                scratch(2, rows=EXT),
                scratch(2, 2, rows=EXT),
                scratch(TILES, 4, rows=8),
                scratch(2),
                scratch(2),
                scratch(9, 2, rows=EXT),
                scratch(2),
                scratch(2),
            ],
            compiler_params=params(20),
            cost_estimate=cost(50_000_000, 6_000_000),
        )(mixing, thickness, source, depth, from_left, from_right, edge)
    with jax.named_scope("sums"):
        everyone = lax.all_to_all(sums, ("bx", "by"), 0, 0, tiled=True)
    with jax.named_scope("patch"):
        tracers_new = pl.pallas_call(
            patch_kernel,
            out_shape=shape(planes, ROWS, LANES),
            in_specs=[HBM, VM],
            out_specs=HBM,
            scratch_shapes=[
                scratch(planes, rows=ROWS),
                pltpu.SemaphoreType.DMA((KL // PATCH,)),
                pltpu.SemaphoreType.DMA((KL // PATCH,)),
            ],
            compiler_params=params(48),
            cost_estimate=cost(10_000_000, 12_000_000),
        )(new, new_edge)
    with jax.named_scope("surface"):
        surface, transports = pl.pallas_call(
            finish_kernel,
            out_shape=(shape(ROWS, LANES), shape(2, ROWS, LANES)),
            in_specs=[VM] * 4,
            out_specs=(VM, VM),
            scratch_shapes=[scratch(rows=SEEN)],
            compiler_params=params(8),
            cost_estimate=cost(1_000_000, 3_000_000),
        )(everyone, seen, beside, near_depth)
    return tracers_new.reshape(tracers.shape), surface, transports


def solution(mesh):
    in_specs = (P(None, None, "bx", "by"), P(), P(), P("bx", "by"), P("bx", "by"))
    out_specs = (P(None, None, "bx", "by"), P("bx", "by"), P(None, "bx", "by"))
    return jax.shard_map(shards, mesh=mesh, in_specs=in_specs, out_specs=out_specs, check_vma=False)
```

```python
import jax
import jax.numpy as jnp
from jax import lax
from jax.experimental import pallas as pl
from jax.experimental.pallas import tpu as pltpu
from jax.sharding import PartitionSpec as P

KL = 22
ROWS = 256
LANES = 128
HALO = 8
EXT = ROWS + 2 * HALO
PAD = 8
BUF = EXT + 2 * PAD
GROUP = 16
GROUPS = LANES // GROUP
TILES = 3
LOADS = 4
MOMENTS = 8
PATCH = 2
GRAVITY = 10.0
SEEN = HALO + ROWS
F32 = jnp.float32
I32 = jnp.int32
MIB = 1024 * 1024


def lane_iota(rows):
    return lax.broadcasted_iota(I32, (rows, LANES), 1)


def first_half(rows):
    return (lane_iota(rows) & 8) == 0


def tall(x, n):
    return jnp.concatenate([x] * (n // 8)) if n > 8 else x


def roll(x, shift):
    return pltpu.roll(x, shift % LANES, 1)


def blocks(start, stop, size):
    out = []
    while start < stop:
        out.append((start, min(size, stop - start)))
        start += size
    return out


CHUNKS = blocks(0, EXT, 32)
OWN_CHUNKS = blocks(HALO, HALO + ROWS, 32)


def interleave(parts):
    for turn in range(len(CHUNKS) + len(parts) - 1):
        for late, part in enumerate(parts):
            if 0 <= turn - late < len(CHUNKS):
                part(*CHUNKS[turn - late])


def wet_levels(levels, land):
    return jnp.where(land == 0, levels, 0)


def tops(thick_ref):
    out = [jnp.float32(0.0)]
    for k in range(KL):
        out.append(out[-1] + thick_ref[k])
    return out


def depth_table(levels):
    table = jnp.zeros((8, LANES), F32)
    for k, top in enumerate(levels):
        table = jnp.where(lane_iota(8) == k, top, table)
    return table


def look_up(table, index):
    rows = [jnp.take_along_axis(table, index[i : i + 8], axis=1) for i in range(0, index.shape[0], 8)]
    return jnp.concatenate(rows) if len(rows) > 1 else rows[0]


def edge_slot(k):
    return k % TILES, k // TILES


def place(x, k, old):
    _, g = edge_slot(k)
    return jnp.where(lane_iota(x.shape[0]) // GROUP == g, roll(x, 8 + GROUP * g), old)


def to_neighbours(a, b):
    first = first_half(a.shape[0])
    return jnp.where(first, a, roll(b, 8)), jnp.where(first, roll(b, -8), a)


def own_edges_kernel(t_ref, wet_ref, edge_ref, right_ref, left_ref, own_ref, sems):
    parts = blocks(0, KL, -(-KL // LOADS))

    def copy(i):
        start, count = parts[i]
        planes = pl.ds(2 * start, 2 * count)
        return pltpu.make_async_copy(t_ref.at[planes], own_ref.at[planes], sems.at[i])

    for i in range(len(parts)):
        copy(i).start()
    size = ROWS
    tile_eff, _ = edge_slot(KL)

    def rows_of(step):
        own = pl.ds(pl.multiple_of(size * step, 8), size)
        return own, pl.ds(pl.multiple_of(HALO + size * step, 8), size)

    def clear(step, carry):
        own, at = rows_of(step)
        zero = jnp.zeros((size, LANES), F32)
        for c in range(2):
            for tile in range(TILES):
                edge_ref[c, tile, at] = zero
            edge_ref[c, tile_eff, at] = place(wet_ref[own], KL, zero)
        return carry

    lax.fori_loop(0, ROWS // size, clear, 0)
    for i, (start, count) in enumerate(parts):
        copy(i).wait()

        def rows(step, carry):
            own, at = rows_of(step)
            for k in range(start, start + count):
                tile, _ = edge_slot(k)
                for c in range(2):
                    edge_ref[c, tile, at] = place(own_ref[2 * k + c, own], k, edge_ref[c, tile, at])
            return carry

        lax.fori_loop(0, ROWS // size, rows, 0)

    def send(step, carry):
        _, at = rows_of(step)
        for tile in range(TILES):
            right_ref[tile, at], left_ref[tile, at] = to_neighbours(edge_ref[0, tile, at], edge_ref[1, tile, at])
        return carry

    lax.fori_loop(0, ROWS // size, send, 0)


def halo_edges_kernel(top_ref, bottom_ref, edge_in, right_in, left_in, edge_ref, right_ref, left_ref):
    for r0, ref in ((0, top_ref), (HALO + ROWS, bottom_ref)):
        at = pl.ds(r0, HALO)
        held = [[jnp.zeros((HALO, LANES), F32) for _ in range(TILES)] for _ in range(2)]
        for k in range(KL + 1):
            tile, _ = edge_slot(k)
            for c in range(2):
                x = ref[2 * k + c] if k < KL else ref[2 * KL]
                held[c][tile] = place(x, k, held[c][tile])
        for tile in range(TILES):
            for c in range(2):
                edge_ref[c, tile, at] = held[c][tile]
            right_ref[tile, at], left_ref[tile, at] = to_neighbours(held[0][tile], held[1][tile])


def count_word(effs, word):
    total = None
    for eff in effs:
        bits = jnp.clip(eff - 10 * word, 0, 10) * 3
        mask = (lax.shift_left(jnp.full_like(bits, 1), bits) - 1) & 0o1111111111
        total = mask if total is None else total + mask
    return total


def neighbours(ref, r0, n):
    x = ref[pl.ds(PAD + r0, n)]
    around = ref[pl.ds(PAD + r0 - 1, n)] + ref[pl.ds(PAD + r0 + 1, n)]
    return x, around + (roll(x, 1) + roll(x, -1))


def block_kernel(
    mixing_ref,
    thick_ref,
    t_ref,
    top_ref,
    bottom_ref,
    wet_ref,
    new_ref,
    source_ref,
    depth_ref,
    ext_ref,
    eff_ref,
    face_ref,
    word_ref,
    u_ref,
    l_ref,
    n_ref,
    rho_ref,
    fx_ref,
    fy_ref,
    begin_ref,
    in_sems,
    out_sems,
):
    def held(k):
        return ext_ref.at[pl.ds(2 * k, 2), pl.ds(HALO, ROWS)]

    def load(k):
        return pltpu.make_async_copy(t_ref.at[pl.ds(2 * k, 2)], held(k), in_sems.at[k])

    def store(k):
        return pltpu.make_async_copy(held(k), new_ref.at[pl.ds(2 * k, 2)], out_sems.at[k])

    def each(body):
        def step(k, carry):
            body(k)
            return carry

        lax.fori_loop(0, KL, step, 0)

    each(lambda k: load(k).start())
    eff_ref[...] = jnp.zeros(eff_ref.shape, I32)
    eff_ref[pl.ds(PAD, HALO)] = top_ref[2 * KL].astype(I32)
    eff_ref[pl.ds(PAD + HALO, ROWS)] = wet_ref[...].astype(I32)
    eff_ref[pl.ds(PAD + HALO + ROWS, HALO)] = bottom_ref[2 * KL].astype(I32)
    ext_ref[:, pl.ds(0, HALO)] = top_ref[pl.ds(0, 2 * KL)]
    ext_ref[:, pl.ds(HALO + ROWS, HALO)] = bottom_ref[pl.ds(0, 2 * KL)]
    for ref in (u_ref, l_ref, rho_ref, fx_ref, fy_ref):
        ref[...] = jnp.zeros(ref.shape, F32)
    levels = tops(thick_ref)
    table = depth_table(levels)
    for k in range(KL):
        begin_ref[k] = levels[k]
    for r0, n in CHUNKS:
        e = eff_ref[pl.ds(PAD + r0, n)]
        up = eff_ref[pl.ds(PAD + r0 - 1, n)]
        west = roll(e, 1)
        depth_ref[pl.ds(r0, n)] = look_up(table, e)
        face_ref[0, pl.ds(r0, n)] = look_up(table, jnp.minimum(e, up))
        face_ref[1, pl.ds(r0, n)] = look_up(table, jnp.minimum(e, west))
        effs = (up, eff_ref[pl.ds(PAD + r0 + 1, n)], west, roll(e, -1))
        for word in range(3):
            word_ref[word, pl.ds(r0, n)] = count_word(effs, word)

    def count(k, r0, n):
        words = word_ref[k // 10, pl.ds(r0, n)]
        shift = jnp.full((n, LANES), 3 * (k % 10), I32)
        return (lax.shift_right_logical(words, shift) & 7).astype(F32)

    def body(step, stages):
        if 0 in stages:
            load(step).wait()
        if 3 in stages:
            store(step - 3).start()
        ku, kl, kd, kf = (step - late for late in range(4))

        def flux(r0, n):
            here = rho_ref[pl.ds(PAD + r0, n)]
            up = rho_ref[pl.ds(PAD + r0 - 1, n)]
            below_x = jnp.maximum(face_ref[0, pl.ds(r0, n)] - begin_ref[kf], 0.0)
            below_y = jnp.maximum(face_ref[1, pl.ds(r0, n)] - begin_ref[kf], 0.0)
            fx_ref[pl.ds(PAD + r0, n)] += below_x * (here - up)
            fy_ref[pl.ds(PAD + r0, n)] += below_y * (here - roll(here, 1))

        def density(r0, n):
            wet = eff_ref[pl.ds(PAD + r0, n)] > kd
            number = n_ref[pl.ds(r0, n)]
            new = []
            for c in range(2):
                x, around = neighbours(l_ref.at[c], r0, n)
                second = jnp.where(wet, around, 0.0) - number * x
                value = ext_ref[2 * kd + c, pl.ds(r0, n)] - mixing_ref[kd, c] * second
                low, high = max(r0, HALO), min(r0 + n, HALO + ROWS)
                ext_ref[2 * kd + c, pl.ds(low, high - low)] = value[low - r0 : high - r0]
                new.append(value)
            rho_ref[pl.ds(PAD + r0, n)] = (0.8 * thick_ref[kd]) * new[1] - (0.2 * thick_ref[kd]) * new[0]

        def first(r0, n):
            wet = eff_ref[pl.ds(PAD + r0, n)] > kl
            number = count(kl, r0, n)
            n_ref[pl.ds(r0, n)] = number
            for c in range(2):
                x, around = neighbours(u_ref.at[c], r0, n)
                l_ref[c, pl.ds(PAD + r0, n)] = jnp.where(wet, around, 0.0) - number * x

        def masked(r0, n):
            wet = eff_ref[pl.ds(PAD + r0, n)] > ku
            for c in range(2):
                u_ref[c, pl.ds(PAD + r0, n)] = jnp.where(wet, ext_ref[2 * ku + c, pl.ds(r0, n)], 0.0)

        work = ((3, flux), (2, density), (1, first), (0, masked))
        interleave([part for late, part in work if late in stages])

    def all_stages(step, carry):
        body(step, range(4))
        return carry

    for step in range(3):
        body(step, range(step + 1))
    lax.fori_loop(3, KL, all_stages, 0)
    for step in range(KL, KL + 3):
        body(step, range(step - KL + 1, 4))
    for r0, n in CHUNKS:
        fx = fx_ref[pl.ds(PAD + r0, n)] - fx_ref[pl.ds(PAD + r0 + 1, n)]
        fy = fy_ref[pl.ds(PAD + r0, n)]
        source_ref[pl.ds(r0, n)] = GRAVITY * (fx + (fy - roll(fy, -1)))
    each(lambda k: store(k).wait())


def patch_kernel(new_ref, edge_ref, out_ref, held_ref, in_sems, out_sems):
    def planes(k):
        return pl.ds(2 * PATCH * k, 2 * PATCH)

    def load(k):
        return pltpu.make_async_copy(new_ref.at[planes(k)], held_ref.at[planes(k)], in_sems.at[k])

    def store(k):
        return pltpu.make_async_copy(held_ref.at[planes(k)], out_ref.at[planes(k)], out_sems.at[k])

    def each(body):
        def step(k, carry):
            body(k)
            return carry

        lax.fori_loop(0, KL // PATCH, step, 0)

    def levels(part):
        load(part).wait()
        for i in range(PATCH):
            k = part * PATCH + i
            tile = k % TILES
            back = (2 * LANES - 8 - GROUP * (k // TILES)) % LANES
            for c in range(2):
                for r0, n in blocks(0, ROWS, 64):
                    lane = lane_iota(n)
                    middle = jnp.logical_and(lane >= 4, lane < LANES - 4)
                    own = pl.ds(r0, n)
                    edge = pltpu.roll(edge_ref[c, tile, own], back, 1)
                    held_ref[2 * k + c, own] = jnp.where(middle, held_ref[2 * k + c, own], edge)
        store(part).start()

    each(lambda k: load(k).start())
    each(levels)
    each(lambda k: store(k).wait())


def two_sum(a, b):
    s = a + b
    v = s - a
    return s, (a - (s - v)) + (b - v)


def quick_sum(a, b):
    s = a + b
    return s, b - (s - a)


def split(a):
    t = a * 4097.0
    high = t - (t - a)
    return high, a - high


def two_prod(a, b, parts_a, parts_b):
    p = a * b
    ah, al = parts_a
    bh, bl = parts_b
    return p, ((ah * bh - p) + ah * bl + al * bh) + al * bl


def pair_add(x, y):
    s, e = two_sum(x[0], y[0])
    return quick_sum(s, e + (x[1] + y[1]))


def loose_add(x, y):
    s, e = two_sum(x[0], y[0])
    return s, e + (x[1] + y[1])


def pair_mul(x, y):
    p, e = two_prod(x[0], y[0], split(x[0]), split(y[0]))
    return quick_sum(p, e + (x[0] * y[1] + x[1] * y[0]))


def pair_neg(x):
    return -x[0], -x[1]


def pair_div(x, y):
    q = x[0] / y[0]
    rest = pair_add(x, pair_neg(pair_mul(y, (q, jnp.zeros_like(q)))))
    return quick_sum(q, rest[0] / y[0])


def pair_clip(x, top):
    inside = jnp.logical_and(x[0] >= 0.0, x[0] <= top)
    high = jnp.where(inside, x[0], jnp.where(x[0] > top, top, 0.0))
    return high, jnp.where(inside, x[1], 0.0)


def group_totals(x):
    x = x + roll(x, GROUP)
    x = x + roll(x, 2 * GROUP)
    return x + roll(x, 4 * GROUP)


def lane_left(main, side):
    lane = lane_iota(main.shape[0])
    a, b = roll(main, 1), roll(side, 1)
    return jnp.where(lane == 0, b, a), jnp.where(lane == 0, a, b)


def lane_right(main, side):
    lane = lane_iota(main.shape[0])
    a, b = roll(main, -1), roll(side, -1)
    return jnp.where(lane == LANES - 1, b, a), jnp.where(lane == LANES - 1, a, b)


SIDES = (0, 1)


def solve_kernel(
    mixing_ref,
    thick_ref,
    source_ref,
    depth_in,
    from_left_ref,
    from_right_ref,
    edge_ref,
    seen_ref,
    beside_ref,
    depth_ref,
    sums_ref,
    new_ref,
    v_ref,
    d_ref,
    e_ref,
    west_ref,
    east_ref,
    f_ref,
    u_ref,
    l_ref,
    n_ref,
    rho_ref,
    fx_ref,
    fy_ref,
    face_ref,
    lanes_ref,
    dl_ref,
    dr_ref,
    w_ref,
    p_ref,
    q_ref,
):
    by = lax.axis_index("by")
    open_side = (by != 0, by != lax.axis_size("by") - 1)

    def clear(ref):
        ref[...] = jnp.zeros(ref.shape, ref.dtype)

    for ref in (e_ref, west_ref, east_ref):
        clear(ref)
    for ref in (u_ref, l_ref, rho_ref, d_ref, v_ref, dl_ref, dr_ref, p_ref, q_ref, fx_ref):
        rank = len(ref.shape) - 2
        lead = [()]
        for size in ref.shape[:rank]:
            lead = [i + (j,) for i in lead for j in range(size)]
        for i in lead:
            for r0 in (0, BUF - PAD):
                ref[i + (pl.ds(r0, PAD),)] = jnp.zeros((PAD, LANES), F32)

    def field(side, c, tile, r0, n):
        own = edge_ref[c, tile, pl.ds(r0, n)]
        first = first_half(n)
        if side == 0:
            far = from_left_ref[tile, pl.ds(r0, n)]
            return jnp.where(first, roll(far, -8) if c else far, own)
        far = from_right_ref[tile, pl.ds(r0, n)]
        return jnp.where(first, own, roll(far, 8) if c else far)

    tile_eff, slot = edge_slot(KL)
    for side in SIDES:
        for r0, n in CHUNKS:
            lane = lane_iota(n)
            x = field(side, 0, tile_eff, r0, n)
            inner = (lane & 8) == (8 if side == 0 else 0)
            keep = jnp.logical_and(lane // GROUP == slot, jnp.logical_or(inner, open_side[side]))
            e = group_totals(jnp.where(keep, x, 0.0)).astype(I32)
            at = pl.ds(PAD + r0, n)
            e_ref[side, at] = e
            west_ref[side, at] = roll(e, 1)
            east_ref[side, at] = roll(e, -1)

    levels = tops(thick_ref)
    table = depth_table(levels)
    group8 = lane_iota(8) // GROUP
    for tile in range(TILES):
        held = [jnp.zeros((8, LANES), F32) for _ in range(4)]
        for g in range(GROUPS):
            k = TILES * g + tile
            if k < KL:
                values = (mixing_ref[k, 0], mixing_ref[k, 1], thick_ref[k], levels[k])
            else:
                values = (0.0, 0.0, 0.0, levels[KL])
            held = [jnp.where(group8 == g, x, old) for x, old in zip(values, held)]
        for i in range(4):
            lanes_ref[tile, i] = held[i]
    for side in SIDES:
        for r0, n in CHUNKS:
            e = e_ref[side, pl.ds(PAD + r0, n)]
            face_ref[side, 0, pl.ds(r0, n)] = look_up(table, jnp.minimum(e, e_ref[side, pl.ds(PAD + r0 - 1, n)]))
            face_ref[side, 1, pl.ds(r0, n)] = look_up(table, jnp.minimum(e, west_ref[side, pl.ds(PAD + r0, n)]))
    pieces = [(tile, side) for tile in range(TILES) for side in SIDES]

    def stages(piece):
        tile, side = pieces[piece]
        slot = piece % 3
        level_of = group8 * TILES + tile
        mix = [lanes_ref[tile, c] for c in range(2)]
        thick = lanes_ref[tile, 2]
        begin = lanes_ref[tile, 3]

        def masked(r0, n):
            at = pl.ds(PAD + r0, n)
            wet = e_ref[side, at] > tall(level_of, n)
            for c in range(2):
                x = field(side, c, tile, r0, n)
                f_ref[slot, c, pl.ds(r0, n)] = x
                u_ref[c, at] = jnp.where(wet, x, 0.0)

        def first(r0, n):
            at = pl.ds(PAD + r0, n)
            wet = e_ref[side, at] > tall(level_of, n)
            number = jnp.where(e_ref[side, pl.ds(PAD + r0 - 1, n)] > tall(level_of, n), 1.0, 0.0)
            number += jnp.where(e_ref[side, pl.ds(PAD + r0 + 1, n)] > tall(level_of, n), 1.0, 0.0)
            number += jnp.where(west_ref[side, at] > tall(level_of, n), 1.0, 0.0)
            number += jnp.where(east_ref[side, at] > tall(level_of, n), 1.0, 0.0)
            n_ref[pl.ds(r0, n)] = number
            for c in range(2):
                x, around = neighbours(u_ref.at[c], r0, n)
                l_ref[c, at] = jnp.where(wet, around, 0.0) - number * x

        def density(r0, n):
            at = pl.ds(PAD + r0, n)
            wet = e_ref[side, at] > tall(level_of, n)
            number = n_ref[pl.ds(r0, n)]
            new = []
            for c in range(2):
                x, around = neighbours(l_ref.at[c], r0, n)
                second = jnp.where(wet, around, 0.0) - number * x
                new.append(f_ref[slot, c, pl.ds(r0, n)] - tall(mix[c], n) * second)
            rho_ref[at] = tall(thick, n) * (0.8 * new[1] - 0.2 * new[0])
            low, high = max(r0, HALO), min(r0 + n, HALO + ROWS)
            own = pl.ds(low - HALO, high - low)
            for c in range(2):
                value = new[c][low - r0 : high - r0]
                if side == 1:
                    value = jnp.where(first_half(high - low), value, new_ref[c, tile, own])
                new_ref[c, tile, own] = value

        def flux(r0, n):
            here = rho_ref[pl.ds(PAD + r0, n)]
            up = rho_ref[pl.ds(PAD + r0 - 1, n)]
            below_x = jnp.maximum(face_ref[side, 0, pl.ds(r0, n)] - tall(begin, n), 0.0)
            below_y = jnp.maximum(face_ref[side, 1, pl.ds(r0, n)] - tall(begin, n), 0.0)
            face_x = below_x * (here - up)
            face_y = below_y * (here - roll(here, 1))
            if tile > 0:
                face_x += fx_ref[side, pl.ds(PAD + r0, n)]
                face_y += fy_ref[side, pl.ds(r0, n)]
            fx_ref[side, pl.ds(PAD + r0, n)] = face_x
            fy_ref[side, pl.ds(r0, n)] = face_y

        return masked, first, density, flux

    for step in range(len(pieces) + 3):
        parts = [stages(step - late)[late] for late in (3, 2, 1, 0) if 0 <= step - late < len(pieces)]
        interleave(parts)

    halves = blocks(0, EXT, EXT // 2)
    for r0, n in halves:
        lane = lane_iota(n)
        at = pl.ds(PAD + r0, n)
        own = pl.ds(r0, n)
        sources = []
        for side in SIDES:
            fy = fy_ref[side, own]
            sources.append(fx_ref[side, at] - fx_ref[side, pl.ds(PAD + r0 + 1, n)] + (fy - roll(fy, -1)))
        for shift in (GROUP, 2 * GROUP, 4 * GROUP):
            sources = [x + roll(x, shift) for x in sources]
        west, east = (GRAVITY * roll(x, 8) for x in sources)
        v_ref[0, 0, at] = jnp.where(lane < 3, west, jnp.where(lane >= LANES - 3, east, source_ref[own]))
        v_ref[0, 1, at] = jnp.where(lane < 8, east, jnp.where(lane >= LANES - 8, west, 0.0))
    for r0, n in halves:
        lane = lane_iota(n)
        at = pl.ds(PAD + r0, n)
        west = roll(e_ref[0, at], 8)
        east = roll(e_ref[1, at], 8)
        beside = jnp.where(lane < 8, east, jnp.where(lane >= LANES - 8, west, 0))
        d_ref[0, at] = depth_in[pl.ds(r0, n)]
        d_ref[1, at] = look_up(table, beside)
    for r0, n in CHUNKS:
        here = pl.ds(PAD + r0, n)
        d_main, d_side = d_ref[0, here], d_ref[1, here]
        dl_ref[0, here], dl_ref[1, here] = lane_left(d_main, d_side)
        dr_ref[0, here], dr_ref[1, here] = lane_right(d_main, d_side)

    def weights(t, carry):
        for r0, n in CHUNKS:
            here = pl.ds(PAD + r0, n)
            above = pl.ds(PAD + r0 - 1, n)
            below = pl.ds(PAD + r0 + 1, n)
            d = d_ref[t, here]
            left, right = dl_ref[t, here], dr_ref[t, here]
            up, down = d_ref[t, above], d_ref[t, below]
            w_west, w_east = jnp.minimum(d, left), jnp.minimum(d, right)
            w_up, w_down = jnp.minimum(d, up), jnp.minimum(d, down)
            corners = (
                jnp.minimum(d, dl_ref[t, above])
                + jnp.minimum(d, dr_ref[t, below])
                + jnp.minimum(d, dr_ref[t, above])
                + jnp.minimum(d, dl_ref[t, below])
            )
            at = pl.ds(r0, n)
            w_ref[0, t, at] = 0.05 + w_up + w_down + w_west + w_east + 0.25 * corners
            w_ref[1, t, at] = w_west
            w_ref[2, t, at] = w_east
            w_ref[3, t, at] = w_down
            w_ref[4, t, at] = 0.25 * jnp.minimum(down, left)
            w_ref[5, t, at] = 0.25 * jnp.minimum(down, right)
            w_ref[6, t, at] = w_up
            w_ref[7, t, at] = 0.25 * jnp.minimum(up, left)
            w_ref[8, t, at] = 0.25 * jnp.minimum(up, right)
        return carry

    lax.fori_loop(0, 2, weights, 0)

    def power(step, carry):
        for r0, n in CHUNKS:
            here = pl.ds(PAD + r0, n)
            at = pl.ds(r0, n)
            v = (v_ref[step, 0, here], v_ref[step, 1, here])
            left = lane_left(*v)
            right = lane_right(*v)
            for t in range(2):
                w = [w_ref[m, t, at] for m in range(9)]
                p_ref[t, here] = w[3] * v[t] + w[4] * left[t] + w[5] * right[t]
                q_ref[t, here] = w[6] * v[t] + w[7] * left[t] + w[8] * right[t]
                v_ref[step + 1, t, here] = w[0] * v[t] - (w[1] * left[t] + w[2] * right[t])
        for r0, n in CHUNKS:
            here = pl.ds(PAD + r0, n)
            for t in range(2):
                beside = p_ref[t, pl.ds(PAD + r0 - 1, n)] + q_ref[t, pl.ds(PAD + r0 + 1, n)]
                v_ref[step + 1, t, here] -= beside
        return carry

    lax.fori_loop(0, 4, power, 0)

    for i in range(4):
        seen_ref[i] = v_ref[i, 0, pl.ds(PAD, SEEN)]
    depth_ref[...] = d_ref[0, pl.ds(PAD, SEEN)]
    for r0, n in blocks(HALO, HALO + ROWS, 128):
        lane = lane_iota(n)
        at = pl.ds(PAD + r0, n)
        beside = roll(d_ref[1, at], 5)
        for i in range(4):
            beside = jnp.where(lane == i, roll(v_ref[i, 1, at], i + 1), beside)
        beside_ref[pl.ds(r0 - HALO, n)] = beside

    def dots(step, carry):
        at = pl.ds(pl.multiple_of(PAD + HALO + 8 * step, 8), 8)
        v = [v_ref[i, 0, at] for i in range(5)]
        parts = [split(x) for x in v]
        out = []
        for m in range(MOMENTS):
            i, j = m // 2, (m + 1) // 2
            p, e = two_prod(v[i], v[j], parts[i], parts[j])
            s, f = two_sum(carry[2 * m], p)
            out += [s, carry[2 * m + 1] + (e + f)]
        return tuple(out)

    zero = jnp.zeros((8, LANES), F32)
    sums = lax.fori_loop(0, ROWS // 8, dots, (zero,) * (2 * MOMENTS), unroll=4)
    sub = lax.broadcasted_iota(I32, (8, LANES), 0)
    pairs = [(sums[2 * m], sums[2 * m + 1]) for m in range(MOMENTS)]
    for half in (4, 2, 1):
        merged = []
        for m in range(half):
            a, b = pairs[m], pairs[m + half]
            upper = (sub & half) == 0
            keep = tuple(jnp.where(upper, x, y) for x, y in zip(a, b))
            other = tuple(jnp.where(upper, pltpu.roll(x, 8 - half, 0), pltpu.roll(y, half, 0)) for x, y in zip(a, b))
            merged.append(loose_add(keep, other))
        pairs = merged
    wide = [jnp.concatenate([x, jnp.zeros((LANES - 8, LANES), F32)]).T for x in pairs[0]]
    rows = [tuple(x[at : at + 8] for x in wide) for at in range(0, LANES, 8)]
    while len(rows) > 1:
        rows = [loose_add(rows[i], rows[i + 1]) for i in range(0, len(rows), 2)]
    total = rows[0]
    for shift in (4, 2, 1):
        total = loose_add(total, tuple(pltpu.roll(x, shift, 0) for x in total))
    total = quick_sum(*total)
    row = total[0] + roll(total[1], MOMENTS)
    for at in range(0, sums_ref.shape[0], 8):
        sums_ref[pl.ds(at, 8)] = row


def finish_kernel(all_ref, seen_ref, beside_ref, depth_ref, surface_ref, flow_ref, s_ref):
    zero = jnp.zeros((8, LANES), F32)
    rows = [(all_ref[pl.ds(at, 8)], zero) for at in range(0, all_ref.shape[0], 8)]
    while len(rows) > 1:
        rows = [loose_add(rows[i], rows[i + 1]) for i in range(0, len(rows), 2)]
    total = rows[0]
    for shift in (4, 2, 1):
        total = loose_add(total, tuple(pltpu.roll(x, shift, 0) for x in total))
    total = pair_add(total, tuple(roll(x, -MOMENTS) for x in total))
    lane = lane_iota(8)

    def moment(m):
        return tuple(
            jnp.broadcast_to(jnp.sum(jnp.where(lane == m, x, 0.0), axis=1, keepdims=True), (8, LANES))
            for x in total
        )

    rho = [moment(m) for m in range(MOMENTS)]
    pi = list(rho)
    nought = (zero, zero)
    one = (zero + 1.0, zero)
    surface = [nought] * 4
    residual = [one] + [nought] * 3
    direction = list(residual)
    for step in range(4):
        alpha = pair_clip(pair_div(rho[step], pi[step + 1]), 20.0)
        for i in range(step + 1):
            surface[i] = pair_add(surface[i], pair_mul(alpha, direction[i]))
        if step == 3:
            break
        minus = pair_neg(alpha)
        new_rho = list(rho)
        for m in range(step + 1, MOMENTS - 1 - step):
            new_rho[m] = pair_add(rho[m], pair_mul(minus, pi[m + 1]))
        beta = pair_clip(pair_div(pair_mul(minus, new_rho[step + 1]), rho[step]), 400.0)
        for m in range(step + 2, MOMENTS - 1 - step):
            pi[m] = pair_add(new_rho[m], pair_mul(beta, pi[m]))
        rho = new_rho
        for i in range(step + 1, 0, -1):
            residual[i] = pair_add(residual[i], pair_mul(minus, direction[i - 1]))
        for i in range(step + 2):
            direction[i] = pair_add(residual[i], pair_mul(beta, direction[i]))
    weight = [s[0] for s in surface]
    lane = lane_iota(8)
    by_lane = zero
    for i in range(4):
        by_lane = jnp.where(lane == i, weight[i], by_lane)
    for r0, n in blocks(0, SEEN, 88):
        at = pl.ds(r0, n)
        total = tall(weight[0], n) * seen_ref[0, at]
        for i in range(1, 4):
            total = total + tall(weight[i], n) * seen_ref[i, at]
        s_ref[at] = total
    for r0, n in blocks(HALO, SEEN, 128):
        at = pl.ds(r0, n)
        above = pl.ds(r0 - 1, n)
        own = pl.ds(r0 - HALO, n)
        lane = lane_iota(n)
        s, d = s_ref[at], depth_ref[at]
        beside = beside_ref[own]
        d_west = jnp.where(lane == 0, roll(beside, -4), roll(d, 1))
        beside = tall(by_lane, n) * beside
        beside = beside + roll(beside, -1)
        west = jnp.where(lane == 0, beside + roll(beside, -2), roll(s, 1))
        surface_ref[own] = s
        flow_ref[0, own] = jnp.minimum(d, depth_ref[above]) * (s_ref[above] - s)
        flow_ref[1, own] = jnp.minimum(d, d_west) * (west - s)


VM = pl.BlockSpec(memory_space=pltpu.VMEM)
SM = pl.BlockSpec(memory_space=pltpu.SMEM)
HBM = pl.BlockSpec(memory_space=pltpu.HBM)


def params(limit):
    return pltpu.CompilerParams(vmem_limit_bytes=limit * MIB)


def cost(flops, moved):
    return pl.CostEstimate(flops=flops, bytes_accessed=moved, transcendentals=0)


def ring(x, axis, step):
    count = lax.axis_size(axis)
    return lax.ppermute(x, axis, [(i, (i + step) % count) for i in range(count)])


def shape(*sizes, dtype=F32):
    return jax.ShapeDtypeStruct(sizes, dtype)


def scratch(*lead, rows=BUF, dtype=F32):
    return pltpu.VMEM(lead + (rows, LANES), dtype)


def shards(tracers, mixing, thickness, levels, land):
    devices = lax.axis_size("bx") * lax.axis_size("by")
    planes = 2 * KL
    wet = wet_levels(levels, land).astype(F32)
    flat = tracers.reshape(planes, ROWS, LANES)
    with jax.named_scope("rows"):
        wet_up = wet_levels(levels[:HALO], land[:HALO]).astype(F32)
        wet_down = wet_levels(levels[-HALO:], land[-HALO:]).astype(F32)
        to_up = jnp.concatenate([flat[:, :HALO], wet_up[None]])
        to_down = jnp.concatenate([flat[:, -HALO:], wet_down[None]])
        top = ring(to_down, "bx", 1)
        bottom = ring(to_up, "bx", -1)
    with jax.named_scope("columns"):
        edges = (shape(2, TILES, EXT, LANES), shape(TILES, EXT, LANES), shape(TILES, EXT, LANES))
        own = pl.pallas_call(
            own_edges_kernel,
            out_shape=edges,
            in_specs=[HBM, VM],
            out_specs=(VM,) * 3,
            scratch_shapes=[scratch(planes, rows=ROWS), pltpu.SemaphoreType.DMA((LOADS,))],
            compiler_params=params(48),
            cost_estimate=cost(10_000_000, 7_000_000),
        )(flat, wet)
        edge, to_right, to_left = pl.pallas_call(
            halo_edges_kernel,
            out_shape=edges,
            in_specs=[VM] * 5,
            out_specs=(VM,) * 3,
            input_output_aliases={i + 2: i for i in range(3)},
            compiler_params=params(16),
            cost_estimate=cost(1_000_000, 700_000),
        )(top, bottom, *own)
        from_left = ring(to_right, "by", 1)
        from_right = ring(to_left, "by", -1)
    with jax.named_scope("block"):
        new, source, depth = pl.pallas_call(
            block_kernel,
            out_shape=(shape(planes, ROWS, LANES), shape(EXT, LANES), shape(EXT, LANES)),
            in_specs=[SM, SM, HBM, VM, VM, VM],
            out_specs=(HBM, VM, VM),
            scratch_shapes=[
                scratch(planes, rows=EXT),
                scratch(dtype=I32),
                scratch(2, rows=EXT),
                scratch(3, rows=EXT, dtype=I32),
                scratch(2),
                scratch(2),
                scratch(rows=EXT),
                scratch(),
                scratch(),
                scratch(),
                pltpu.SMEM((KL,), F32),
                pltpu.SemaphoreType.DMA((KL,)),
                pltpu.SemaphoreType.DMA((KL,)),
            ],
            compiler_params=params(48),
            cost_estimate=cost(50_000_000, 12_000_000),
        )(mixing, thickness, flat, top, bottom, wet)
    with jax.named_scope("powers"):
        seen, beside, near_depth, sums, new_edge = pl.pallas_call(
            solve_kernel,
            out_shape=(
                shape(4, SEEN, LANES),
                shape(ROWS, LANES),
                shape(SEEN, LANES),
                shape(devices, LANES),
                shape(2, TILES, ROWS, LANES),
            ),
            in_specs=[SM, SM] + [VM] * 5,
            out_specs=(VM,) * 5,
            scratch_shapes=[
                scratch(5, 2),
                scratch(2),
                scratch(2, dtype=I32),
                scratch(2, dtype=I32),
                scratch(2, dtype=I32),
                scratch(3, 2, rows=EXT),
                scratch(2),
                scratch(2),
                scratch(rows=EXT),
                scratch(),
                scratch(2),
                scratch(2, rows=EXT),
                scratch(2, 2, rows=EXT),
                scratch(TILES, 4, rows=8),
                scratch(2),
                scratch(2),
                scratch(9, 2, rows=EXT),
                scratch(2),
                scratch(2),
            ],
            compiler_params=params(20),
            cost_estimate=cost(50_000_000, 6_000_000),
        )(mixing, thickness, source, depth, from_left, from_right, edge)
    with jax.named_scope("sums"):
        everyone = lax.all_to_all(sums, ("bx", "by"), 0, 0, tiled=True)
    with jax.named_scope("patch"):
        tracers_new = pl.pallas_call(
            patch_kernel,
            out_shape=shape(planes, ROWS, LANES),
            in_specs=[HBM, VM],
            out_specs=HBM,
            scratch_shapes=[
                scratch(planes, rows=ROWS),
                pltpu.SemaphoreType.DMA((KL // PATCH,)),
                pltpu.SemaphoreType.DMA((KL // PATCH,)),
            ],
            compiler_params=params(48),
            cost_estimate=cost(10_000_000, 12_000_000),
        )(new, new_edge)
    with jax.named_scope("surface"):
        surface, transports = pl.pallas_call(
            finish_kernel,
            out_shape=(shape(ROWS, LANES), shape(2, ROWS, LANES)),
            in_specs=[VM] * 4,
            out_specs=(VM, VM),
            scratch_shapes=[scratch(rows=SEEN)],
            compiler_params=params(8),
            cost_estimate=cost(1_000_000, 3_000_000),
        )(everyone, seen, beside, near_depth)
    return tracers_new.reshape(tracers.shape), surface, transports


def solution(mesh):
    in_specs = (P(None, None, "bx", "by"), P(), P(), P("bx", "by"), P("bx", "by"))
    out_specs = (P(None, None, "bx", "by"), P("bx", "by"), P(None, "bx", "by"))
    return jax.shard_map(shards, mesh=mesh, in_specs=in_specs, out_specs=out_specs, check_vma=False)
```
